128 devices in a mesh: layer: 2 (over core), feat: 32 (over z_lo, y, x), dp: 2 (over z_hi).
Axes of the slice: x: 4, y: 4, z: 4 (z_hi: 2, z_lo: 2; z = z_hi * 2 + z_lo), core: 2. Of those that a mesh axis runs over, the one named last changes fastest.
Arguments:
- acts: bfloat16 [2, 2048, 3584], P('layer', 'dp', 'feat'), may hold values from -6 to 6
- targets: bfloat16 [2, 2048, 3584], P('layer', 'dp', 'feat'), may hold values from -6 to 6
- enc: bfloat16 [2, 3584, 16384], P('layer', None, 'feat'), may hold values from -0.09375 to 0.09375
- enc_bias: float32 [2, 16384], P('layer', 'feat'), may hold values from -1 to 0.5
- dec_own: bfloat16 [2, 16384, 3584], P('layer', 'feat'), may hold values from -0.046875 to 0.046875
- dec_cross: bfloat16 [16384, 3584], P('feat', 'layer'), may hold values from -0.046875 to 0.046875
- dec_bias: bfloat16 [2, 3584], P('layer', 'feat'), may hold values from -3 to 3
Outputs:
- residual: float32 [2, 2048, 3584], P('layer', 'dp', 'feat')
- grad_enc: float32 [2, 3584, 16384], P('layer', 'dp', 'feat')
- grad_dec_own: float32 [2, 16384, 3584], P('layer', 'feat', 'dp')
- grad_dec_cross: float32 [16384, 3584], P('feat', ('layer', 'dp'))
The draws below stay inside these ranges and needn't reach their ends.
All inputs are finite; a program needn't handle non-finite values.
Results may differ from the reference program's by a relative error of at most 0.025.
Values may be sent and summed in bfloat16 or wider, within the bound.
A program may use at most 192 MiB of HBM per device.

```python
import jax
import jax.numpy as jnp
from jax import lax

D = 3584
F = 16384
LAYERS = 2
TOK_DEV = 1024
TOKENS = 2048
N_DP = 2


def block_levels(key, shape, pieces, low, top_value):
    loudness, own = 1.0, jax.random.fold_in(key, 6)
    for axis_at, parts in pieces:
        heights = jnp.exp(jax.random.uniform(jax.random.fold_in(own, axis_at), (parts,), jnp.float32, low / len(pieces), top_value / len(pieces)))
        loudness = loudness * jnp.repeat(heights, shape[axis_at] // parts).reshape([-1 if axis == axis_at else 1 for axis in range(len(shape))])
    return loudness


def scatter_about(own_key, shape, spread, most, pieces=(), kind=jnp.bfloat16):
    array = spread * jax.random.normal(own_key, shape, jnp.float32)
    if pieces:
        array = array * block_levels(own_key, shape, pieces, -0.22, 0.18)
    return jnp.clip(array, -most, most).astype(kind)


def setup_inputs(seed: int = 0) -> dict:
    seeds = jax.random.split(jax.random.key(seed), 8)
    return {
        "acts": scatter_about(seeds[0], (LAYERS, TOKENS, D), 1.0, 6.0, ((0, 2), (1, 2), (2, 32))),
        "targets": scatter_about(seeds[1], (LAYERS, TOKENS, D), 1.0, 6.0, ((0, 2), (1, 2), (2, 32))),
        "enc": scatter_about(seeds[2], (LAYERS, D, F), D ** -0.5, 0.09375, ((0, 2), (2, 32))),
        "enc_bias": jnp.clip(-1.0 + 1.5 * jax.random.uniform(seeds[3], (LAYERS, F), jnp.float32) ** block_levels(seeds[3], (LAYERS, F), ((0, 2), (1, 32)), -0.2, 0.2), -1.0, 0.5),
        "dec_own": scatter_about(seeds[4], (LAYERS, F, D), F ** -0.5, 0.046875, ((0, 2), (1, 32))),
        "dec_cross": scatter_about(seeds[5], (F, D), F ** -0.5, 0.046875, ((0, 32), (1, 2))),
        "dec_bias": scatter_about(seeds[6], (LAYERS, D), 0.5, 3.0, ((0, 2), (1, 32))),
    }


def block_sum(left_rows, right_rows):
    total = jnp.zeros((left_rows.shape[1], right_rows.shape[1]), jnp.float32)
    for block_idx in range(N_DP):
        left_part = left_rows[block_idx * TOK_DEV:(block_idx + 1) * TOK_DEV]
        right_part = right_rows[block_idx * TOK_DEV:(block_idx + 1) * TOK_DEV]
        partial_sum = jnp.dot(left_part.T, right_part, preferred_element_type=jnp.float32)
        rounded = lax.optimization_barrier(partial_sum.astype(jnp.bfloat16))
        total = total + rounded.astype(jnp.float32)
    return total


def reference(acts, targets, enc, enc_bias, dec_own, dec_cross, dec_bias):
    grad_scale = float(TOKENS) ** -0.5
    positive = []
    features = []
    for level in range(2):
        pre_act = jnp.dot(acts[level], enc[level], preferred_element_type=jnp.float32) + enc_bias[level]
        pos_part = jnp.maximum(pre_act, 0.0)
        positive.append(pos_part)
        features.append((pos_part * pos_part).astype(jnp.bfloat16))
    recon_low = jnp.dot(features[0], dec_own[0], preferred_element_type=jnp.float32)
    recon_high = jnp.dot(features[1], dec_own[1], preferred_element_type=jnp.float32) + jnp.dot(features[0], dec_cross, preferred_element_type=jnp.float32)
    recons = [recon_low, recon_high]
    residuals = []
    grad_out = []
    for level in range(2):
        resid_part = recons[level] + dec_bias[level].astype(jnp.float32) - targets[level].astype(jnp.float32)
        residuals.append(resid_part)
        grad_out.append((resid_part * grad_scale).astype(jnp.bfloat16))
    grad_low = jnp.dot(grad_out[0], dec_own[0].T, preferred_element_type=jnp.float32) + jnp.dot(grad_out[1], dec_cross.T, preferred_element_type=jnp.float32)
    grad_high = jnp.dot(grad_out[1], dec_own[1].T, preferred_element_type=jnp.float32)
    grad_feats = [grad_low, grad_high]
    enc_list = []
    own_list = []
    for level in range(2):
        grad_pre = (grad_feats[level] * 2.0 * positive[level]).astype(jnp.bfloat16)
        enc_list.append(block_sum(acts[level], grad_pre))
        own_list.append(block_sum(features[level], grad_out[level]))
    cross_grad = block_sum(features[0], grad_out[1])
    return (jnp.stack(residuals), jnp.stack(enc_list), jnp.stack(own_list), cross_grad)
```

```python
import functools

import jax
import jax.numpy as jnp
from jax import lax
from jax.experimental import pallas as pl
from jax.experimental.pallas import tpu as pltpu
from jax.sharding import PartitionSpec as P

MESH = pl.DeviceIdType.MESH
ALL = slice(None)
SIDE = 4
JOBS = 8


class Place:
    def __init__(self):
        feat = lax.axis_index("feat")
        self.core = lax.axis_index("layer")
        self.dp = lax.axis_index("dp")
        self.x = lax.rem(feat, SIDE)
        self.y = lax.rem(lax.div(feat, SIDE), SIDE)
        self.zl = lax.div(feat, SIDE * SIDE)

    def feat(self, zl=None, y=None, x=None):
        zl = self.zl if zl is None else zl
        y = self.y if y is None else y
        x = self.x if x is None else x
        return (zl * SIDE + y) * SIDE + x

    def at(self, axis):
        return self.x if axis == "x" else self.y

    def along(self, axis, step):
        return lax.rem(self.at(axis) + (step + SIDE), SIDE)

    def neighbour(self, axis, step):
        return {"feat": self.feat(**{axis: self.along(axis, step)})}

    def pair(self):
        return {"feat": self.feat(zl=1 - self.zl)}

    def across(self, zl):
        return {"feat": self.feat(zl=zl), "dp": 1 - self.dp}

    def other_core(self):
        return {"layer": 1 - self.core}

    def greet(self, core):
        peers = [self.neighbour(a, s) for a in "xy" for s in (1, -1)]
        peers += [self.pair(), self.across(0), self.across(1)]
        if core:
            peers.append(self.other_core())
        barrier = pltpu.get_barrier_semaphore()
        for peer in peers:
            pl.semaphore_signal(barrier, inc=1, device_id=peer, device_id_type=MESH)
        pl.semaphore_wait(barrier, len(peers))


def remote(src, dst, send, recv, device):
    return pltpu.make_async_remote_copy(
        src_ref=src, dst_ref=dst, send_sem=send, recv_sem=recv, device_id=device, device_id_type=MESH
    )


class Gather:
    sems = 11
    steps = 6

    def __init__(self, place, buf, own, lanes, flip, split, send, recv, local, job):
        self.place, self.buf, self.own, self.lanes = place, buf, own, lanes
        self.first, self.second = ("y", "x") if flip else ("x", "y")
        self.send, self.recv, self.local, self.job = send, recv, local, job
        self.right, self.left = (slice(0, 2), slice(2, 3)) if split else (slice(0, 1), slice(1, 3))
        self.sent = []

    def first_block(self, slots, at):
        p = self.place
        index = (slots, p.y, at, ALL, self.lanes) if self.first == "x" else (slots, at, p.x, ALL, self.lanes)
        return self.buf.at[index]

    def second_block(self, slots, at):
        index = (slots, at, ALL, ALL, self.lanes) if self.second == "y" else (slots, ALL, at, ALL, self.lanes)
        return self.buf.at[index]

    def copy(self, sem, src, dst, device, recv=None):
        return remote(src, dst, self.send.at[self.job, sem], self.recv.at[self.job, sem if recv is None else recv], device)

    def out(self, sem, block, device):
        copy = self.copy(sem, block, block, device)
        copy.start()
        self.sent.append(copy)
        return copy

    def ring(self, sem, axis, block):
        p = self.place
        own = block(slice(0, 3), p.at(axis))
        return (self.out(sem, own, p.neighbour(axis, 1)), self.out(sem + 1, own, p.neighbour(axis, -1)))

    def forward(self, sem, axis, block):
        p = self.place
        return (
            self.out(sem, block(self.right, p.along(axis, -1)), p.neighbour(axis, 1)),
            self.out(sem + 1, block(self.left, p.along(axis, 1)), p.neighbour(axis, -1)),
        )

    def step(self, number):
        p = self.place
        if number == 0:
            here = self.buf.at[p.zl, p.y, p.x, :, self.lanes]
            self.kept = pltpu.make_async_copy(self.own, here, self.local.at[self.job])
            self.kept.start()
            pair = self.copy(0, self.own, here, p.pair())
            pair.start()
            self.sent.append(pair)
            there = self.buf.at[2, p.y, p.x, :, self.lanes]
            self.cross = [self.copy(1 + zl, self.own, there, p.across(zl), recv=1) for zl in (0, 1)]

            @pl.when(p.zl != p.dp)
            def _():
                for copy in self.cross:
                    copy.start()

            self.waits = [pair, self.cross[0]]
            return
        for copy in self.waits:
            copy.wait_recv()
        if number == 1:
            self.kept.wait()
            self.waits = self.ring(3, self.first, self.first_block)
        elif number == 2:
            self.waits = self.forward(5, self.first, self.first_block)
        elif number == 3:
            self.waits = self.ring(7, self.second, self.second_block)
        elif number == 4:
            self.waits = self.forward(9, self.second, self.second_block)

    def finish(self):
        for copy in self.sent:
            copy.wait_send()
        p = self.place

        @pl.when(p.zl != p.dp)
        def _():
            for copy in self.cross:
                copy.wait_send()


class Reduce:
    sems = 13
    steps = 6

    def __init__(self, place, part, lanes, flip, room, send, recv, job, finish):
        self.place, self.part, self.lanes = place, part, lanes
        self.first, self.second = ("x", "y") if flip else ("y", "x")
        self.far1, self.far2, self.near1, self.near2, self.last = room
        self.send, self.recv, self.job, self.done = send, recv, job, finish
        self.sent = []

    def first_block(self, z, at):
        return (z, at, ALL, ALL, self.lanes) if self.first == "y" else (z, ALL, at, ALL, self.lanes)

    def second_block(self, z, at):
        p = self.place
        return (z, p.y, at, ALL, self.lanes) if self.first == "y" else (z, at, p.x, ALL, self.lanes)

    def out(self, sem, src, dst, device):
        copy = remote(src, dst, self.send.at[self.job, sem], self.recv.at[self.job, sem], device)
        copy.start()
        self.sent.append(copy)
        return copy

    def add(self, index, *refs):
        total = self.part[index].astype(jnp.float32)
        for ref in refs:
            total = total + ref[...].astype(jnp.float32)
        self.part[index] = total.astype(self.part.dtype)

    def begin(self, sem, axis, block, one, two):
        p = self.place
        right, left = p.neighbour(axis, 1), p.neighbour(axis, -1)
        far, up, down = p.along(axis, 2), p.along(axis, 1), p.along(axis, -1)
        j = self.job
        self.relay = (
            self.out(sem, self.part.at[block(0, far)], one.at[j, 0], right),
            self.out(sem + 1, self.part.at[block(1, far)], one.at[j, 1], left),
        )
        self.early = (
            self.out(sem + 2, self.part.at[block(1, up)], two.at[j, 0, 1], right),
            self.out(sem + 3, self.part.at[block(0, down)], two.at[j, 1, 0], left),
        )

    def pass_on(self, sem, axis, block, one, two):
        p = self.place
        right, left = p.neighbour(axis, 1), p.neighbour(axis, -1)
        up, down = p.along(axis, 1), p.along(axis, -1)
        j = self.job
        self.relay[0].wait_recv()
        self.add(block(0, up), one.at[j, 0])
        late = self.out(sem, self.part.at[block(0, up)], two.at[j, 0, 0], right)
        self.relay[1].wait_recv()
        self.add(block(1, down), one.at[j, 1])
        self.late = (late, self.out(sem + 1, self.part.at[block(1, down)], two.at[j, 1, 1], left))

    def collect(self, axis, block, two):
        for copy in self.early + self.late:
            copy.wait_recv()
        self.add(block(slice(0, 2), self.place.at(axis)), two.at[self.job, 0], two.at[self.job, 1])

    def step(self, number):
        p = self.place
        if number == 0:
            self.begin(0, self.first, self.first_block, self.far1, self.far2)
        elif number == 1:
            self.pass_on(4, self.first, self.first_block, self.far1, self.far2)
        elif number == 2:
            self.collect(self.first, self.first_block, self.far2)
            self.begin(6, self.second, self.second_block, self.near1, self.near2)
        elif number == 3:
            self.pass_on(10, self.second, self.second_block, self.near1, self.near2)
        elif number == 4:
            self.collect(self.second, self.second_block, self.near2)
            gone = self.part.at[1 - p.zl, p.y, p.x, :, self.lanes]
            self.pair = self.out(12, gone, self.last.at[self.job], p.pair())
        else:
            self.pair.wait_recv()
            mine = self.part[p.zl, p.y, p.x, :, self.lanes].astype(jnp.float32)
            self.done(mine + self.last[self.job].astype(jnp.float32), self.lanes)

    def finish(self):
        for copy in self.sent:
            copy.wait_send()


def run_skewed(lines, skew):
    length = max(len(line) for line in lines)
    for tick in range(length + skew * (len(lines) - 1)):
        for i, line in enumerate(lines):
            at = tick - skew * i
            if 0 <= at < len(line):
                for step in line[at]:
                    step()


def lanes_of(job, tokens):
    width = tokens // JOBS
    return pl.ds(job * width, width)


def gather_kernel(tokens, own_ref, cross_ref, buf, both, send, recv, local, core_sem):
    place = Place()
    place.greet(core=True)
    kept = pltpu.make_async_copy(cross_ref, both.at[place.core], core_sem.at[0])
    kept.start()
    swap = remote(cross_ref, both.at[place.core], core_sem.at[1], core_sem.at[2], place.other_core())
    swap.start()
    jobs = []
    for job in range(JOBS):
        lanes = lanes_of(job, tokens)
        jobs.append(Gather(place, buf, own_ref.at[:, lanes], lanes, job % 2, (job // 2) % 2, send, recv, local, job))
    lines = []
    for a, b in zip(jobs[::2], jobs[1::2]):
        lines.append([[functools.partial(g.step, n) for g in (a, b)] for n in range(Gather.steps)])
    run_skewed(lines, 1)
    for job in jobs:
        job.finish()
    kept.wait()
    swap.wait()


def exchange_kernel(
    tokens, scale, part_in, target_ref, bias_ref, resid_ref, buf, part, shard, far1, far2, near1, near2, last,
    send_r, recv_r, send_g, recv_g, local, load_sem
):
    place = Place()
    load = pltpu.make_async_copy(part_in, part, load_sem.at[0])
    load.start()
    place.greet(core=False)
    load.wait()

    def finish(total, lanes):
        resid = total + bias_ref[...] - target_ref[:, lanes].astype(jnp.float32)
        resid_ref[:, lanes] = resid
        shard[:, lanes] = (resid * scale).astype(shard.dtype)

    room = (far1, far2, near1, near2, last)
    reduces, gathers = [], []
    for job in range(JOBS):
        lanes = lanes_of(job, tokens)
        reduces.append(Reduce(place, part, lanes, job % 2, room, send_r, recv_r, job, finish))
        gathers.append(
            Gather(place, buf, shard.at[:, lanes], lanes, job % 2, (job // 2) % 2, send_g, recv_g, local, job)
        )
    lines = []
    for c in range(0, JOBS, 2):
        line = [[functools.partial(r.step, n) for r in reduces[c : c + 2]] for n in range(Reduce.steps)]
        line += [[functools.partial(g.step, n) for g in gathers[c : c + 2]] for n in range(Gather.steps)]
        lines.append(line)
    run_skewed(lines, 2)
    for job in reduces + gathers:
        job.finish()


def gather_acts(own, cross):
    rows, tokens = own.shape
    return pl.pallas_call(
        functools.partial(gather_kernel, tokens),
        out_shape=(
            jax.ShapeDtypeStruct((3, SIDE, SIDE, rows, tokens), own.dtype),
            jax.ShapeDtypeStruct((2,) + cross.shape, cross.dtype),
        ),
        in_specs=[pl.BlockSpec(memory_space=pltpu.VMEM), pl.BlockSpec(memory_space=pl.ANY)],
        out_specs=(pl.BlockSpec(memory_space=pl.ANY),) * 2,
        scratch_shapes=[
            pltpu.SemaphoreType.DMA((JOBS, Gather.sems)),
            pltpu.SemaphoreType.DMA((JOBS, Gather.sems)),
            pltpu.SemaphoreType.DMA((JOBS,)),
            pltpu.SemaphoreType.DMA((3,)),
        ],
        compiler_params=pltpu.CompilerParams(
            collective_id=1, has_side_effects=True, vmem_limit_bytes=56 * 1024 * 1024
        ),
        name="gather_acts",
    )(own, cross)


def exchange(part, targets, bias, scale):
    rows, tokens = targets.shape
    width = tokens // JOBS
    kind = part.dtype
    return pl.pallas_call(
        functools.partial(exchange_kernel, tokens, scale),
        out_shape=(
            jax.ShapeDtypeStruct((rows, tokens), jnp.float32),
            jax.ShapeDtypeStruct((3, SIDE, SIDE, rows, tokens), kind),
        ),
        in_specs=[
            pl.BlockSpec(memory_space=pl.ANY),
            pl.BlockSpec(memory_space=pltpu.VMEM),
            pl.BlockSpec(memory_space=pltpu.VMEM),
        ],
        out_specs=(pl.BlockSpec(memory_space=pltpu.VMEM), pl.BlockSpec(memory_space=pl.ANY)),
        scratch_shapes=[
            pltpu.VMEM(part.shape, kind),
            pltpu.VMEM((rows, tokens), kind),
            pltpu.VMEM((JOBS, 2, SIDE, rows, width), kind),
            pltpu.VMEM((JOBS, 2, 2, SIDE, rows, width), kind),
            pltpu.VMEM((JOBS, 2, rows, width), kind),
            pltpu.VMEM((JOBS, 2, 2, rows, width), kind),
            pltpu.VMEM((JOBS, rows, width), kind),
            pltpu.SemaphoreType.DMA((JOBS, Reduce.sems)),
            pltpu.SemaphoreType.DMA((JOBS, Reduce.sems)),
            pltpu.SemaphoreType.DMA((JOBS, Gather.sems)),
            pltpu.SemaphoreType.DMA((JOBS, Gather.sems)),
            pltpu.SemaphoreType.DMA((JOBS,)),
            pltpu.SemaphoreType.DMA((1,)),
        ],
        compiler_params=pltpu.CompilerParams(
            collective_id=2, has_side_effects=True, vmem_limit_bytes=56 * 1024 * 1024
        ),
        name="exchange",
    )(part, targets, bias)


def dot(a, b, over_a, over_b):
    return lax.dot_general(a, b, (((over_a,), (over_b,)), ((), ())), preferred_element_type=jnp.float32)


def local(acts, targets, enc, enc_bias, dec_own, dec_cross, dec_bias):
    tokens, rows = acts.shape[1:]
    n_dp = lax.axis_size("dp")
    width = enc.shape[1]
    half = width // 2
    feats_here = enc.shape[2]
    scale = float(tokens * n_dp) ** (-0.5)
    core, dp = lax.axis_index("layer"), lax.axis_index("dp")
    swap = [(0, 1), (1, 0)]
    bf16, f32 = jnp.bfloat16, jnp.float32

    gathered, cross_both = gather_acts(acts[0].T, dec_cross)
    acts_own = gathered[:2].reshape(width, tokens)
    pre_act = dot(enc[0], acts_own, 0, 0) + enc_bias[0][:, None]
    positive = jnp.maximum(pre_act, 0.0)
    features = (positive * positive).astype(bf16)
    lower = lax.ppermute(features, "layer", [(0, 1)])
    features_far = lax.ppermute(features, "dp", swap)
    cross = jnp.concatenate([cross_both[0], cross_both[1]], axis=1)
    part = dot(dec_own[0], features, 0, 0) + dot(cross, lower, 0, 0)
    part = part.astype(bf16).reshape(2, SIDE, SIDE, rows, tokens)

    bias = dec_bias.astype(f32).reshape(rows, 1)
    residual, grads = exchange(part, targets[0].T, bias, scale)

    grad_out = grads[:2].reshape(width, tokens)
    grad_far = grads[2].reshape(half, tokens)
    down = lax.ppermute(dot(cross, grad_out, 1, 0).astype(bf16), "layer", [(1, 0)])
    lent = lax.ppermute(grad_out[:half], "layer", [(1, 0)])
    grad_feats = dot(dec_own[0], grad_out, 1, 0) + down.astype(f32)
    grad_pre = (grad_feats * 2.0 * positive).astype(bf16)
    grad_pre_far = lax.ppermute(grad_pre, "dp", swap)

    first = jnp.where(core == 0, features, lower)
    own_half = jnp.where(core == 0, lent, grad_out[half:])
    by_dp = dot(first, own_half, 1, 1).reshape(feats_here, n_dp, half // n_dp)
    kept = lax.dynamic_index_in_dim(by_dp, dp, 1, keepdims=False)
    given = lax.dynamic_index_in_dim(by_dp, 1 - dp, 1, keepdims=False).astype(bf16)
    grad_cross = kept + lax.ppermute(given, "dp", swap).astype(f32)

    grad_half = lax.dynamic_index_in_dim(grads, dp, 0, keepdims=False).reshape(half, tokens)
    grad_own = dot(features, grad_half, 1, 1) + dot(features_far, grad_far, 1, 1)
    acts_half = lax.dynamic_index_in_dim(gathered, dp, 0, keepdims=False).reshape(half, tokens)
    acts_far = gathered[2].reshape(half, tokens)
    grad_enc = dot(acts_half, grad_pre, 1, 1) + dot(acts_far, grad_pre_far, 1, 1)
    return (residual.T[None], grad_enc[None], grad_own[None], grad_cross)


def solution(mesh):
    in_specs = (
        P("layer", "dp", "feat"),
        P("layer", "dp", "feat"),
        P("layer", None, "feat"),
        P("layer", "feat"),
        P("layer", "feat", None),
        P("feat", "layer"),
        P("layer", "feat"),
    )
    out_specs = (
        P("layer", "dp", "feat"),
        P("layer", "dp", "feat"),
        P("layer", "feat", "dp"),
        P("feat", ("layer", "dp")),
    )
    return jax.shard_map(local, mesh=mesh, in_specs=in_specs, out_specs=out_specs, check_vma=False)
```

```python
import functools

import jax
import jax.numpy as jnp
from jax import lax
from jax.experimental import pallas as pl
from jax.experimental.pallas import tpu as pltpu
from jax.sharding import PartitionSpec as P

MESH = pl.DeviceIdType.MESH
ALL = slice(None)
SIDE = 4
JOBS = 8


class Place:
    def __init__(self):
        feat = lax.axis_index("feat")
        self.core = lax.axis_index("layer")
        self.dp = lax.axis_index("dp")
        self.x = lax.rem(feat, SIDE)
        self.y = lax.rem(lax.div(feat, SIDE), SIDE)
        self.zl = lax.div(feat, SIDE * SIDE)

    def feat(self, zl=None, y=None, x=None):
        zl = self.zl if zl is None else zl
        y = self.y if y is None else y
        x = self.x if x is None else x
        return (zl * SIDE + y) * SIDE + x

    def at(self, axis):
        return self.x if axis == "x" else self.y

    def along(self, axis, step):
        return lax.rem(self.at(axis) + (step + SIDE), SIDE)

    def neighbour(self, axis, step):
        return {"feat": self.feat(**{axis: self.along(axis, step)})}

    def pair(self):
        return {"feat": self.feat(zl=1 - self.zl)}

    def across(self, zl):
        return {"feat": self.feat(zl=zl), "dp": 1 - self.dp}

    def other_core(self):
        return {"layer": 1 - self.core}

    def greet(self, core):
        peers = [self.neighbour(a, s) for a in "xy" for s in (1, -1)]
        peers += [self.pair(), self.across(0), self.across(1)]
        if core:
            peers.append(self.other_core())
        barrier = pltpu.get_barrier_semaphore()
        for peer in peers:
            pl.semaphore_signal(barrier, inc=1, device_id=peer, device_id_type=MESH)
        pl.semaphore_wait(barrier, len(peers))


def remote(src, dst, send, recv, device):
    return pltpu.make_async_remote_copy(
        src_ref=src, dst_ref=dst, send_sem=send, recv_sem=recv, device_id=device, device_id_type=MESH
    )


class Gather:
    sems = 11
    steps = 6

    def __init__(self, place, buf, own, lanes, flip, split, send, recv, local, job):
        self.place, self.buf, self.own, self.lanes = place, buf, own, lanes
        self.first, self.second = ("y", "x") if flip else ("x", "y")
        self.send, self.recv, self.local, self.job = send, recv, local, job
        self.right, self.left = (slice(0, 2), slice(2, 3)) if split else (slice(0, 1), slice(1, 3))
        self.sent = []

    def first_block(self, slots, at):
        p = self.place
        index = (slots, p.y, at, ALL, self.lanes) if self.first == "x" else (slots, at, p.x, ALL, self.lanes)
        return self.buf.at[index]

    def second_block(self, slots, at):
        index = (slots, at, ALL, ALL, self.lanes) if self.second == "y" else (slots, ALL, at, ALL, self.lanes)
        return self.buf.at[index]

    def copy(self, sem, src, dst, device, recv=None):
        return remote(src, dst, self.send.at[self.job, sem], self.recv.at[self.job, sem if recv is None else recv], device)

    def out(self, sem, block, device):
        copy = self.copy(sem, block, block, device)
        copy.start()
        self.sent.append(copy)
        return copy

    def ring(self, sem, axis, block):
        p = self.place
        own = block(slice(0, 3), p.at(axis))
        return (self.out(sem, own, p.neighbour(axis, 1)), self.out(sem + 1, own, p.neighbour(axis, -1)))

    def forward(self, sem, axis, block):
        p = self.place
        return (
            self.out(sem, block(self.right, p.along(axis, -1)), p.neighbour(axis, 1)),
            self.out(sem + 1, block(self.left, p.along(axis, 1)), p.neighbour(axis, -1)),
        )

    def step(self, number):
        p = self.place
        if number == 0:
            here = self.buf.at[p.zl, p.y, p.x, :, self.lanes]
            self.kept = pltpu.make_async_copy(self.own, here, self.local.at[self.job])
            self.kept.start()
            pair = self.copy(0, self.own, here, p.pair())
            pair.start()
            self.sent.append(pair)
            there = self.buf.at[2, p.y, p.x, :, self.lanes]
            self.cross = [self.copy(1 + zl, self.own, there, p.across(zl), recv=1) for zl in (0, 1)]

            @pl.when(p.zl != p.dp)
            def _():
                for copy in self.cross:
                    copy.start()

            self.waits = [pair, self.cross[0]]
            return
        for copy in self.waits:
            copy.wait_recv()
        if number == 1:
            self.kept.wait()
            self.waits = self.ring(3, self.first, self.first_block)
        elif number == 2:
            self.waits = self.forward(5, self.first, self.first_block)
        elif number == 3:
            self.waits = self.ring(7, self.second, self.second_block)
        elif number == 4:
            self.waits = self.forward(9, self.second, self.second_block)

    def finish(self):
        for copy in self.sent:
            copy.wait_send()
        p = self.place

        @pl.when(p.zl != p.dp)
        def _():
            for copy in self.cross:
                copy.wait_send()


class Reduce:
    sems = 13
    steps = 6

    def __init__(self, place, part, lanes, flip, room, send, recv, job, finish):
        self.place, self.part, self.lanes = place, part, lanes
        self.first, self.second = ("x", "y") if flip else ("y", "x")
        self.far1, self.far2, self.near1, self.near2, self.last = room
        self.send, self.recv, self.job, self.done = send, recv, job, finish
        self.sent = []

    def first_block(self, z, at):
        return (z, at, ALL, ALL, self.lanes) if self.first == "y" else (z, ALL, at, ALL, self.lanes)

    def second_block(self, z, at):
        p = self.place
        return (z, p.y, at, ALL, self.lanes) if self.first == "y" else (z, at, p.x, ALL, self.lanes)

    def out(self, sem, src, dst, device):
        copy = remote(src, dst, self.send.at[self.job, sem], self.recv.at[self.job, sem], device)
        copy.start()
        self.sent.append(copy)
        return copy

    def add(self, index, *refs):
        total = self.part[index].astype(jnp.float32)
        for ref in refs:
            total = total + ref[...].astype(jnp.float32)
        self.part[index] = total.astype(self.part.dtype)

    def begin(self, sem, axis, block, one, two):
        p = self.place
        right, left = p.neighbour(axis, 1), p.neighbour(axis, -1)
        far, up, down = p.along(axis, 2), p.along(axis, 1), p.along(axis, -1)
        j = self.job
        self.relay = (
            self.out(sem, self.part.at[block(0, far)], one.at[j, 0], right),
            self.out(sem + 1, self.part.at[block(1, far)], one.at[j, 1], left),
        )
        self.early = (
            self.out(sem + 2, self.part.at[block(1, up)], two.at[j, 0, 1], right),
            self.out(sem + 3, self.part.at[block(0, down)], two.at[j, 1, 0], left),
        )

    def pass_on(self, sem, axis, block, one, two):
        p = self.place
        right, left = p.neighbour(axis, 1), p.neighbour(axis, -1)
        up, down = p.along(axis, 1), p.along(axis, -1)
        j = self.job
        self.relay[0].wait_recv()
        self.add(block(0, up), one.at[j, 0])
        late = self.out(sem, self.part.at[block(0, up)], two.at[j, 0, 0], right)
        self.relay[1].wait_recv()
        self.add(block(1, down), one.at[j, 1])
        self.late = (late, self.out(sem + 1, self.part.at[block(1, down)], two.at[j, 1, 1], left))

    def collect(self, axis, block, two):
        for copy in self.early + self.late:
            copy.wait_recv()
        self.add(block(slice(0, 2), self.place.at(axis)), two.at[self.job, 0], two.at[self.job, 1])

    def step(self, number):
        p = self.place
        if number == 0:
            self.begin(0, self.first, self.first_block, self.far1, self.far2)
        elif number == 1:
            self.pass_on(4, self.first, self.first_block, self.far1, self.far2)
        elif number == 2:
            self.collect(self.first, self.first_block, self.far2)
            self.begin(6, self.second, self.second_block, self.near1, self.near2)
        elif number == 3:
            self.pass_on(10, self.second, self.second_block, self.near1, self.near2)
        elif number == 4:
            self.collect(self.second, self.second_block, self.near2)
            gone = self.part.at[1 - p.zl, p.y, p.x, :, self.lanes]
            self.pair = self.out(12, gone, self.last.at[self.job], p.pair())
        else:
            self.pair.wait_recv()
            mine = self.part[p.zl, p.y, p.x, :, self.lanes].astype(jnp.float32)
            self.done(mine + self.last[self.job].astype(jnp.float32), self.lanes)

    def finish(self):
        for copy in self.sent:
            copy.wait_send()


class Swap:
    sems = 4

    def __init__(self, place, src, relay, dst, send, recv, job):
        self.place, self.src, self.relay, self.dst = place, src, relay, dst
        self.send, self.recv, self.job = send, recv, job
        self.sent = []

    def out(self, sem, src, dst):
        p = self.place
        turn = p.zl if sem % 2 == 0 else 1 - p.zl
        device = {"feat": p.feat(zl=1 - p.zl), "dp": lax.rem(p.dp + turn, 2)}
        copy = remote(src, dst, self.send.at[self.job, sem], self.recv.at[self.job, sem], device)
        copy.start()
        self.sent.append(copy)

    def step(self, number):
        if number == 0:
            for way in (0, 1):
                self.out(way, self.src[way], self.relay[way])
        elif number == 1:
            for way in (0, 1):
                self.sent[way].wait_recv()
                self.out(2 + way, self.relay[way], self.dst[way])
        else:
            for way in (0, 1):
                self.sent[2 + way].wait_recv()

    def finish(self):
        for copy in self.sent:
            copy.wait_send()


def matmul(a, b, over_a=1, over_b=0):
    return lax.dot_general(a, b, (((over_a,), (over_b,)), ((), ())), preferred_element_type=jnp.float32)


CHUNKS = JOBS // 2
SKEW = 3


def band_kernel(
    scale, acts_in, target_ref, bias_ref, enc_bias_ref, enc_in, dec_in, cross_in,
    resid_ref, acts_buf, grad_buf, positive_ref, feats_ref, lower_ref, far_ref, cross_ref,
    enc_n, dec_n, enc_t, dec_t, cross_t, chunk, part, shard, far1, far2, near1, near2, last, relay,
    send_a, recv_a, send_r, recv_r, send_g, recv_g, send_s, recv_s, local_a, local_g, load_sem, chunk_sem, core_send, core_recv,
):
    tokens = acts_in.shape[1]
    wide = tokens // CHUNKS
    lane = wide // 2
    rows = acts_in.shape[0]
    n_feat = feats_ref.shape[0]
    half = cross_ref.shape[2]
    width = 2 * half
    place = Place()
    first_core = place.core == 0

    loads = [
        pltpu.make_async_copy(enc_in, enc_n, load_sem.at[0]),
        pltpu.make_async_copy(dec_in, dec_n, load_sem.at[1]),
        pltpu.make_async_copy(cross_in, cross_ref.at[place.core], load_sem.at[2]),
    ]
    for load in loads:
        load.start()
    place.greet(core=True)

    def swap_cross():
        copy = remote(cross_in, cross_ref.at[place.core], core_send.at[CHUNKS], core_recv.at[CHUNKS], place.other_core())
        copy.start()
        return copy

    def finish_residual(total, lanes):
        resid = total + bias_ref[...] - target_ref[:, lanes].astype(jnp.float32)
        resid_ref[:, lanes] = resid
        shard[:, lanes] = (resid * scale).astype(shard.dtype)

    room = (far1, far2, near1, near2, last)
    gathers, reduces, grads, swaps, lent = [], [], [], [], []
    for job in range(JOBS):
        c, flip, split = job // 2, job % 2, (job // 2) % 2
        lanes = pl.ds(job * lane, lane)
        gathers.append(
            Gather(place, acts_buf, acts_in.at[:, lanes], lanes, flip, split, send_a, recv_a, local_a, job)
        )
        grads.append(Gather(place, grad_buf, shard.at[:, lanes], lanes, flip, split, send_g, recv_g, local_g, job))
        inner = pl.ds(flip * lane, lane)
        done = functools.partial(lambda whole, total, _: finish_residual(total, whole), lanes)
        reduces.append(Reduce(place, part.at[c], inner, flip, room, send_r, recv_r, job, done))
    for c in range(CHUNKS):
        lanes = pl.ds(c * wide, wide)
        ways = [pl.ds(way * (n_feat // 2), n_feat // 2) for way in (0, 1)]
        swaps.append(
            Swap(
                place, [feats_ref.at[w, lanes] for w in ways], [relay.at[c, way] for way in (0, 1)],
                [far_ref.at[w, lanes] for w in ways], send_s, recv_s, c,
            )
        )
        lent.append(
            remote(feats_ref.at[:, lanes], lower_ref.at[:, lanes], core_send.at[c], core_recv.at[c], place.other_core())
        )

    def load_chunk(c):
        return pltpu.make_async_copy(
            acts_buf.at[pl.ds(0, 2), :, :, :, pl.ds(c * wide, wide)], chunk.at[c % 2], chunk_sem.at[c]
        )

    def encode(c):
        load_chunk(c).wait()
        lanes = pl.ds(c * wide, wide)
        pre_act = matmul(enc_t[...], chunk[c % 2].reshape(width, wide)) + enc_bias_ref[...]
        positive = jnp.maximum(pre_act, 0.0)
        positive_ref[:, lanes] = positive
        feats_ref[:, lanes] = (positive * positive).astype(feats_ref.dtype)

        @pl.when(first_core)
        def _():
            lent[c].start()

        swaps[c].step(0)

    def decode(c):
        lanes = pl.ds(c * wide, wide)
        block = SIDE * rows

        def store(i, total):
            part[c, lax.div(i, SIDE), lax.rem(i, SIDE)] = total.astype(part.dtype).reshape(SIDE, rows, wide)

        def at(i):
            return pl.ds(pl.multiple_of(i * block, 16), block)

        @pl.when(first_core)
        def _():
            @pl.loop(0, 2 * SIDE)
            def _(i):
                store(i, matmul(dec_t[at(i), :], feats_ref[:, lanes]))

        @pl.when(jnp.logical_not(first_core))
        def _():
            lent[c].wait_recv()

            @pl.loop(0, 2 * SIDE)
            def _(i):
                total = matmul(dec_t[at(i), :], feats_ref[:, lanes]) + matmul(cross_t[at(i), :], lower_ref[:, lanes])
                store(i, total)

    cross_swap = []

    def turn_enc(i):
        if i == 0:
            loads[0].wait()
        block = pl.ds(i * n_feat, n_feat)
        enc_t[:, block] = enc_n[block, :].T

    def turn_dec(i):
        if i == 0:
            loads[1].wait()
        block = pl.ds(i * n_feat, n_feat)
        dec_t[block, :] = dec_n[:, block].T

    def turn_cross(i):
        if i == 0:
            loads[2].wait()
            cross_swap[0].wait_recv()
        z, at = divmod(i * 256, half)
        cross_t[pl.ds(i * 256, 256), :] = cross_ref[z, :, pl.ds(at, 256)].T

    background = [functools.partial(turn_enc, i) for i in range(width // n_feat)]
    background += [functools.partial(turn_dec, i) for i in range(width // n_feat)]
    background += [functools.partial(turn_cross, i) for i in range(width // 256)]

    def finish_gather(c):
        for job in (2 * c, 2 * c + 1):
            gathers[job].step(Gather.steps - 1)
        load_chunk(c).start()

    def line(c):
        pair = (2 * c, 2 * c + 1)
        steps = [[functools.partial(gathers[j].step, n) for j in pair] for n in range(Gather.steps - 1)]
        steps.append([functools.partial(finish_gather, c)])
        steps += [[functools.partial(encode, c)], [functools.partial(decode, c)]]
        steps += [[functools.partial(reduces[j].step, n) for j in pair] for n in range(Reduce.steps)]
        steps[-1].append(functools.partial(swaps[c].step, 1))
        steps += [[functools.partial(grads[j].step, n) for j in pair] for n in range(Gather.steps)]
        return steps

    lines = [line(c) for c in range(CHUNKS)]
    length = len(lines[0])
    for tick in range(length + SKEW * (CHUNKS - 1)):
        for c in range(CHUNKS):
            at = tick - SKEW * c
            if 0 <= at < length:
                for step in lines[c][at]:
                    step()
        if tick == 0:
            cross_swap.append(swap_cross())
        elif background:
            for _ in range(6):
                if background:
                    background.pop(0)()
    for swap in swaps:
        swap.step(2)
    for job in gathers + reduces + grads + swaps:
        job.finish()
    cross_swap[0].wait_send()

    @pl.when(first_core)
    def _():
        for copy in lent:
            copy.wait_send()


def band(acts, targets, bias, enc_bias, enc, dec_own, dec_cross, scale):
    rows, tokens = targets.shape
    width, n_feat = enc.shape
    lane = tokens // JOBS
    wide = tokens // CHUNKS
    kind = acts.dtype
    whole = pl.BlockSpec(memory_space=pltpu.VMEM)
    away = pl.BlockSpec(memory_space=pl.ANY)
    gathered = jax.ShapeDtypeStruct((3, SIDE, SIDE, rows, tokens), kind)
    feats = jax.ShapeDtypeStruct((n_feat, tokens), kind)
    dma = pltpu.SemaphoreType.DMA
    return pl.pallas_call(
        functools.partial(band_kernel, scale),
        out_shape=(
            jax.ShapeDtypeStruct((rows, tokens), jnp.float32),
            gathered,
            gathered,
            jax.ShapeDtypeStruct((n_feat, tokens), jnp.float32),
            feats,
            feats,
            feats,
            jax.ShapeDtypeStruct((2,) + dec_cross.shape, kind),
        ),
        in_specs=[whole] * 4 + [away] * 3,
        out_specs=(whole, away, away) + (whole,) * 5,
        scratch_shapes=[
            pltpu.VMEM((width, n_feat), kind),
            pltpu.VMEM((n_feat, width), kind),
            pltpu.VMEM((n_feat, width), kind),
            pltpu.VMEM((width, n_feat), kind),
            pltpu.VMEM((width, n_feat), kind),
            pltpu.VMEM((2, 2, SIDE, SIDE, rows, wide), kind),
            pltpu.VMEM((CHUNKS, 2, SIDE, SIDE, rows, wide), kind),
            pltpu.VMEM((rows, tokens), kind),
            pltpu.VMEM((JOBS, 2, SIDE, rows, lane), kind),
            pltpu.VMEM((JOBS, 2, 2, SIDE, rows, lane), kind),
            pltpu.VMEM((JOBS, 2, rows, lane), kind),
            pltpu.VMEM((JOBS, 2, 2, rows, lane), kind),
            pltpu.VMEM((JOBS, rows, lane), kind),
            pltpu.VMEM((CHUNKS, 2, n_feat // 2, wide), kind),
            dma((JOBS, Gather.sems)),
            dma((JOBS, Gather.sems)),
            dma((JOBS, Reduce.sems)),
            dma((JOBS, Reduce.sems)),
            dma((JOBS, Gather.sems)),
            dma((JOBS, Gather.sems)),
            dma((CHUNKS, Swap.sems)),
            dma((CHUNKS, Swap.sems)),
            dma((JOBS,)),
            dma((JOBS,)),
            dma((3,)),
            dma((CHUNKS,)),
            dma((CHUNKS + 1,)),
            dma((CHUNKS + 1,)),
        ],
        compiler_params=pltpu.CompilerParams(
            collective_id=1, has_side_effects=True, vmem_limit_bytes=60 * 1024 * 1024
        ),
        name="band",
    )(acts, targets, bias, enc_bias, enc, dec_own, dec_cross)


def dot(a, b, over_a, over_b):
    return lax.dot_general(a, b, (((over_a,), (over_b,)), ((), ())), preferred_element_type=jnp.float32)


def local(acts, targets, enc, enc_bias, dec_own, dec_cross, dec_bias):
    tokens, rows = acts.shape[1:]
    n_dp = lax.axis_size("dp")
    width = enc.shape[1]
    half = width // 2
    feats_here = enc.shape[2]
    scale = float(tokens * n_dp) ** (-0.5)
    core, dp = lax.axis_index("layer"), lax.axis_index("dp")
    swap = [(0, 1), (1, 0)]
    bf16, f32 = jnp.bfloat16, jnp.float32

    bias = dec_bias.astype(f32).reshape(rows, 1)
    residual, gathered, grads, positive, features, lower, features_far, cross_both = band(
        acts[0].T, targets[0].T, bias, enc_bias.reshape(feats_here, 1), enc[0], dec_own[0], dec_cross, scale
    )
    cross = jnp.concatenate([cross_both[0], cross_both[1]], axis=1)

    grad_out = grads[:2].reshape(width, tokens)
    grad_far = grads[2].reshape(half, tokens)
    down = lax.ppermute(dot(cross, grad_out, 1, 0).astype(bf16), "layer", [(1, 0)])
    lent = lax.ppermute(grad_out[:half], "layer", [(1, 0)])
    grad_feats = dot(dec_own[0], grad_out, 1, 0) + down.astype(f32)
    grad_pre = (grad_feats * 2.0 * positive).astype(bf16)
    grad_pre_far = lax.ppermute(grad_pre, "dp", swap)

    first = jnp.where(core == 0, features, lower)
    own_half = jnp.where(core == 0, lent, grad_out[half:])
    by_dp = dot(first, own_half, 1, 1).reshape(feats_here, n_dp, half // n_dp)
    kept = lax.dynamic_index_in_dim(by_dp, dp, 1, keepdims=False)
    given = lax.dynamic_index_in_dim(by_dp, 1 - dp, 1, keepdims=False).astype(bf16)
    grad_cross = kept + lax.ppermute(given, "dp", swap).astype(f32)

    grad_half = lax.dynamic_index_in_dim(grads, dp, 0, keepdims=False).reshape(half, tokens)
    grad_own = dot(features, grad_half, 1, 1) + dot(features_far, grad_far, 1, 1)
    acts_half = lax.dynamic_index_in_dim(gathered, dp, 0, keepdims=False).reshape(half, tokens)
    acts_far = gathered[2].reshape(half, tokens)
    grad_enc = dot(acts_half, grad_pre, 1, 1) + dot(acts_far, grad_pre_far, 1, 1)
    return (residual.T[None], grad_enc[None], grad_own[None], grad_cross)


def solution(mesh):
    in_specs = (
        P("layer", "dp", "feat"),
        P("layer", "dp", "feat"),
        P("layer", None, "feat"),
        P("layer", "feat"),
        P("layer", "feat", None),
        P("feat", "layer"),
        P("layer", "feat"),
    )
    out_specs = (
        P("layer", "dp", "feat"),
        P("layer", "dp", "feat"),
        P("layer", "feat", "dp"),
        P("feat", ("layer", "dp")),
    )
    return jax.shard_map(local, mesh=mesh, in_specs=in_specs, out_specs=out_specs, check_vma=False)
```

```python
import functools

import jax
import jax.numpy as jnp
from jax import lax
from jax.experimental import pallas as pl
from jax.experimental.pallas import tpu as pltpu
from jax.sharding import PartitionSpec as P

MESH = pl.DeviceIdType.MESH
ALL = slice(None)
SIDE = 4
JOBS = 8


class Place:
    def __init__(self):
        feat = lax.axis_index("feat")
        self.core = lax.axis_index("layer")
        self.dp = lax.axis_index("dp")
        self.x = lax.rem(feat, SIDE)
        self.y = lax.rem(lax.div(feat, SIDE), SIDE)
        self.zl = lax.div(feat, SIDE * SIDE)

    def feat(self, zl=None, y=None, x=None):
        zl = self.zl if zl is None else zl
        y = self.y if y is None else y
        x = self.x if x is None else x
        return (zl * SIDE + y) * SIDE + x

    def at(self, axis):
        return self.x if axis == "x" else self.y

    def along(self, axis, step):
        return lax.rem(self.at(axis) + (step + SIDE), SIDE)

    def neighbour(self, axis, step):
        return {"feat": self.feat(**{axis: self.along(axis, step)})}

    def pair(self):
        return {"feat": self.feat(zl=1 - self.zl)}

    def across(self, zl):
        return {"feat": self.feat(zl=zl), "dp": 1 - self.dp}

    def other_core(self):
        return {"layer": 1 - self.core}

    def greet(self):
        peers = [self.neighbour(a, s) for a in "xy" for s in (1, -1)]
        peers += [self.pair(), self.across(0), self.across(1)]
        peers.append(self.other_core())
        peers += [dict(self.pair(), **self.other_core()), dict(self.across(1 - self.zl), **self.other_core())]
        barrier = pltpu.get_barrier_semaphore()
        for peer in peers:
            pl.semaphore_signal(barrier, inc=1, device_id=peer, device_id_type=MESH)
        pl.semaphore_wait(barrier, len(peers))


def remote(src, dst, send, recv, device):
    return pltpu.make_async_remote_copy(
        src_ref=src, dst_ref=dst, send_sem=send, recv_sem=recv, device_id=device, device_id_type=MESH
    )


class Gather:
    sems = 11
    steps = 6

    def __init__(self, place, buf, own, lanes, flip, split, send, recv, local, job):
        self.place, self.buf, self.own, self.lanes = place, buf, own, lanes
        self.first, self.second = ("y", "x") if flip else ("x", "y")
        self.send, self.recv, self.local, self.job = send, recv, local, job
        self.right, self.left = (slice(0, 2), slice(2, 3)) if split else (slice(0, 1), slice(1, 3))
        self.sent = []

    def first_block(self, slots, at):
        p = self.place
        index = (slots, p.y, at, ALL, self.lanes) if self.first == "x" else (slots, at, p.x, ALL, self.lanes)
        return self.buf.at[index]

    def second_block(self, slots, at):
        index = (slots, at, ALL, ALL, self.lanes) if self.second == "y" else (slots, ALL, at, ALL, self.lanes)
        return self.buf.at[index]

    def copy(self, sem, src, dst, device, recv=None):
        return remote(src, dst, self.send.at[self.job, sem], self.recv.at[self.job, sem if recv is None else recv], device)

    def out(self, sem, block, device):
        copy = self.copy(sem, block, block, device)
        copy.start()
        self.sent.append(copy)
        return copy

    def ring(self, sem, axis, block):
        p = self.place
        own = block(slice(0, 3), p.at(axis))
        return (self.out(sem, own, p.neighbour(axis, 1)), self.out(sem + 1, own, p.neighbour(axis, -1)))

    def forward(self, sem, axis, block):
        p = self.place
        return (
            self.out(sem, block(self.right, p.along(axis, -1)), p.neighbour(axis, 1)),
            self.out(sem + 1, block(self.left, p.along(axis, 1)), p.neighbour(axis, -1)),
        )

    def step(self, number):
        p = self.place
        if number == 0:
            here = self.buf.at[p.zl, p.y, p.x, :, self.lanes]
            self.kept = pltpu.make_async_copy(self.own, here, self.local.at[self.job])
            self.kept.start()
            pair = self.copy(0, self.own, here, p.pair())
            pair.start()
            self.sent.append(pair)
            there = self.buf.at[2, p.y, p.x, :, self.lanes]
            self.cross = [self.copy(1 + zl, self.own, there, p.across(zl), recv=1) for zl in (0, 1)]

            @pl.when(p.zl != p.dp)
            def _():
                for copy in self.cross:
                    copy.start()

            self.waits = [pair, self.cross[0]]
            return
        for copy in self.waits:
            copy.wait_recv()
        if number == 1:
            self.kept.wait()
            self.waits = self.ring(3, self.first, self.first_block)
        elif number == 2:
            self.waits = self.forward(5, self.first, self.first_block)
        elif number == 3:
            self.waits = self.ring(7, self.second, self.second_block)
        elif number == 4:
            self.waits = self.forward(9, self.second, self.second_block)

    def finish(self):
        for copy in self.sent:
            copy.wait_send()
        p = self.place

        @pl.when(p.zl != p.dp)
        def _():
            for copy in self.cross:
                copy.wait_send()


class Reduce:
    sems = 13
    steps = 6

    def __init__(self, place, part, lanes, flip, room, send, recv, job, finish):
        self.place, self.part, self.lanes = place, part, lanes
        self.first, self.second = ("x", "y") if flip else ("y", "x")
        self.far1, self.far2, self.near1, self.near2, self.last = room
        self.send, self.recv, self.job, self.done = send, recv, job, finish
        self.sent = []

    def first_block(self, z, at):
        return (z, at, ALL, ALL, self.lanes) if self.first == "y" else (z, ALL, at, ALL, self.lanes)

    def second_block(self, z, at):
        p = self.place
        return (z, p.y, at, ALL, self.lanes) if self.first == "y" else (z, at, p.x, ALL, self.lanes)

    def out(self, sem, src, dst, device):
        copy = remote(src, dst, self.send.at[self.job, sem], self.recv.at[self.job, sem], device)
        copy.start()
        self.sent.append(copy)
        return copy

    def add(self, index, *refs):
        total = self.part[index].astype(jnp.float32)
        for ref in refs:
            total = total + ref[...].astype(jnp.float32)
        self.part[index] = total.astype(self.part.dtype)

    def begin(self, sem, axis, block, one, two):
        p = self.place
        right, left = p.neighbour(axis, 1), p.neighbour(axis, -1)
        far, up, down = p.along(axis, 2), p.along(axis, 1), p.along(axis, -1)
        j = self.job
        self.relay = (
            self.out(sem, self.part.at[block(0, far)], one.at[j, 0], right),
            self.out(sem + 1, self.part.at[block(1, far)], one.at[j, 1], left),
        )
        self.early = (
            self.out(sem + 2, self.part.at[block(1, up)], two.at[j, 0, 1], right),
            self.out(sem + 3, self.part.at[block(0, down)], two.at[j, 1, 0], left),
        )

    def pass_on(self, sem, axis, block, one, two):
        p = self.place
        right, left = p.neighbour(axis, 1), p.neighbour(axis, -1)
        up, down = p.along(axis, 1), p.along(axis, -1)
        j = self.job
        self.relay[0].wait_recv()
        self.add(block(0, up), one.at[j, 0])
        late = self.out(sem, self.part.at[block(0, up)], two.at[j, 0, 0], right)
        self.relay[1].wait_recv()
        self.add(block(1, down), one.at[j, 1])
        self.late = (late, self.out(sem + 1, self.part.at[block(1, down)], two.at[j, 1, 1], left))

    def collect(self, axis, block, two):
        for copy in self.early + self.late:
            copy.wait_recv()
        self.add(block(slice(0, 2), self.place.at(axis)), two.at[self.job, 0], two.at[self.job, 1])

    def step(self, number):
        p = self.place
        if number == 0:
            self.begin(0, self.first, self.first_block, self.far1, self.far2)
        elif number == 1:
            self.pass_on(4, self.first, self.first_block, self.far1, self.far2)
        elif number == 2:
            self.collect(self.first, self.first_block, self.far2)
            self.begin(6, self.second, self.second_block, self.near1, self.near2)
        elif number == 3:
            self.pass_on(10, self.second, self.second_block, self.near1, self.near2)
        elif number == 4:
            self.collect(self.second, self.second_block, self.near2)
            gone = self.part.at[1 - p.zl, p.y, p.x, :, self.lanes]
            self.pair = self.out(12, gone, self.last.at[self.job], p.pair())
        else:
            self.pair.wait_recv()
            mine = self.part[p.zl, p.y, p.x, :, self.lanes].astype(jnp.float32)
            self.done(mine + self.last[self.job].astype(jnp.float32), self.lanes)

    def finish(self):
        for copy in self.sent:
            copy.wait_send()


class Swap:
    sems = 4

    def __init__(self, place, src, relay, dst, send, recv, job):
        self.place, self.src, self.relay, self.dst = place, src, relay, dst
        self.send, self.recv, self.job = send, recv, job
        self.sent = []

    def device(self, sem):
        p = self.place
        turn = p.zl if sem % 2 == 0 else 1 - p.zl
        return {"feat": p.feat(zl=1 - p.zl), "dp": lax.rem(p.dp + turn, 2)}

    def out(self, sem, src, dst):
        copy = remote(src, dst, self.send.at[self.job, sem], self.recv.at[self.job, sem], self.device(sem))
        copy.start()
        self.sent.append(copy)

    def step(self, number):
        if number == 0:
            for way in (0, 1):
                self.out(way, self.src[way], self.relay[way])
        elif number == 1:
            for way in (0, 1):
                self.sent[way].wait_recv()
                self.out(2 + way, self.relay[way], self.dst[way])
        else:
            for way in (0, 1):
                self.sent[2 + way].wait_recv()

    def finish(self):
        for copy in self.sent:
            copy.wait_send()


class Lend:
    sems = 8

    def __init__(self, place, buf, relay, rows, lanes, send, recv, local, job):
        p = self.place = place
        self.lanes = lanes
        half = SIDE // 2
        self.upper = p.core == 1
        self.upper_own = jnp.logical_and(self.upper, p.dp == 1)
        self.upper_gives = jnp.logical_and(self.upper, p.dp == 0)
        self.lower_gets = jnp.logical_and(p.core == 0, p.dp == 0)
        self.over_z = p.core == 1 - p.dp
        ys = pl.ds(half * p.dp, half)
        own, far = rows.at[0, :, :, :, lanes], rows.at[1, :, :, :, lanes]
        copy = lambda sem, src, dst, device: remote(src, dst, send.at[job, sem], recv.at[job, sem], device)
        self.keep_own = pltpu.make_async_copy(buf.at[1, ys, :, :, lanes], own, local.at[job, 0])
        self.keep_far = pltpu.make_async_copy(buf.at[2, ys, :, :, lanes], far, local.at[job, 1])
        self.give_own = copy(0, buf.at[0, ys, :, :, lanes], own, p.other_core())
        self.give_far = copy(1, buf.at[2, ys, :, :, lanes], far, p.other_core())
        self.first, self.second = [], []
        for way in range(2):
            turn = p.zl if way == 0 else 1 - p.zl
            dp = lax.rem(p.dp + turn, 2)
            device = {"feat": p.feat(zl=1 - p.zl), "dp": dp}
            src = buf.at[p.dp, pl.ds(half * (1 - p.dp) + way, 1), :, :, lanes]
            self.first.append(copy(2 + way, src, relay.at[job, way], device))
            dst = rows.at[1, pl.ds(way, 1), :, :, lanes]
            self.second.append(copy(4 + way, relay.at[job, way], dst, dict(device, layer=1 - dp)))

    def step(self, number):
        if number == 0:

            @pl.when(self.upper)
            def _():
                for copy in self.first + [self.give_own, self.keep_own]:
                    copy.start()

            @pl.when(self.upper_gives)
            def _():
                self.give_far.start()

            @pl.when(self.upper_own)
            def _():
                self.keep_far.start()

        elif number == 1:

            @pl.when(self.upper)
            def _():
                for way in range(2):
                    self.first[way].wait_recv()
                    self.second[way].start()

    def finish(self):
        @pl.when(self.upper)
        def _():
            for copy in self.first + self.second + [self.give_own]:
                copy.wait_send()
            self.keep_own.wait()

        @pl.when(jnp.logical_not(self.upper))
        def _():
            self.give_own.wait_recv()

        @pl.when(self.upper_gives)
        def _():
            self.give_far.wait_send()

        @pl.when(self.upper_own)
        def _():
            self.keep_far.wait()

        @pl.when(self.lower_gets)
        def _():
            self.give_far.wait_recv()

        @pl.when(self.over_z)
        def _():
            for copy in self.second:
                copy.wait_recv()


def matmul(a, b, over_a=1, over_b=0):
    return lax.dot_general(a, b, (((over_a,), (over_b,)), ((), ())), preferred_element_type=jnp.float32)


CHUNKS = JOBS // 2
SKEW = 2


def band_kernel(
    scale, acts_in, target_ref, bias_ref, enc_bias_ref, enc_in, dec_in, cross_in,
    resid_ref, acts_buf, grad_buf, feats_ref, lower_ref, far_ref, far_lower_ref, pre_ref, far_pre_ref, rows_buf,
    relay, pre_relay, rows_relay,
    enc_n, dec_n, enc_t, dec_t, cross_t, cross_ref, positive_ref, down_ref, up_ref,
    chunk, part, shard, far1, far2, near1, near2, last,
    send_a, recv_a, send_r, recv_r, send_g, recv_g, send_s, recv_s, send_p, recv_p, send_l, recv_l,
    local_a, local_g, local_l, load_sem, chunk_sem, grad_sem, core_send, core_recv,
):
    tokens = acts_in.shape[1]
    wide = tokens // CHUNKS
    lane = wide // 2
    rows = acts_in.shape[0]
    n_feat = feats_ref.shape[0]
    half = cross_ref.shape[2]
    width = 2 * half
    place = Place()
    first_core = place.core == 0

    loads = [
        pltpu.make_async_copy(enc_in, enc_n, load_sem.at[0]),
        pltpu.make_async_copy(dec_in, dec_n, load_sem.at[1]),
        pltpu.make_async_copy(cross_in, cross_ref.at[place.core], load_sem.at[2]),
    ]
    for load in loads:
        load.start()
    place.greet()

    def swap_cross():
        at = 3 * CHUNKS
        copy = remote(cross_in, cross_ref.at[place.core], core_send.at[at], core_recv.at[at], place.other_core())
        copy.start()
        return copy

    def finish_residual(total, lanes):
        resid = total + bias_ref[...] - target_ref[:, lanes].astype(jnp.float32)
        resid_ref[:, lanes] = resid
        shard[:, lanes] = (resid * scale).astype(shard.dtype)

    room = (far1, far2, near1, near2, last)
    gathers, reduces, grads, swaps, lent, far_lent, pre_swaps, lends, downs = [], [], [], [], [], [], [], [], []
    for job in range(JOBS):
        c, flip, split = job // 2, job % 2, (job // 2) % 2
        lanes = pl.ds(job * lane, lane)
        gathers.append(
            Gather(place, acts_buf, acts_in.at[:, lanes], lanes, flip, split, send_a, recv_a, local_a, job)
        )
        grads.append(Gather(place, grad_buf, shard.at[:, lanes], lanes, flip, split, send_g, recv_g, local_g, job))
        inner = pl.ds(flip * lane, lane)
        done = functools.partial(lambda whole, total, _: finish_residual(total, whole), lanes)
        reduces.append(Reduce(place, part.at[c], inner, flip, room, send_r, recv_r, job, done))
    for c in range(CHUNKS):
        lanes = pl.ds(c * wide, wide)
        ways = [pl.ds(way * (n_feat // 2), n_feat // 2) for way in (0, 1)]

        def dp_swap(here, between, there, send, recv):
            return Swap(
                place, [here.at[w, lanes] for w in ways], [between.at[c, way] for way in (0, 1)],
                [there.at[w, lanes] for w in ways], send, recv, c,
            )

        def to_core(kind, here, there):
            at = kind * CHUNKS + c
            return remote(
                here.at[:, lanes], there.at[:, lanes], core_send.at[at], core_recv.at[at], place.other_core()
            )

        swaps.append(dp_swap(feats_ref, relay, far_ref, send_s, recv_s))
        pre_swaps.append(dp_swap(pre_ref, pre_relay, far_pre_ref, send_p, recv_p))
        lent.append(to_core(0, feats_ref, lower_ref))
        far_lent.append(to_core(1, far_ref, far_lower_ref))
        downs.append(to_core(2, down_ref, up_ref))
        lends.append(Lend(place, grad_buf, rows_relay, rows_buf, lanes, send_l, recv_l, local_l, c))

    def load_chunk(c):
        return pltpu.make_async_copy(
            acts_buf.at[pl.ds(0, 2), :, :, :, pl.ds(c * wide, wide)], chunk.at[c % 2], chunk_sem.at[c]
        )

    def encode(c):
        load_chunk(c).wait()
        lanes = pl.ds(c * wide, wide)
        pre_act = matmul(enc_t[...], chunk[c % 2].reshape(width, wide)) + enc_bias_ref[...]
        positive = jnp.maximum(pre_act, 0.0)
        positive_ref[:, lanes] = positive
        feats_ref[:, lanes] = (positive * positive).astype(feats_ref.dtype)

        @pl.when(first_core)
        def _():
            lent[c].start()
            lower_ref[:, lanes] = feats_ref[:, lanes]

        swaps[c].step(0)

    def lend_far(c):
        swaps[c].step(2)
        lanes = pl.ds(c * wide, wide)

        @pl.when(first_core)
        def _():
            far_lent[c].start()
            far_lower_ref[:, lanes] = far_ref[:, lanes]

    def decode(c):
        lanes = pl.ds(c * wide, wide)
        block = SIDE * rows

        def store(i, total):
            part[c, lax.div(i, SIDE), lax.rem(i, SIDE)] = total.astype(part.dtype).reshape(SIDE, rows, wide)

        def at(i):
            return pl.ds(pl.multiple_of(i * block, 16), block)

        @pl.when(first_core)
        def _():
            @pl.loop(0, 2 * SIDE)
            def _(i):
                store(i, matmul(dec_t[at(i), :], feats_ref[:, lanes]))

        @pl.when(jnp.logical_not(first_core))
        def _():
            lent[c].wait_recv()

            @pl.loop(0, 2 * SIDE)
            def _(i):
                total = matmul(dec_t[at(i), :], feats_ref[:, lanes]) + matmul(cross_t[at(i), :], lower_ref[:, lanes])
                store(i, total)

    def load_grads(c):
        return pltpu.make_async_copy(
            grad_buf.at[pl.ds(0, 2), :, :, :, pl.ds(c * wide, wide)], chunk.at[c % 2], grad_sem.at[c]
        )

    def finish_grads(c):
        for job in (2 * c, 2 * c + 1):
            grads[job].step(Gather.steps - 1)
        load_grads(c).start()
        lends[c].step(0)

    def backward(c):
        lanes = pl.ds(c * wide, wide)
        load_grads(c).wait()
        here = chunk.at[c % 2]

        @pl.when(jnp.logical_not(first_core))
        def _():
            down = matmul(cross_ref[0], here[0].reshape(half, wide)) + matmul(cross_ref[1], here[1].reshape(half, wide))
            down_ref[:, lanes] = down.astype(down_ref.dtype)
            downs[c].start()

        grad_feats = matmul(dec_n[...], here[...].reshape(width, wide))

        @pl.when(first_core)
        def _():
            downs[c].wait_recv()
            total = grad_feats + up_ref[:, lanes].astype(jnp.float32)
            pre_ref[:, lanes] = (total * 2.0 * positive_ref[:, lanes]).astype(pre_ref.dtype)

        @pl.when(jnp.logical_not(first_core))
        def _():
            pre_ref[:, lanes] = (grad_feats * 2.0 * positive_ref[:, lanes]).astype(pre_ref.dtype)

        pre_swaps[c].step(0)

    cross_swap = []

    def turn_enc(i):
        if i == 0:
            loads[0].wait()
        block = pl.ds(i * n_feat, n_feat)
        enc_t[:, block] = enc_n[block, :].T

    def turn_dec(i):
        if i == 0:
            loads[1].wait()
        block = pl.ds(i * n_feat, n_feat)
        dec_t[block, :] = dec_n[:, block].T

    def turn_cross(i):
        if i == 0:
            loads[2].wait()
            cross_swap[0].wait_recv()
        z, at = divmod(i * 256, half)
        cross_t[pl.ds(i * 256, 256), :] = cross_ref[z, :, pl.ds(at, 256)].T

    background = [functools.partial(turn_enc, i) for i in range(width // n_feat)]
    background += [functools.partial(turn_dec, i) for i in range(width // n_feat)]
    background += [functools.partial(turn_cross, i) for i in range(width // 256)]

    def finish_gather(c):
        for job in (2 * c, 2 * c + 1):
            gathers[job].step(Gather.steps - 1)
        load_chunk(c).start()

    def line(c):
        pair = (2 * c, 2 * c + 1)
        steps = [[functools.partial(gathers[j].step, n) for j in pair] for n in range(Gather.steps - 1)]
        steps.append([functools.partial(finish_gather, c)])
        steps += [[functools.partial(encode, c)], [functools.partial(decode, c)]]
        steps += [[functools.partial(reduces[j].step, n) for j in pair] for n in range(Reduce.steps)]
        steps[-1].append(functools.partial(swaps[c].step, 1))
        steps += [[functools.partial(grads[j].step, n) for j in pair] for n in range(Gather.steps - 1)]
        steps[-2].append(functools.partial(lend_far, c))
        steps += [[functools.partial(finish_grads, c)], [functools.partial(backward, c)]]
        steps.append([functools.partial(pre_swaps[c].step, 1), functools.partial(lends[c].step, 1)])
        return steps

    lines = [line(c) for c in range(CHUNKS)]
    length = len(lines[0])
    for tick in range(length + SKEW * (CHUNKS - 1)):
        for c in reversed(range(CHUNKS)):
            at = tick - SKEW * c
            if 0 <= at < length:
                for step in lines[c][at]:
                    step()
        if tick == 0:
            cross_swap.append(swap_cross())
        elif background:
            for _ in range(6):
                if background:
                    background.pop(0)()
    for swap in pre_swaps:
        swap.step(2)
    for job in gathers + reduces + grads + swaps + pre_swaps + lends:
        job.finish()
    cross_swap[0].wait_send()

    @pl.when(first_core)
    def _():
        for copy in lent + far_lent:
            copy.wait_send()

    @pl.when(jnp.logical_not(first_core))
    def _():
        for copy in far_lent:
            copy.wait_recv()
        for copy in downs:
            copy.wait_send()


def band(acts, targets, bias, enc_bias, enc, dec_own, dec_cross, scale):
    rows, tokens = targets.shape
    width, n_feat = enc.shape
    lane = tokens // JOBS
    wide = tokens // CHUNKS
    kind = acts.dtype
    whole = pl.BlockSpec(memory_space=pltpu.VMEM)
    away = pl.BlockSpec(memory_space=pl.ANY)
    gathered = jax.ShapeDtypeStruct((3, SIDE, SIDE, rows, tokens), kind)
    feats = jax.ShapeDtypeStruct((n_feat, tokens), kind)
    dma = pltpu.SemaphoreType.DMA
    return pl.pallas_call(
        functools.partial(band_kernel, scale),
        out_shape=(
            jax.ShapeDtypeStruct((rows, tokens), jnp.float32),
            gathered,
            gathered,
            feats, feats, feats, feats, feats, feats,
            jax.ShapeDtypeStruct((2, SIDE // 2, SIDE, rows, tokens), kind),
            jax.ShapeDtypeStruct((CHUNKS, 2, n_feat // 2, wide), kind),
            jax.ShapeDtypeStruct((CHUNKS, 2, n_feat // 2, wide), kind),
            jax.ShapeDtypeStruct((CHUNKS, 2, 1, SIDE, rows, wide), kind),
        ),
        in_specs=[whole] * 4 + [away] * 3,
        out_specs=(whole, away, away) + (whole,) * 6 + (away,) * 4,
        scratch_shapes=[
            pltpu.VMEM((width, n_feat), kind),
            pltpu.VMEM((n_feat, width), kind),
            pltpu.VMEM((n_feat, width), kind),
            pltpu.VMEM((width, n_feat), kind),
            pltpu.VMEM((width, n_feat), kind),
            pltpu.VMEM((2,) + dec_cross.shape, kind),
            pltpu.VMEM((n_feat, tokens), jnp.float32),
            pltpu.VMEM((n_feat, tokens), kind),
            pltpu.VMEM((n_feat, tokens), kind),
            pltpu.VMEM((2, 2, SIDE, SIDE, rows, wide), kind),
            pltpu.VMEM((CHUNKS, 2, SIDE, SIDE, rows, wide), kind),
            pltpu.VMEM((rows, tokens), kind),
            pltpu.VMEM((JOBS, 2, SIDE, rows, lane), kind),
            pltpu.VMEM((JOBS, 2, 2, SIDE, rows, lane), kind),
            pltpu.VMEM((JOBS, 2, rows, lane), kind),
            pltpu.VMEM((JOBS, 2, 2, rows, lane), kind),
            pltpu.VMEM((JOBS, rows, lane), kind),
            dma((JOBS, Gather.sems)),
            dma((JOBS, Gather.sems)),
            dma((JOBS, Reduce.sems)),
            dma((JOBS, Reduce.sems)),
            dma((JOBS, Gather.sems)),
            dma((JOBS, Gather.sems)),
            dma((CHUNKS, Swap.sems)),
            dma((CHUNKS, Swap.sems)),
            dma((CHUNKS, Swap.sems)),
            dma((CHUNKS, Swap.sems)),
            dma((CHUNKS, Lend.sems)),
            dma((CHUNKS, Lend.sems)),
            dma((JOBS,)),
            dma((JOBS,)),
            dma((CHUNKS, 2)),
            dma((3,)),
            dma((CHUNKS,)),
            dma((CHUNKS,)),
            dma((3 * CHUNKS + 1,)),
            dma((3 * CHUNKS + 1,)),
        ],
        compiler_params=pltpu.CompilerParams(
            collective_id=1, has_side_effects=True, vmem_limit_bytes=60 * 1024 * 1024
        ),
        name="band",
    )(acts, targets, bias, enc_bias, enc, dec_own, dec_cross)


def weights_kernel(
    acts_in, grads_in, rows_in, feats_in, far_in, first_in, far_first_in, pre_in, far_pre_in,
    enc_out, own_out, cross_out,
    acts, grads, rows, feats, first, pre, enc_g, own_g, cross_g, load_sem, store_sem,
):
    dp = lax.axis_index("dp")
    half = SIDE // 2
    n_feat, width = own_g.shape
    block = width // 2
    started = []

    def load(src, dst):
        copy = pltpu.make_async_copy(src, dst, load_sem.at[len(started)])
        copy.start()
        started.append(copy)
        return copy

    ys = [pl.ds(half * part, half) for part in (0, 1)]
    first_loads = [load(feats_in, feats.at[0]), load(far_in, feats.at[1])]
    grad_loads = [[load(grads_in.at[slot, y], grads.at[i, y]) for i, slot in ((0, dp), (1, 2))] for y in ys]
    pre_loads = [load(pre_in, pre.at[0]), load(far_pre_in, pre.at[1])]
    act_loads = [[load(acts_in.at[slot, y], acts.at[i, y]) for i, slot in ((0, dp), (1, 2))] for y in ys]
    cross_loads = [load(first_in, first.at[0]), load(far_first_in, first.at[1]), load(rows_in, rows)]
    stores = []

    def store(src, dst):
        copy = pltpu.make_async_copy(src, dst, store_sem.at[len(stores)])
        copy.start()
        stores.append(copy)

    def both(a, b):
        return matmul(a[0], b[0], 1, 1) + matmul(a[1], b[1], 1, 1)

    step = n_feat // 2

    def by_feats(left, right, out, columns):
        @pl.loop(0, 2)
        def _(m):
            at = pl.ds(pl.multiple_of(m * step, step), step)
            out[at, columns] = both((left[0, at, :], left[1, at, :]), right())

    for copy in first_loads:
        copy.wait()
    for part in (0, 1):
        for copy in grad_loads[part]:
            copy.wait()
        columns = pl.ds(part * block, block)
        by_feats(feats, lambda: [grads[i, ys[part]].reshape(block, -1) for i in (0, 1)], own_g, columns)
        store(own_g.at[:, columns], own_out.at[:, columns])
    for copy in pre_loads:
        copy.wait()
    for part in (0, 1):
        for copy in act_loads[part]:
            copy.wait()
        for y in range(half * part, half * part + half):
            at = pl.ds(y * (width // SIDE), width // SIDE)
            enc_g[at, :] = both([acts[i, y].reshape(width // SIDE, -1) for i in (0, 1)], [pre[0], pre[1]])
            store(enc_g.at[at, :], enc_out.at[at, :])
    for copy in cross_loads:
        copy.wait()
    by_feats(first, lambda: [rows[i].reshape(block, -1) for i in (0, 1)], cross_g, pl.ds(0, block))
    store(cross_g, cross_out)
    for copy in stores:
        copy.wait()


def weights(acts, grads, lent, feats, far, first, far_first, pre, far_pre):
    rows, tokens = acts.shape[3:]
    n_feat = feats.shape[0]
    half = SIDE * SIDE * rows
    kind = acts.dtype
    f32 = jnp.float32
    away = pl.BlockSpec(memory_space=pl.ANY)
    shapes = [(half, n_feat), (n_feat, half), (n_feat, half // 2)]
    return pl.pallas_call(
        weights_kernel,
        out_shape=[jax.ShapeDtypeStruct(s, f32) for s in shapes],
        in_specs=[away] * 9,
        out_specs=[away] * 3,
        scratch_shapes=[
            pltpu.VMEM((2, SIDE, SIDE, rows, tokens), kind),
            pltpu.VMEM((2, SIDE, SIDE, rows, tokens), kind),
            pltpu.VMEM(lent.shape, kind),
            pltpu.VMEM((2, n_feat, tokens), kind),
            pltpu.VMEM((2, n_feat, tokens), kind),
            pltpu.VMEM((2, n_feat, tokens), kind),
        ]
        + [pltpu.VMEM(s, f32) for s in shapes]
        + [pltpu.SemaphoreType.DMA((16,)), pltpu.SemaphoreType.DMA((8,))],
        compiler_params=pltpu.CompilerParams(vmem_limit_bytes=60 * 1024 * 1024),
        name="weights",
    )(acts, grads, lent, feats, far, first, far_first, pre, far_pre)


def local(acts, targets, enc, enc_bias, dec_own, dec_cross, dec_bias):
    tokens, rows = acts.shape[1:]
    scale = float(tokens * lax.axis_size("dp")) ** (-0.5)
    bias = dec_bias.astype(jnp.float32).reshape(rows, 1)
    residual, gathered, grads, feats, first, far, far_first, pre, far_pre, lent = band(
        acts[0].T, targets[0].T, bias, enc_bias.reshape(-1, 1), enc[0], dec_own[0], dec_cross, scale
    )[:10]
    grad_enc, grad_own, grad_cross = weights(gathered, grads, lent, feats, far, first, far_first, pre, far_pre)
    return (residual.T[None], grad_enc[None], grad_own[None], grad_cross)


def solution(mesh):
    in_specs = (
        P("layer", "dp", "feat"),
        P("layer", "dp", "feat"),
        P("layer", None, "feat"),
        P("layer", "feat"),
        P("layer", "feat", None),
        P("feat", "layer"),
        P("layer", "feat"),
    )
    out_specs = (
        P("layer", "dp", "feat"),
        P("layer", "dp", "feat"),
        P("layer", "feat", "dp"),
        P("feat", ("layer", "dp")),
    )
    return jax.shard_map(local, mesh=mesh, in_specs=in_specs, out_specs=out_specs, check_vma=False)
```

```python
import functools

import jax
import jax.numpy as jnp
from jax import lax
from jax.experimental import pallas as pl
from jax.experimental.pallas import tpu as pltpu
from jax.sharding import PartitionSpec as P

MESH = pl.DeviceIdType.MESH
ALL = slice(None)
SIDE = 4
JOBS = 8


class Place:
    def __init__(self):
        feat = lax.axis_index("feat")
        self.core = lax.axis_index("layer")
        self.dp = lax.axis_index("dp")
        self.x = lax.rem(feat, SIDE)
        self.y = lax.rem(lax.div(feat, SIDE), SIDE)
        self.zl = lax.div(feat, SIDE * SIDE)

    def feat(self, zl=None, y=None, x=None):
        zl = self.zl if zl is None else zl
        y = self.y if y is None else y
        x = self.x if x is None else x
        return (zl * SIDE + y) * SIDE + x

    def at(self, axis):
        return self.x if axis == "x" else self.y

    def along(self, axis, step):
        return lax.rem(self.at(axis) + (step + SIDE), SIDE)

    def neighbour(self, axis, step):
        return {"feat": self.feat(**{axis: self.along(axis, step)})}

    def pair(self):
        return {"feat": self.feat(zl=1 - self.zl)}

    def across(self, zl):
        return {"feat": self.feat(zl=zl), "dp": 1 - self.dp}

    def other_core(self):
        return {"layer": 1 - self.core}

    def greet(self):
        peers = [self.neighbour(a, s) for a in "xy" for s in (1, -1)]
        peers += [self.pair(), self.across(0), self.across(1)]
        peers.append(self.other_core())
        peers += [dict(self.pair(), **self.other_core()), dict(self.across(1 - self.zl), **self.other_core())]
        barrier = pltpu.get_barrier_semaphore()
        for peer in peers:
            pl.semaphore_signal(barrier, inc=1, device_id=peer, device_id_type=MESH)
        pl.semaphore_wait(barrier, len(peers))


def remote(src, dst, send, recv, device):
    return pltpu.make_async_remote_copy(
        src_ref=src, dst_ref=dst, send_sem=send, recv_sem=recv, device_id=device, device_id_type=MESH
    )


class Gather:
    sems = 11
    steps = 6

    def __init__(self, place, buf, own, lanes, flip, split, send, recv, local, job):
        self.place, self.buf, self.own, self.lanes = place, buf, own, lanes
        self.first, self.second = ("y", "x") if flip else ("x", "y")
        self.send, self.recv, self.local, self.job = send, recv, local, job
        self.right, self.left = (slice(0, 2), slice(2, 3)) if split else (slice(0, 1), slice(1, 3))
        self.sent = []

    def first_block(self, slots, at):
        p = self.place
        index = (slots, p.y, at, ALL, self.lanes) if self.first == "x" else (slots, at, p.x, ALL, self.lanes)
        return self.buf.at[index]

    def second_block(self, slots, at):
        index = (slots, at, ALL, ALL, self.lanes) if self.second == "y" else (slots, ALL, at, ALL, self.lanes)
        return self.buf.at[index]

    def copy(self, sem, src, dst, device, recv=None):
        return remote(src, dst, self.send.at[self.job, sem], self.recv.at[self.job, sem if recv is None else recv], device)

    def out(self, sem, block, device):
        copy = self.copy(sem, block, block, device)
        copy.start()
        self.sent.append(copy)
        return copy

    def ring(self, sem, axis, block):
        p = self.place
        own = block(slice(0, 3), p.at(axis))
        return (self.out(sem, own, p.neighbour(axis, 1)), self.out(sem + 1, own, p.neighbour(axis, -1)))

    def forward(self, sem, axis, block):
        p = self.place
        return (
            self.out(sem, block(self.right, p.along(axis, -1)), p.neighbour(axis, 1)),
            self.out(sem + 1, block(self.left, p.along(axis, 1)), p.neighbour(axis, -1)),
        )

    def step(self, number):
        p = self.place
        if number == 0:
            here = self.buf.at[p.zl, p.y, p.x, :, self.lanes]
            self.kept = pltpu.make_async_copy(self.own, here, self.local.at[self.job])
            self.kept.start()
            pair = self.copy(0, self.own, here, p.pair())
            pair.start()
            self.sent.append(pair)
            there = self.buf.at[2, p.y, p.x, :, self.lanes]
            self.cross = [self.copy(1 + zl, self.own, there, p.across(zl), recv=1) for zl in (0, 1)]

            @pl.when(p.zl != p.dp)
            def _():
                for copy in self.cross:
                    copy.start()

            self.waits = [pair, self.cross[0]]
            return
        for copy in self.waits:
            copy.wait_recv()
        if number == 1:
            self.kept.wait()
            self.waits = self.ring(3, self.first, self.first_block)
        elif number == 2:
            self.waits = self.forward(5, self.first, self.first_block)
        elif number == 3:
            self.waits = self.ring(7, self.second, self.second_block)
        elif number == 4:
            self.waits = self.forward(9, self.second, self.second_block)

    def finish(self):
        for copy in self.sent:
            copy.wait_send()
        p = self.place

        @pl.when(p.zl != p.dp)
        def _():
            for copy in self.cross:
                copy.wait_send()


class Reduce:
    sems = 13
    steps = 6

    def __init__(self, place, part, lanes, flip, room, send, recv, job, finish):
        self.place, self.part, self.lanes = place, part, lanes
        self.first, self.second = ("x", "y") if flip else ("y", "x")
        self.far1, self.far2, self.near1, self.near2, self.last = room
        self.send, self.recv, self.job, self.done = send, recv, job, finish
        self.sent = []

    def first_block(self, z, at):
        return (z, at, ALL, ALL, self.lanes) if self.first == "y" else (z, ALL, at, ALL, self.lanes)

    def second_block(self, z, at):
        p = self.place
        return (z, p.y, at, ALL, self.lanes) if self.first == "y" else (z, at, p.x, ALL, self.lanes)

    def out(self, sem, src, dst, device):
        copy = remote(src, dst, self.send.at[self.job, sem], self.recv.at[self.job, sem], device)
        copy.start()
        self.sent.append(copy)
        return copy

    def add(self, index, *refs):
        total = self.part[index].astype(jnp.float32)
        for ref in refs:
            total = total + ref[...].astype(jnp.float32)
        self.part[index] = total.astype(self.part.dtype)

    def begin(self, sem, axis, block, one, two):
        p = self.place
        right, left = p.neighbour(axis, 1), p.neighbour(axis, -1)
        far, up, down = p.along(axis, 2), p.along(axis, 1), p.along(axis, -1)
        j = self.job
        self.relay = (
            self.out(sem, self.part.at[block(0, far)], one.at[j, 0], right),
            self.out(sem + 1, self.part.at[block(1, far)], one.at[j, 1], left),
        )
        self.early = (
            self.out(sem + 2, self.part.at[block(1, up)], two.at[j, 0, 1], right),
            self.out(sem + 3, self.part.at[block(0, down)], two.at[j, 1, 0], left),
        )

    def pass_on(self, sem, axis, block, one, two):
        p = self.place
        right, left = p.neighbour(axis, 1), p.neighbour(axis, -1)
        up, down = p.along(axis, 1), p.along(axis, -1)
        j = self.job
        self.relay[0].wait_recv()
        self.add(block(0, up), one.at[j, 0])
        late = self.out(sem, self.part.at[block(0, up)], two.at[j, 0, 0], right)
        self.relay[1].wait_recv()
        self.add(block(1, down), one.at[j, 1])
        self.late = (late, self.out(sem + 1, self.part.at[block(1, down)], two.at[j, 1, 1], left))

    def collect(self, axis, block, two):
        for copy in self.early + self.late:
            copy.wait_recv()
        self.add(block(slice(0, 2), self.place.at(axis)), two.at[self.job, 0], two.at[self.job, 1])

    def step(self, number):
        p = self.place
        if number == 0:
            self.begin(0, self.first, self.first_block, self.far1, self.far2)
        elif number == 1:
            self.pass_on(4, self.first, self.first_block, self.far1, self.far2)
        elif number == 2:
            self.collect(self.first, self.first_block, self.far2)
            self.begin(6, self.second, self.second_block, self.near1, self.near2)
        elif number == 3:
            self.pass_on(10, self.second, self.second_block, self.near1, self.near2)
        elif number == 4:
            self.collect(self.second, self.second_block, self.near2)
            gone = self.part.at[1 - p.zl, p.y, p.x, :, self.lanes]
            self.pair = self.out(12, gone, self.last.at[self.job], p.pair())
        else:
            self.pair.wait_recv()
            mine = self.part[p.zl, p.y, p.x, :, self.lanes].astype(jnp.float32)
            self.done(mine + self.last[self.job].astype(jnp.float32), self.lanes)

    def finish(self):
        for copy in self.sent:
            copy.wait_send()


class Swap:
    sems = 4

    def __init__(self, place, src, relay, dst, send, recv, job):
        self.place, self.src, self.relay, self.dst = place, src, relay, dst
        self.send, self.recv, self.job = send, recv, job
        self.sent = []

    def device(self, sem):
        p = self.place
        turn = p.zl if sem % 2 == 0 else 1 - p.zl
        return {"feat": p.feat(zl=1 - p.zl), "dp": lax.rem(p.dp + turn, 2)}

    def out(self, sem, src, dst):
        copy = remote(src, dst, self.send.at[self.job, sem], self.recv.at[self.job, sem], self.device(sem))
        copy.start()
        self.sent.append(copy)

    def step(self, number):
        if number == 0:
            for way in (0, 1):
                self.out(way, self.src[way], self.relay[way])
        elif number == 1:
            for way in (0, 1):
                self.sent[way].wait_recv()
                self.out(2 + way, self.relay[way], self.dst[way])
        else:
            for way in (0, 1):
                self.sent[2 + way].wait_recv()

    def finish(self):
        for copy in self.sent:
            copy.wait_send()


class Lend:
    sems = 8

    def __init__(self, place, buf, relay, rows, lanes, send, recv, job):
        p = self.place = place
        self.lanes = lanes
        half = SIDE // 2
        self.upper = p.core == 1
        self.upper_gives = jnp.logical_and(self.upper, p.dp == 0)
        self.lower_gets = jnp.logical_and(p.core == 0, p.dp == 0)
        self.over_z = p.core == 1 - p.dp
        ys = pl.ds(half * p.dp, half)
        own, far = rows.at[0, :, :, :, lanes], rows.at[1, :, :, :, lanes]
        copy = lambda sem, src, dst, device: remote(src, dst, send.at[job, sem], recv.at[job, sem], device)
        self.give_own = copy(0, buf.at[0, ys, :, :, lanes], own, p.other_core())
        self.give_far = copy(1, buf.at[2, ys, :, :, lanes], far, p.other_core())
        self.first, self.second = [], []
        for way in range(2):
            turn = p.zl if way == 0 else 1 - p.zl
            dp = lax.rem(p.dp + turn, 2)
            device = {"feat": p.feat(zl=1 - p.zl), "dp": dp}
            src = buf.at[p.dp, pl.ds(half * (1 - p.dp) + way, 1), :, :, lanes]
            self.first.append(copy(2 + way, src, relay.at[job, way], device))
            dst = rows.at[1, pl.ds(way, 1), :, :, lanes]
            self.second.append(copy(4 + way, relay.at[job, way], dst, dict(device, layer=1 - dp)))

    def step(self, number):
        if number == 0:

            @pl.when(self.upper)
            def _():
                for copy in self.first + [self.give_own]:
                    copy.start()

            @pl.when(self.upper_gives)
            def _():
                self.give_far.start()

        elif number == 1:

            @pl.when(self.upper)
            def _():
                for way in range(2):
                    self.first[way].wait_recv()
                    self.second[way].start()

    def finish(self):
        @pl.when(self.upper)
        def _():
            for copy in self.first + self.second + [self.give_own]:
                copy.wait_send()

        @pl.when(jnp.logical_not(self.upper))
        def _():
            self.give_own.wait_recv()

        @pl.when(self.upper_gives)
        def _():
            self.give_far.wait_send()

        @pl.when(self.lower_gets)
        def _():
            self.give_far.wait_recv()

        @pl.when(self.over_z)
        def _():
            for copy in self.second:
                copy.wait_recv()


def matmul(a, b, over_a=1, over_b=0):
    return lax.dot_general(a, b, (((over_a,), (over_b,)), ((), ())), preferred_element_type=jnp.float32)


CHUNKS = JOBS // 2
SKEW = 2


def band_kernel(
    scale, acts_in, target_ref, bias_ref, enc_bias_ref, enc_in, dec_in, cross_in,
    resid_ref, acts_buf, grad_buf, feats_ref, lower_ref, far_ref, far_lower_ref, pre_ref, far_pre_ref, rows_buf,
    relay, pre_relay, rows_relay,
    enc_n, dec_n, enc_t, dec_t, cross_t, cross_ref, positive_ref, down_ref, up_ref,
    chunk, part, shard, far1, far2, near1, near2, last,
    send_a, recv_a, send_r, recv_r, send_g, recv_g, send_s, recv_s, send_p, recv_p, send_l, recv_l,
    local_a, local_g, load_sem, chunk_sem, grad_sem, core_send, core_recv,
):
    tokens = acts_in.shape[1]
    wide = tokens // CHUNKS
    lane = wide // 2
    rows = acts_in.shape[0]
    n_feat = feats_ref.shape[0]
    half = cross_ref.shape[2]
    width = 2 * half
    place = Place()
    first_core = place.core == 0

    loads = [
        pltpu.make_async_copy(enc_in, enc_n, load_sem.at[0]),
        pltpu.make_async_copy(dec_in, dec_n, load_sem.at[1]),
        pltpu.make_async_copy(cross_in, cross_ref.at[place.core], load_sem.at[2]),
    ]
    for load in loads:
        load.start()
    place.greet()

    def swap_cross():
        at = 3 * CHUNKS
        copy = remote(cross_in, cross_ref.at[place.core], core_send.at[at], core_recv.at[at], place.other_core())
        copy.start()
        return copy

    def finish_residual(total, lanes):
        resid = total + bias_ref[...] - target_ref[:, lanes].astype(jnp.float32)
        resid_ref[:, lanes] = resid
        shard[:, lanes] = (resid * scale).astype(shard.dtype)

    room = (far1, far2, near1, near2, last)
    gathers, reduces, grads, swaps, lent, far_lent, pre_swaps, lends, downs = [], [], [], [], [], [], [], [], []
    for job in range(JOBS):
        c, flip, split = job // 2, job % 2, (job // 2) % 2
        lanes = pl.ds(job * lane, lane)
        gathers.append(
            Gather(place, acts_buf, acts_in.at[:, lanes], lanes, flip, split, send_a, recv_a, local_a, job)
        )
        grads.append(Gather(place, grad_buf, shard.at[:, lanes], lanes, flip, split, send_g, recv_g, local_g, job))
        inner = pl.ds(flip * lane, lane)
        done = functools.partial(lambda whole, total, _: finish_residual(total, whole), lanes)
        reduces.append(Reduce(place, part.at[c], inner, flip, room, send_r, recv_r, job, done))
    for c in range(CHUNKS):
        lanes = pl.ds(c * wide, wide)
        ways = [pl.ds(way * (n_feat // 2), n_feat // 2) for way in (0, 1)]

        def dp_swap(here, between, there, send, recv):
            return Swap(
                place, [here.at[w, lanes] for w in ways], [between.at[c, way] for way in (0, 1)],
                [there.at[w, lanes] for w in ways], send, recv, c,
            )

        def to_core(kind, here, there):
            at = kind * CHUNKS + c
            return remote(
                here.at[:, lanes], there.at[:, lanes], core_send.at[at], core_recv.at[at], place.other_core()
            )

        swaps.append(dp_swap(feats_ref, relay, far_ref, send_s, recv_s))
        pre_swaps.append(dp_swap(pre_ref, pre_relay, far_pre_ref, send_p, recv_p))
        lent.append(to_core(0, feats_ref, lower_ref))
        far_lent.append(to_core(1, far_ref, far_lower_ref))
        downs.append(to_core(2, down_ref, up_ref))
        lends.append(Lend(place, grad_buf, rows_relay, rows_buf, lanes, send_l, recv_l, c))

    def load_chunk(c):
        return pltpu.make_async_copy(
            acts_buf.at[pl.ds(0, 2), :, :, :, pl.ds(c * wide, wide)], chunk.at[c % 2], chunk_sem.at[c]
        )

    def encode(c):
        load_chunk(c).wait()
        lanes = pl.ds(c * wide, wide)
        pre_act = matmul(enc_t[...], chunk[c % 2].reshape(width, wide)) + enc_bias_ref[...]
        positive = jnp.maximum(pre_act, 0.0)
        positive_ref[:, lanes] = positive
        feats_ref[:, lanes] = (positive * positive).astype(feats_ref.dtype)

        @pl.when(first_core)
        def _():
            lent[c].start()
            lower_ref[:, lanes] = feats_ref[:, lanes]

        swaps[c].step(0)

    def lend_far(c):
        swaps[c].step(2)
        lanes = pl.ds(c * wide, wide)

        @pl.when(first_core)
        def _():
            far_lent[c].start()
            far_lower_ref[:, lanes] = far_ref[:, lanes]

    def decode(c):
        lanes = pl.ds(c * wide, wide)
        block = SIDE * rows

        def store(i, total):
            part[c, lax.div(i, SIDE), lax.rem(i, SIDE)] = total.astype(part.dtype).reshape(SIDE, rows, wide)

        def at(i):
            return pl.ds(pl.multiple_of(i * block, 16), block)

        @pl.when(first_core)
        def _():
            @pl.loop(0, 2 * SIDE)
            def _(i):
                store(i, matmul(dec_t[at(i), :], feats_ref[:, lanes]))

        @pl.when(jnp.logical_not(first_core))
        def _():
            lent[c].wait_recv()

            @pl.loop(0, 2 * SIDE)
            def _(i):
                total = matmul(dec_t[at(i), :], feats_ref[:, lanes]) + matmul(cross_t[at(i), :], lower_ref[:, lanes])
                store(i, total)

    def load_grads(c):
        return pltpu.make_async_copy(
            grad_buf.at[pl.ds(0, 2), :, :, :, pl.ds(c * wide, wide)], chunk.at[c % 2], grad_sem.at[c]
        )

    def finish_grads(c):
        for job in (2 * c, 2 * c + 1):
            grads[job].step(Gather.steps - 1)
        load_grads(c).start()
        lends[c].step(0)

    def backward(c):
        lanes = pl.ds(c * wide, wide)
        load_grads(c).wait()
        here = chunk.at[c % 2]

        @pl.when(jnp.logical_not(first_core))
        def _():
            down = matmul(cross_ref[0], here[0].reshape(half, wide)) + matmul(cross_ref[1], here[1].reshape(half, wide))
            down_ref[:, lanes] = down.astype(down_ref.dtype)
            downs[c].start()

        grad_feats = matmul(dec_n[...], here[...].reshape(width, wide))

        @pl.when(first_core)
        def _():
            downs[c].wait_recv()
            total = grad_feats + up_ref[:, lanes].astype(jnp.float32)
            pre_ref[:, lanes] = (total * 2.0 * positive_ref[:, lanes]).astype(pre_ref.dtype)

        @pl.when(jnp.logical_not(first_core))
        def _():
            pre_ref[:, lanes] = (grad_feats * 2.0 * positive_ref[:, lanes]).astype(pre_ref.dtype)

        pre_swaps[c].step(0)

    cross_swap = []

    def turn_enc(i):
        if i == 0:
            loads[0].wait()
        block = pl.ds(i * n_feat, n_feat)
        enc_t[:, block] = enc_n[block, :].T

    def turn_dec(i):
        if i == 0:
            loads[1].wait()
        block = pl.ds(i * n_feat, n_feat)
        dec_t[block, :] = dec_n[:, block].T

    def turn_cross(i):
        if i == 0:
            loads[2].wait()
            cross_swap[0].wait_recv()
        z, at = divmod(i * 256, half)
        cross_t[pl.ds(i * 256, 256), :] = cross_ref[z, :, pl.ds(at, 256)].T

    background = [functools.partial(turn_enc, i) for i in range(width // n_feat)]
    background += [functools.partial(turn_dec, i) for i in range(width // n_feat)]
    background += [functools.partial(turn_cross, i) for i in range(width // 256)]

    def finish_gather(c):
        for job in (2 * c, 2 * c + 1):
            gathers[job].step(Gather.steps - 1)
        load_chunk(c).start()

    def line(c):
        pair = (2 * c, 2 * c + 1)
        steps = [[functools.partial(gathers[j].step, n) for j in pair] for n in range(Gather.steps - 1)]
        steps.append([functools.partial(finish_gather, c)])
        steps += [[functools.partial(encode, c)], [functools.partial(decode, c)]]
        steps += [[functools.partial(reduces[j].step, n) for j in pair] for n in range(Reduce.steps)]
        steps[-1].append(functools.partial(swaps[c].step, 1))
        steps += [[functools.partial(grads[j].step, n) for j in pair] for n in range(Gather.steps - 1)]
        steps[-2].append(functools.partial(lend_far, c))
        steps += [[functools.partial(finish_grads, c)], [functools.partial(backward, c)]]
        steps.append([functools.partial(pre_swaps[c].step, 1), functools.partial(lends[c].step, 1)])
        return steps

    lines = [line(c) for c in range(CHUNKS)]
    length = len(lines[0])
    for tick in range(length + SKEW * (CHUNKS - 1)):
        for c in reversed(range(CHUNKS)):
            at = tick - SKEW * c
            if 0 <= at < length:
                for step in lines[c][at]:
                    step()
        if tick == 0:
            cross_swap.append(swap_cross())
        elif background:
            for _ in range(6):
                if background:
                    background.pop(0)()
    for swap in pre_swaps:
        swap.step(2)
    for job in gathers + reduces + grads + swaps + pre_swaps + lends:
        job.finish()
    cross_swap[0].wait_send()

    @pl.when(first_core)
    def _():
        for copy in lent + far_lent:
            copy.wait_send()

    @pl.when(jnp.logical_not(first_core))
    def _():
        for copy in far_lent:
            copy.wait_recv()
        for copy in downs:
            copy.wait_send()


def band(acts, targets, bias, enc_bias, enc, dec_own, dec_cross, scale):
    rows, tokens = targets.shape
    width, n_feat = enc.shape
    lane = tokens // JOBS
    wide = tokens // CHUNKS
    kind = acts.dtype
    whole = pl.BlockSpec(memory_space=pltpu.VMEM)
    away = pl.BlockSpec(memory_space=pl.ANY)
    gathered = jax.ShapeDtypeStruct((3, SIDE, SIDE, rows, tokens), kind)
    feats = jax.ShapeDtypeStruct((n_feat, tokens), kind)
    dma = pltpu.SemaphoreType.DMA
    return pl.pallas_call(
        functools.partial(band_kernel, scale),
        out_shape=(
            jax.ShapeDtypeStruct((rows, tokens), jnp.float32),
            gathered,
            gathered,
            feats, feats, feats, feats, feats, feats,
            jax.ShapeDtypeStruct((2, SIDE // 2, SIDE, rows, tokens), kind),
            jax.ShapeDtypeStruct((CHUNKS, 2, n_feat // 2, wide), kind),
            jax.ShapeDtypeStruct((CHUNKS, 2, n_feat // 2, wide), kind),
            jax.ShapeDtypeStruct((CHUNKS, 2, 1, SIDE, rows, wide), kind),
        ),
        in_specs=[whole] * 4 + [away] * 3,
        out_specs=(whole, away, away) + (whole,) * 6 + (away,) * 4,
        scratch_shapes=[
            pltpu.VMEM((width, n_feat), kind),
            pltpu.VMEM((n_feat, width), kind),
            pltpu.VMEM((n_feat, width), kind),
            pltpu.VMEM((width, n_feat), kind),
            pltpu.VMEM((width, n_feat), kind),
            pltpu.VMEM((2,) + dec_cross.shape, kind),
            pltpu.VMEM((n_feat, tokens), jnp.float32),
            pltpu.VMEM((n_feat, tokens), kind),
            pltpu.VMEM((n_feat, tokens), kind),
            pltpu.VMEM((2, 2, SIDE, SIDE, rows, wide), kind),
            pltpu.VMEM((CHUNKS, 2, SIDE, SIDE, rows, wide), kind),
            pltpu.VMEM((rows, tokens), kind),
            pltpu.VMEM((JOBS, 2, SIDE, rows, lane), kind),
            pltpu.VMEM((JOBS, 2, 2, SIDE, rows, lane), kind),
            pltpu.VMEM((JOBS, 2, rows, lane), kind),
            pltpu.VMEM((JOBS, 2, 2, rows, lane), kind),
            pltpu.VMEM((JOBS, rows, lane), kind),
            dma((JOBS, Gather.sems)),
            dma((JOBS, Gather.sems)),
            dma((JOBS, Reduce.sems)),
            dma((JOBS, Reduce.sems)),
            dma((JOBS, Gather.sems)),
            dma((JOBS, Gather.sems)),
            dma((CHUNKS, Swap.sems)),
            dma((CHUNKS, Swap.sems)),
            dma((CHUNKS, Swap.sems)),
            dma((CHUNKS, Swap.sems)),
            dma((CHUNKS, Lend.sems)),
            dma((CHUNKS, Lend.sems)),
            dma((JOBS,)),
            dma((JOBS,)),
            dma((3,)),
            dma((CHUNKS,)),
            dma((CHUNKS,)),
            dma((3 * CHUNKS + 1,)),
            dma((3 * CHUNKS + 1,)),
        ],
        compiler_params=pltpu.CompilerParams(
            collective_id=1, has_side_effects=True, vmem_limit_bytes=60 * 1024 * 1024
        ),
        name="band",
    )(acts, targets, bias, enc_bias, enc, dec_own, dec_cross)


def weights_kernel(
    acts_in, grads_in, rows_in, feats_in, far_in, first_in, far_first_in, pre_in, far_pre_in,
    enc_out, own_out, cross_out,
    acts, grads, rows, feats, first, pre, enc_g, own_g, cross_g, load_sem, store_sem,
):
    dp = lax.axis_index("dp")
    half = SIDE // 2
    n_feat, width = own_g.shape
    block = width // 2
    started = []

    def load(src, dst):
        copy = pltpu.make_async_copy(src, dst, load_sem.at[len(started)])
        copy.start()
        started.append(copy)
        return copy

    ys = [pl.ds(half * part, half) for part in (0, 1)]
    first_loads = [load(feats_in, feats.at[0]), load(far_in, feats.at[1])]
    grad_loads = [[load(grads_in.at[slot, y], grads.at[i, y]) for i, slot in ((0, dp), (1, 2))] for y in ys]
    pre_loads = [load(pre_in, pre.at[0]), load(far_pre_in, pre.at[1])]
    act_loads = [[load(acts_in.at[slot, y], acts.at[i, y]) for i, slot in ((0, dp), (1, 2))] for y in ys]
    cross_loads = [load(first_in, first.at[0]), load(far_first_in, first.at[1])]
    upper = lax.axis_index("layer") == 1
    mine = pl.ds(half * dp, half)

    def load_rows(i, here, slot):
        at = len(started)

        @pl.when(here)
        def _():
            pltpu.make_async_copy(grads_in.at[slot, mine], rows.at[i], load_sem.at[at]).start()

        @pl.when(jnp.logical_not(here))
        def _():
            pltpu.make_async_copy(rows_in.at[i], rows.at[i], load_sem.at[at]).start()

        started.append(pltpu.make_async_copy(rows_in.at[i], rows.at[i], load_sem.at[at]))
        return started[-1]

    cross_loads += [load_rows(0, upper, 1), load_rows(1, jnp.logical_and(upper, dp == 1), 2)]
    stores = []

    def store(src, dst):
        copy = pltpu.make_async_copy(src, dst, store_sem.at[len(stores)])
        copy.start()
        stores.append(copy)

    def both(a, b):
        return matmul(a[0], b[0], 1, 1) + matmul(a[1], b[1], 1, 1)

    step = n_feat // 2

    def by_feats(left, right, out, columns):
        @pl.loop(0, 2)
        def _(m):
            at = pl.ds(pl.multiple_of(m * step, step), step)
            out[at, columns] = both((left[0, at, :], left[1, at, :]), right())

    for copy in first_loads:
        copy.wait()
    for part in (0, 1):
        for copy in grad_loads[part]:
            copy.wait()
        columns = pl.ds(part * block, block)
        by_feats(feats, lambda: [grads[i, ys[part]].reshape(block, -1) for i in (0, 1)], own_g, columns)
        store(own_g.at[:, columns], own_out.at[:, columns])
    for copy in pre_loads:
        copy.wait()
    for part in (0, 1):
        for copy in act_loads[part]:
            copy.wait()
        for y in range(half * part, half * part + half):
            at = pl.ds(y * (width // SIDE), width // SIDE)
            enc_g[at, :] = both([acts[i, y].reshape(width // SIDE, -1) for i in (0, 1)], [pre[0], pre[1]])
            store(enc_g.at[at, :], enc_out.at[at, :])
    for copy in cross_loads:
        copy.wait()
    by_feats(first, lambda: [rows[i].reshape(block, -1) for i in (0, 1)], cross_g, pl.ds(0, block))
    store(cross_g, cross_out)
    for copy in stores:
        copy.wait()


def weights(acts, grads, lent, feats, far, first, far_first, pre, far_pre):
    rows, tokens = acts.shape[3:]
    n_feat = feats.shape[0]
    half = SIDE * SIDE * rows
    kind = acts.dtype
    f32 = jnp.float32
    away = pl.BlockSpec(memory_space=pl.ANY)
    shapes = [(half, n_feat), (n_feat, half), (n_feat, half // 2)]
    return pl.pallas_call(
        weights_kernel,
        out_shape=[jax.ShapeDtypeStruct(s, f32) for s in shapes],
        in_specs=[away] * 9,
        out_specs=[away] * 3,
        scratch_shapes=[
            pltpu.VMEM((2, SIDE, SIDE, rows, tokens), kind),
            pltpu.VMEM((2, SIDE, SIDE, rows, tokens), kind),
            pltpu.VMEM(lent.shape, kind),
            pltpu.VMEM((2, n_feat, tokens), kind),
            pltpu.VMEM((2, n_feat, tokens), kind),
            pltpu.VMEM((2, n_feat, tokens), kind),
        ]
        + [pltpu.VMEM(s, f32) for s in shapes]
        + [pltpu.SemaphoreType.DMA((16,)), pltpu.SemaphoreType.DMA((8,))],
        compiler_params=pltpu.CompilerParams(vmem_limit_bytes=60 * 1024 * 1024),
        name="weights",
    )(acts, grads, lent, feats, far, first, far_first, pre, far_pre)


def local(acts, targets, enc, enc_bias, dec_own, dec_cross, dec_bias):
    tokens, rows = acts.shape[1:]
    scale = float(tokens * lax.axis_size("dp")) ** (-0.5)
    bias = dec_bias.astype(jnp.float32).reshape(rows, 1)
    residual, gathered, grads, feats, first, far, far_first, pre, far_pre, lent = band(
        acts[0].T, targets[0].T, bias, enc_bias.reshape(-1, 1), enc[0], dec_own[0], dec_cross, scale
    )[:10]
    grad_enc, grad_own, grad_cross = weights(gathered, grads, lent, feats, far, first, far_first, pre, far_pre)
    return (residual.T[None], grad_enc[None], grad_own[None], grad_cross)


def solution(mesh):
    in_specs = (
        P("layer", "dp", "feat"),
        P("layer", "dp", "feat"),
        P("layer", None, "feat"),
        P("layer", "feat"),
        P("layer", "feat", None),
        P("feat", "layer"),
        P("layer", "feat"),
    )
    out_specs = (
        P("layer", "dp", "feat"),
        P("layer", "dp", "feat"),
        P("layer", "feat", "dp"),
        P("feat", ("layer", "dp")),
    )
    return jax.shard_map(local, mesh=mesh, in_specs=in_specs, out_specs=out_specs, check_vma=False)
```

```python
import functools

import jax
import jax.numpy as jnp
from jax import lax
from jax.experimental import pallas as pl
from jax.experimental.pallas import tpu as pltpu
from jax.sharding import PartitionSpec as P

MESH = pl.DeviceIdType.MESH
ALL = slice(None)
SIDE = 4
JOBS = 8


class Place:
    def __init__(self):
        feat = lax.axis_index("feat")
        self.core = lax.axis_index("layer")
        self.dp = lax.axis_index("dp")
        self.x = lax.rem(feat, SIDE)
        self.y = lax.rem(lax.div(feat, SIDE), SIDE)
        self.zl = lax.div(feat, SIDE * SIDE)

    def feat(self, zl=None, y=None, x=None):
        zl = self.zl if zl is None else zl
        y = self.y if y is None else y
        x = self.x if x is None else x
        return (zl * SIDE + y) * SIDE + x

    def at(self, axis):
        return self.x if axis == "x" else self.y

    def along(self, axis, step):
        return lax.rem(self.at(axis) + (step + SIDE), SIDE)

    def neighbour(self, axis, step):
        return {"feat": self.feat(**{axis: self.along(axis, step)})}

    def pair(self):
        return {"feat": self.feat(zl=1 - self.zl)}

    def across(self, zl):
        return {"feat": self.feat(zl=zl), "dp": 1 - self.dp}

    def other_core(self):
        return {"layer": 1 - self.core}

    def greet(self):
        peers = [self.neighbour(a, s) for a in "xy" for s in (1, -1)]
        peers += [self.pair(), self.across(0), self.across(1)]
        peers.append(self.other_core())
        peers += [dict(self.pair(), **self.other_core()), dict(self.across(1 - self.zl), **self.other_core())]
        barrier = pltpu.get_barrier_semaphore()
        for peer in peers:
            pl.semaphore_signal(barrier, inc=1, device_id=peer, device_id_type=MESH)
        pl.semaphore_wait(barrier, len(peers))


def remote(src, dst, send, recv, device):
    return pltpu.make_async_remote_copy(
        src_ref=src, dst_ref=dst, send_sem=send, recv_sem=recv, device_id=device, device_id_type=MESH
    )


class Gather:
    sems = 11
    steps = 6

    whole, right, left = (slice(0, 2), ALL), (slice(0, 1), ALL), (slice(1, 2), ALL)

    def __init__(self, place, buf, own, lanes, flip, send, recv, local, job):
        self.place, self.buf, self.own, self.lanes = place, buf, own, lanes
        self.first, self.second = ("y", "x") if flip else ("x", "y")
        self.send, self.recv, self.local, self.job = send, recv, local, job
        self.sent = []

    def first_block(self, part, at):
        p = self.place
        slots, rows = part
        index = (slots, p.y, at, rows, self.lanes) if self.first == "x" else (slots, at, p.x, rows, self.lanes)
        return self.buf.at[index]

    def second_block(self, part, at):
        slots, rows = part
        index = (slots, at, ALL, rows, self.lanes) if self.second == "y" else (slots, ALL, at, rows, self.lanes)
        return self.buf.at[index]

    def copy(self, sem, src, dst, device, recv=None):
        return remote(src, dst, self.send.at[self.job, sem], self.recv.at[self.job, sem if recv is None else recv], device)

    def out(self, sem, block, device):
        copy = self.copy(sem, block, block, device)
        copy.start()
        self.sent.append(copy)
        return copy

    def ring(self, sem, axis, block):
        p = self.place
        own = block(self.whole, p.at(axis))
        return (self.out(sem, own, p.neighbour(axis, 1)), self.out(sem + 1, own, p.neighbour(axis, -1)))

    def forward(self, sem, axis, block):
        p = self.place
        return (
            self.out(sem, block(self.right, p.along(axis, -1)), p.neighbour(axis, 1)),
            self.out(sem + 1, block(self.left, p.along(axis, 1)), p.neighbour(axis, -1)),
        )

    def begin(self):
        p = self.place
        here = self.buf.at[p.zl, p.y, p.x, :, self.lanes]
        self.kept = pltpu.make_async_copy(self.own, here, self.local.at[self.job])
        self.kept.start()
        self.waits = [self.copy(0, self.own, here, p.pair())]
        self.waits[0].start()
        self.sent += self.waits

    def settle(self):
        self.kept.wait()

    def step(self, number):
        if number == 0:
            self.begin()
            return
        for copy in self.waits:
            copy.wait_recv()
        if number == 1:
            self.settle()
            self.waits = self.ring(3, self.first, self.first_block)
        elif number == 2:
            self.waits = self.forward(5, self.first, self.first_block)
        elif number == 3:
            self.waits = self.ring(7, self.second, self.second_block)
        elif number == 4:
            self.waits = self.forward(9, self.second, self.second_block)

    def finish(self):
        for copy in self.sent:
            copy.wait_send()


class Extra(Gather):
    def __init__(self, *args):
        super().__init__(*args)
        rows = self.own.shape[0]
        cut = (rows // 32 + rows % 32 // 16) * 16
        slot = slice(2, 3)
        self.whole, self.right, self.left = (slot, ALL), (slot, pl.ds(0, cut)), (slot, pl.ds(cut, rows - cut))

    def begin(self):
        p = self.place
        there = self.buf.at[2, p.y, p.x, :, self.lanes]
        self.cross = [self.copy(1 + zl, self.own, there, p.across(zl), recv=1) for zl in (0, 1)]

        @pl.when(p.zl != p.dp)
        def _():
            for copy in self.cross:
                copy.start()

        self.waits = [self.cross[0]]

    def settle(self):
        pass

    def finish(self):
        super().finish()

        @pl.when(self.place.zl != self.place.dp)
        def _():
            for copy in self.cross:
                copy.wait_send()


class Reduce:
    sems = 13
    steps = 6

    def __init__(self, place, part, lanes, flip, room, send, recv, job, finish):
        self.place, self.part, self.lanes = place, part, lanes
        self.first, self.second = ("x", "y") if flip else ("y", "x")
        self.far1, self.far2, self.near1, self.near2, self.last = room
        self.send, self.recv, self.job, self.done = send, recv, job, finish
        self.sent = []

    def first_block(self, z, at):
        return (z, at, ALL, ALL, self.lanes) if self.first == "y" else (z, ALL, at, ALL, self.lanes)

    def second_block(self, z, at):
        p = self.place
        return (z, p.y, at, ALL, self.lanes) if self.first == "y" else (z, at, p.x, ALL, self.lanes)

    def out(self, sem, src, dst, device):
        copy = remote(src, dst, self.send.at[self.job, sem], self.recv.at[self.job, sem], device)
        copy.start()
        self.sent.append(copy)
        return copy

    def add(self, index, *refs):
        total = self.part[index].astype(jnp.float32)
        for ref in refs:
            total = total + ref[...].astype(jnp.float32)
        self.part[index] = total.astype(self.part.dtype)

    def begin(self, sem, axis, block, one, two):
        p = self.place
        right, left = p.neighbour(axis, 1), p.neighbour(axis, -1)
        far, up, down = p.along(axis, 2), p.along(axis, 1), p.along(axis, -1)
        j = self.job
        self.relay = (
            self.out(sem, self.part.at[block(0, far)], one.at[j, 0], right),
            self.out(sem + 1, self.part.at[block(1, far)], one.at[j, 1], left),
        )
        self.early = (
            self.out(sem + 2, self.part.at[block(1, up)], two.at[j, 0, 1], right),
            self.out(sem + 3, self.part.at[block(0, down)], two.at[j, 1, 0], left),
        )

    def pass_on(self, sem, axis, block, one, two):
        p = self.place
        right, left = p.neighbour(axis, 1), p.neighbour(axis, -1)
        up, down = p.along(axis, 1), p.along(axis, -1)
        j = self.job
        self.relay[0].wait_recv()
        self.add(block(0, up), one.at[j, 0])
        late = self.out(sem, self.part.at[block(0, up)], two.at[j, 0, 0], right)
        self.relay[1].wait_recv()
        self.add(block(1, down), one.at[j, 1])
        self.late = (late, self.out(sem + 1, self.part.at[block(1, down)], two.at[j, 1, 1], left))

    def collect(self, axis, block, two):
        for copy in self.early + self.late:
            copy.wait_recv()
        self.add(block(slice(0, 2), self.place.at(axis)), two.at[self.job, 0], two.at[self.job, 1])

    def step(self, number):
        p = self.place
        if number == 0:
            self.begin(0, self.first, self.first_block, self.far1, self.far2)
        elif number == 1:
            self.pass_on(4, self.first, self.first_block, self.far1, self.far2)
        elif number == 2:
            self.collect(self.first, self.first_block, self.far2)
            self.begin(6, self.second, self.second_block, self.near1, self.near2)
        elif number == 3:
            self.pass_on(10, self.second, self.second_block, self.near1, self.near2)
        elif number == 4:
            self.collect(self.second, self.second_block, self.near2)
            gone = self.part.at[1 - p.zl, p.y, p.x, :, self.lanes]
            self.pair = self.out(12, gone, self.last.at[self.job], p.pair())
        else:
            self.pair.wait_recv()
            mine = self.part[p.zl, p.y, p.x, :, self.lanes].astype(jnp.float32)
            self.done(mine + self.last[self.job].astype(jnp.float32), self.lanes)

    def finish(self):
        for copy in self.sent:
            copy.wait_send()


class Swap:
    sems = 4

    def __init__(self, place, src, relay, dst, send, recv, job):
        self.place, self.src, self.relay, self.dst = place, src, relay, dst
        self.send, self.recv, self.job = send, recv, job
        self.sent = []

    def device(self, sem):
        p = self.place
        turn = p.zl if sem % 2 == 0 else 1 - p.zl
        return {"feat": p.feat(zl=1 - p.zl), "dp": lax.rem(p.dp + turn, 2)}

    def out(self, sem, src, dst):
        copy = remote(src, dst, self.send.at[self.job, sem], self.recv.at[self.job, sem], self.device(sem))
        copy.start()
        self.sent.append(copy)

    def step(self, number):
        if number == 0:
            for way in (0, 1):
                self.out(way, self.src[way], self.relay[way])
        elif number == 1:
            for way in (0, 1):
                self.sent[way].wait_recv()
                self.out(2 + way, self.relay[way], self.dst[way])
        else:
            for way in (0, 1):
                self.sent[2 + way].wait_recv()

    def finish(self):
        for copy in self.sent:
            copy.wait_send()


class Lend:
    sems = 8

    def __init__(self, place, buf, relay, rows, lanes, send, recv, job):
        p = self.place = place
        self.lanes = lanes
        half = SIDE // 2
        self.upper = p.core == 1
        self.upper_gives = jnp.logical_and(self.upper, p.dp == 0)
        self.lower_gets = jnp.logical_and(p.core == 0, p.dp == 0)
        self.over_z = p.core == 1 - p.dp
        ys = pl.ds(half * p.dp, half)
        own, far = rows.at[0, :, :, :, lanes], rows.at[1, :, :, :, lanes]
        copy = lambda sem, src, dst, device: remote(src, dst, send.at[job, sem], recv.at[job, sem], device)
        self.give_own = copy(0, buf.at[0, ys, :, :, lanes], own, p.other_core())
        self.give_far = copy(1, buf.at[2, ys, :, :, lanes], far, p.other_core())
        self.first, self.second = [], []
        for way in range(2):
            turn = p.zl if way == 0 else 1 - p.zl
            dp = lax.rem(p.dp + turn, 2)
            device = {"feat": p.feat(zl=1 - p.zl), "dp": dp}
            src = buf.at[p.dp, pl.ds(half * (1 - p.dp) + way, 1), :, :, lanes]
            self.first.append(copy(2 + way, src, relay.at[job, way], device))
            dst = rows.at[1, pl.ds(way, 1), :, :, lanes]
            self.second.append(copy(4 + way, relay.at[job, way], dst, dict(device, layer=1 - dp)))

    def step(self, number):
        if number == 0:

            @pl.when(self.upper)
            def _():
                for copy in self.first + [self.give_own]:
                    copy.start()

        elif number == 1:

            @pl.when(self.upper)
            def _():
                for way in range(2):
                    self.first[way].wait_recv()
                    self.second[way].start()

        else:

            @pl.when(self.upper_gives)
            def _():
                self.give_far.start()

    def finish(self):
        @pl.when(self.upper)
        def _():
            for copy in self.first + self.second + [self.give_own]:
                copy.wait_send()

        @pl.when(jnp.logical_not(self.upper))
        def _():
            self.give_own.wait_recv()

        @pl.when(self.upper_gives)
        def _():
            self.give_far.wait_send()

        @pl.when(self.lower_gets)
        def _():
            self.give_far.wait_recv()

        @pl.when(self.over_z)
        def _():
            for copy in self.second:
                copy.wait_recv()


def matmul(a, b, over_a=1, over_b=0):
    return lax.dot_general(a, b, (((over_a,), (over_b,)), ((), ())), preferred_element_type=jnp.float32)


CHUNKS = JOBS // 2

ORDER = (
    ("A", 6, 0), ("A", 7, 0), ("A", 4, 0), ("A", 5, 0), ("A", 2, 0), ("A", 3, 0), ("A", 0, 0), ("A", 1, 0),
    ("a", 0, 0), ("A", 6, 1), ("A", 7, 1), ("A", 4, 1), ("A", 5, 1), ("a", 1, 0), ("T", 0), ("A", 2, 1),
    ("A", 3, 1), ("a", 2, 0), ("T", 1), ("A", 0, 1), ("A", 1, 1), ("T", 2), ("a", 3, 0), ("T", 3), ("A", 6, 2),
    ("A", 7, 2), ("T", 4), ("T", 5), ("A", 4, 2), ("A", 5, 2), ("T", 6), ("T", 7), ("a", 0, 1), ("A", 2, 2),
    ("A", 3, 2), ("T", 8), ("a", 1, 1), ("T", 9), ("A", 0, 2), ("A", 1, 2), ("T", 10), ("A", 6, 3), ("A", 7, 3),
    ("T", 11), ("A", 4, 3), ("A", 5, 3), ("T", 12), ("A", 3, 3), ("T", 13), ("T", 14), ("T", 15), ("A", 2, 3),
    ("T", 16), ("A", 0, 3), ("A", 1, 3), ("T", 17), ("T", 18), ("T", 19), ("T", 20), ("T", 21), ("T", 22),
    ("T", 23), ("T", 24), ("T", 25), ("T", 26), ("T", 27), ("A", 7, 4), ("A", 6, 4), ("A", 5, 4), ("A", 4, 4),
    ("A", 3, 4), ("A", 2, 4), ("A", 1, 4), ("A", 0, 4), ("A", 7, 5), ("A", 6, 5), ("L", 3), ("F", 3), ("A", 5, 5),
    ("A", 4, 5), ("L", 2), ("a", 2, 1), ("a", 3, 1), ("A", 3, 5), ("A", 2, 5), ("L", 1), ("F", 2), ("D", 3, 0),
    ("D", 3, 1), ("R", 6, 0), ("R", 7, 0), ("S", 3, 1), ("D", 2, 0), ("D", 2, 1), ("R", 4, 0), ("R", 5, 0),
    ("R", 6, 1), ("R", 7, 1), ("S", 3, 2), ("S", 2, 1), ("F", 1), ("A", 1, 5), ("A", 0, 5), ("L", 0), ("R", 4, 1),
    ("R", 5, 1), ("S", 2, 2), ("D", 1, 0), ("D", 1, 1), ("R", 2, 0), ("R", 3, 0), ("S", 1, 1), ("R", 6, 2),
    ("R", 7, 2), ("F", 0), ("R", 4, 2), ("R", 5, 2), ("S", 1, 2), ("R", 2, 1), ("R", 3, 1), ("D", 0, 0),
    ("R", 7, 3), ("R", 6, 3), ("R", 5, 3), ("R", 4, 3), ("D", 0, 1), ("R", 0, 0), ("R", 1, 0), ("S", 0, 1),
    ("R", 2, 2), ("R", 7, 4), ("R", 6, 4), ("R", 5, 4), ("R", 4, 4), ("R", 3, 2), ("R", 0, 1), ("R", 1, 1),
    ("R", 7, 5), ("G", 7, 0), ("R", 6, 5), ("G", 6, 0), ("R", 5, 5), ("G", 5, 0), ("R", 4, 5), ("G", 4, 0),
    ("S", 0, 2), ("g", 2, 0), ("R", 3, 3), ("g", 3, 0), ("R", 2, 3), ("a", 1, 2), ("G", 7, 1), ("a", 0, 2),
    ("G", 6, 1), ("G", 5, 1), ("G", 4, 1), ("R", 0, 2), ("R", 3, 4), ("R", 2, 4), ("R", 1, 2), ("a", 2, 2),
    ("G", 7, 2), ("a", 3, 2), ("G", 6, 2), ("a", 0, 3), ("R", 3, 5), ("G", 3, 0), ("R", 2, 5), ("G", 5, 2),
    ("G", 2, 0), ("G", 4, 2), ("g", 1, 0), ("a", 1, 3), ("R", 1, 3), ("R", 0, 3), ("G", 7, 3), ("G", 3, 1),
    ("G", 2, 1), ("G", 6, 3), ("G", 4, 3), ("G", 5, 3), ("R", 1, 4), ("R", 0, 4), ("G", 3, 2), ("R", 1, 5),
    ("G", 1, 0), ("R", 0, 5), ("G", 0, 0), ("g", 0, 0), ("G", 1, 1), ("G", 0, 1), ("G", 7, 4), ("G", 6, 4),
    ("G", 2, 2), ("G", 4, 4), ("G", 5, 4), ("G", 3, 3), ("G", 0, 2), ("G", 1, 2), ("G", 7, 5), ("G", 6, 5),
    ("M", 3), ("g", 3, 1), ("G", 2, 3), ("B", 3, 0), ("G", 4, 5), ("G", 5, 5), ("M", 2), ("G", 1, 3), ("W", 3),
    ("B", 2, 0), ("B", 3, 1), ("W", 2), ("G", 3, 4), ("a", 2, 3), ("B", 2, 1), ("G", 2, 4), ("G", 0, 3),
    ("P", 3, 1), ("g", 2, 1), ("G", 1, 4), ("G", 3, 5), ("a", 3, 3), ("G", 2, 5), ("M", 1), ("P", 2, 1),
    ("B", 1, 0), ("G", 1, 5), ("g", 1, 1), ("a", 0, 4), ("P", 3, 2), ("a", 1, 4), ("G", 0, 4), ("B", 1, 1),
    ("W", 1), ("g", 0, 1), ("g", 3, 2), ("g", 2, 2), ("P", 2, 2), ("a", 0, 5), ("a", 2, 4), ("a", 3, 4),
    ("a", 1, 5), ("G", 0, 5), ("M", 0), ("P", 1, 1), ("g", 1, 2), ("g", 0, 2), ("g", 2, 3), ("g", 3, 3),
    ("B", 0, 0), ("a", 2, 5), ("a", 3, 5), ("W", 0), ("B", 0, 1), ("g", 1, 3), ("g", 0, 3), ("P", 1, 2),
    ("g", 2, 4), ("g", 3, 4), ("P", 0, 1), ("g", 0, 4), ("g", 1, 4), ("g", 2, 5), ("g", 3, 5), ("P", 0, 2),
    ("g", 0, 5), ("g", 1, 5),
)


def band_kernel(
    scale, acts_in, target_ref, bias_ref, enc_bias_ref, enc_in, dec_in, cross_in,
    resid_ref, acts_buf, grad_buf, feats_ref, lower_ref, far_ref, far_lower_ref, pre_ref, far_pre_ref, rows_buf,
    relay, pre_relay, rows_relay, acts_relay,
    enc_n, dec_n, enc_t, dec_t, cross_t, cross_ref, enc_bias_t, positive_ref, down_ref, up_ref,
    chunk, part, shard, far1, far2, near1, near2, last,
    send_a, recv_a, send_r, recv_r, send_g, recv_g, send_s, recv_s, send_p, recv_p, send_l, recv_l,
    send_xa, recv_xa, send_xg, recv_xg, send_z, recv_z,
    local_a, local_g, load_sem, chunk_sem, grad_sem, core_send, core_recv,
):
    tokens = acts_in.shape[1]
    wide = tokens // CHUNKS
    lane = wide // 2
    rows = acts_in.shape[0]
    n_feat = feats_ref.shape[0]
    half = cross_ref.shape[2]
    width = 2 * half
    place = Place()
    first_core = place.core == 0

    loads = [
        pltpu.make_async_copy(enc_in, enc_n, load_sem.at[0]),
        pltpu.make_async_copy(dec_in, dec_n, load_sem.at[1]),
        pltpu.make_async_copy(cross_in, cross_ref.at[place.core], load_sem.at[2]),
    ]
    for load in loads:
        load.start()
    place.greet()

    def swap_cross():
        at = 3 * CHUNKS
        copy = remote(cross_in, cross_ref.at[place.core], core_send.at[at], core_recv.at[at], place.other_core())
        copy.start()
        return copy

    def finish_residual(total, lanes):
        resid = total + bias_ref[...] - target_ref[:, lanes].astype(jnp.float32)
        resid_ref[:, lanes] = resid
        shard[:, lanes] = (resid * scale).astype(shard.dtype)

    room = (far1, far2, near1, near2, last)
    gathers, reduces, grads, swaps, lent, far_lent, pre_swaps, lends, downs = [], [], [], [], [], [], [], [], []
    act_extras, grad_extras, act_swaps = [], [], []
    for job in range(JOBS):
        c, flip = job // 2, job % 2
        lanes = pl.ds(job * lane, lane)
        gathers.append(
            Gather(place, acts_buf, acts_in.at[:, lanes], lanes, flip, send_a, recv_a, local_a, job)
        )
        grads.append(Gather(place, grad_buf, shard.at[:, lanes], lanes, flip, send_g, recv_g, local_g, job))
        inner = pl.ds(flip * lane, lane)
        done = functools.partial(lambda whole, total, _: finish_residual(total, whole), lanes)
        reduces.append(Reduce(place, part.at[c], inner, flip, room, send_r, recv_r, job, done))
    for c in range(CHUNKS):
        lanes = pl.ds(c * wide, wide)
        ways = [pl.ds(way * (n_feat // 2), n_feat // 2) for way in (0, 1)]

        def dp_swap(here, between, there, send, recv):
            return Swap(
                place, [here.at[w, lanes] for w in ways], [between.at[c, way] for way in (0, 1)],
                [there.at[w, lanes] for w in ways], send, recv, c,
            )

        def to_core(kind, here, there):
            at = kind * CHUNKS + c
            return remote(
                here.at[:, lanes], there.at[:, lanes], core_send.at[at], core_recv.at[at], place.other_core()
            )

        swaps.append(dp_swap(feats_ref, relay, far_ref, send_s, recv_s))
        pre_swaps.append(dp_swap(pre_ref, pre_relay, far_pre_ref, send_p, recv_p))
        lent.append(to_core(0, feats_ref, lower_ref))
        far_lent.append(to_core(1, far_ref, far_lower_ref))
        downs.append(to_core(2, down_ref, up_ref))
        act_extras.append(
            Extra(place, acts_buf, acts_in.at[:, lanes], lanes, c % 2, send_xa, recv_xa, None, c)
        )
        grad_extras.append(Extra(place, grad_buf, shard.at[:, lanes], lanes, c % 2, send_xg, recv_xg, None, c))
        y_halves = [pl.ds(way * (SIDE // 2), SIDE // 2) for way in (0, 1)]
        act_swaps.append(
            Swap(
                place, [acts_buf.at[1 - place.dp, ys, :, :, lanes] for ys in y_halves],
                [acts_relay.at[c, way] for way in (0, 1)], [acts_buf.at[2, ys, :, :, lanes] for ys in y_halves],
                send_z, recv_z, c,
            )
        )
        lends.append(Lend(place, grad_buf, rows_relay, rows_buf, lanes, send_l, recv_l, c))

    def load_chunk(c):
        return pltpu.make_async_copy(
            acts_buf.at[pl.ds(0, 2), :, :, :, pl.ds(c * wide, wide)], chunk.at[c % 2], chunk_sem.at[c]
        )

    def encode(c):
        load_chunk(c).wait()
        lanes = pl.ds(c * wide, wide)
        pre_act = matmul(enc_t[...], chunk[c % 2].reshape(width, wide)) + enc_bias_t[:, 0:1]
        positive = jnp.maximum(pre_act, 0.0)
        positive_ref[:, lanes] = positive
        feats_ref[:, lanes] = (positive * positive).astype(feats_ref.dtype)

        @pl.when(first_core)
        def _():
            lent[c].start()
            lower_ref[:, lanes] = feats_ref[:, lanes]

        swaps[c].step(0)

    def lend_far(c):
        swaps[c].step(2)
        lanes = pl.ds(c * wide, wide)

        @pl.when(first_core)
        def _():
            far_lent[c].start()
            far_lower_ref[:, lanes] = far_ref[:, lanes]

    def decode(c, side):
        lanes = pl.ds(c * wide, wide)
        block = SIDE * rows

        def store(i, total):
            part[c, lax.div(i, SIDE), lax.rem(i, SIDE)] = total.astype(part.dtype).reshape(SIDE, rows, wide)

        def at(i):
            return pl.ds(pl.multiple_of(i * block, 16), block)

        @pl.when(first_core)
        def _():
            @pl.loop(side * SIDE, side * SIDE + SIDE)
            def _(i):
                store(i, matmul(dec_t[at(i), :], feats_ref[:, lanes]))

        @pl.when(jnp.logical_not(first_core))
        def _():
            if side == 0:
                lent[c].wait_recv()

            @pl.loop(side * SIDE, side * SIDE + SIDE)
            def _(i):
                total = matmul(dec_t[at(i), :], feats_ref[:, lanes]) + matmul(cross_t[at(i), :], lower_ref[:, lanes])
                store(i, total)

    def load_grads(c):
        return pltpu.make_async_copy(
            grad_buf.at[pl.ds(0, 2), :, :, :, pl.ds(c * wide, wide)], chunk.at[c % 2], grad_sem.at[c]
        )

    def finish_grads(c):
        load_grads(c).start()
        lends[c].step(0)

    def extra_grads(c, number):
        grad_extras[c].step(number)
        if number == Gather.steps - 1:
            lends[c].step(2)

    def backward(c, part):
        lanes = pl.ds(c * wide, wide)
        here = chunk.at[c % 2]
        if part == 0:
            load_grads(c).wait()
            send_down(c, lanes, here)
        else:
            make_pre(c, lanes, here)

    def send_down(c, lanes, here):
        @pl.when(jnp.logical_not(first_core))
        def _():
            down = matmul(cross_ref[0], here[0].reshape(half, wide)) + matmul(cross_ref[1], here[1].reshape(half, wide))
            down_ref[:, lanes] = down.astype(down_ref.dtype)
            downs[c].start()

    def make_pre(c, lanes, here):
        grad_feats = matmul(dec_n[...], here[...].reshape(width, wide))

        @pl.when(first_core)
        def _():
            downs[c].wait_recv()
            total = grad_feats + up_ref[:, lanes].astype(jnp.float32)
            pre_ref[:, lanes] = (total * 2.0 * positive_ref[:, lanes]).astype(pre_ref.dtype)

        @pl.when(jnp.logical_not(first_core))
        def _():
            pre_ref[:, lanes] = (grad_feats * 2.0 * positive_ref[:, lanes]).astype(pre_ref.dtype)

        pre_swaps[c].step(0)

    cross_swap = []

    def turn_enc(i):
        if i == 0:
            enc_bias_t[...] = jnp.broadcast_to(enc_bias_ref[...], (128, n_feat)).T
            loads[0].wait()
        block = pl.ds(i * n_feat, n_feat)
        enc_t[:, block] = enc_n[block, :].T

    def turn_dec(i):
        if i == 0:
            loads[1].wait()
        block = pl.ds(i * n_feat, n_feat)
        dec_t[block, :] = dec_n[:, block].T

    def turn_cross(i):
        if i == 0:
            loads[2].wait()
            cross_swap[0].wait_recv()
        z, at = divmod(i * 256, half)
        cross_t[pl.ds(i * 256, 256), :] = cross_ref[z, :, pl.ds(at, 256)].T

    background = [functools.partial(turn_enc, i) for i in range(width // n_feat)]
    background += [functools.partial(turn_dec, i) for i in range(width // n_feat)]
    background += [functools.partial(turn_cross, i) for i in range(width // 256)]

    cross_swap.append(swap_cross())
    act_jobs = {
        "A": lambda i, n: gathers[i].step(n),
        "a": lambda i, n: act_extras[i].step(n),
        "Z": lambda i, n: act_swaps[i].step(n),
        "T": lambda i: background[i](),
        "L": lambda i: load_chunk(i).start(),
        "F": encode,
        "D": decode,
        "R": lambda i, n: reduces[i].step(n),
        "G": lambda i, n: grads[i].step(n),
        "g": extra_grads,
        "M": finish_grads,
        "B": backward,
        "S": lambda i, n: swaps[i].step(1) if n == 1 else lend_far(i),
        "P": lambda i, n: pre_swaps[i].step(n),
        "W": lambda i: lends[i].step(1),
    }
    for name, *numbers in ORDER:
        act_jobs[name](*numbers)
    used = {(name, numbers[0]) for name, *numbers in ORDER}
    act_extras = [job for i, job in enumerate(act_extras) if ("a", i) in used]
    act_swaps = [job for i, job in enumerate(act_swaps) if ("Z", i) in used]
    everything = gathers + act_extras + act_swaps + reduces + grads + grad_extras + swaps + pre_swaps + lends
    for job in everything:
        job.finish()
    cross_swap[0].wait_send()

    @pl.when(first_core)
    def _():
        for copy in lent + far_lent:
            copy.wait_send()

    @pl.when(jnp.logical_not(first_core))
    def _():
        for copy in far_lent:
            copy.wait_recv()
        for copy in downs:
            copy.wait_send()


def band(acts, targets, bias, enc_bias, enc, dec_own, dec_cross, scale):
    rows, tokens = targets.shape
    width, n_feat = enc.shape
    lane = tokens // JOBS
    wide = tokens // CHUNKS
    kind = acts.dtype
    whole = pl.BlockSpec(memory_space=pltpu.VMEM)
    away = pl.BlockSpec(memory_space=pl.ANY)
    gathered = jax.ShapeDtypeStruct((3, SIDE, SIDE, rows, tokens), kind)
    feats = jax.ShapeDtypeStruct((n_feat, tokens), kind)
    dma = pltpu.SemaphoreType.DMA
    return pl.pallas_call(
        functools.partial(band_kernel, scale),
        out_shape=(
            jax.ShapeDtypeStruct((rows, tokens), jnp.float32),
            gathered,
            gathered,
            feats, feats, feats, feats, feats, feats,
            jax.ShapeDtypeStruct((2, SIDE // 2, SIDE, rows, tokens), kind),
            jax.ShapeDtypeStruct((CHUNKS, 2, n_feat // 2, wide), kind),
            jax.ShapeDtypeStruct((CHUNKS, 2, n_feat // 2, wide), kind),
            jax.ShapeDtypeStruct((CHUNKS, 2, 1, SIDE, rows, wide), kind),
            jax.ShapeDtypeStruct((CHUNKS, 2, SIDE // 2, SIDE, rows, wide), kind),
        ),
        in_specs=[whole] * 4 + [away] * 3,
        out_specs=(whole, away, away) + (whole,) * 6 + (away,) * 5,
        scratch_shapes=[
            pltpu.VMEM((width, n_feat), kind),
            pltpu.VMEM((n_feat, width), kind),
            pltpu.VMEM((n_feat, width), kind),
            pltpu.VMEM((width, n_feat), kind),
            pltpu.VMEM((width, n_feat), kind),
            pltpu.VMEM((2,) + dec_cross.shape, kind),
            pltpu.VMEM((n_feat, 128), jnp.float32),
            pltpu.VMEM((n_feat, tokens), jnp.float32),
            pltpu.VMEM((n_feat, tokens), kind),
            pltpu.VMEM((n_feat, tokens), kind),
            pltpu.VMEM((2, 2, SIDE, SIDE, rows, wide), kind),
            pltpu.VMEM((CHUNKS, 2, SIDE, SIDE, rows, wide), kind),
            pltpu.VMEM((rows, tokens), kind),
            pltpu.VMEM((JOBS, 2, SIDE, rows, lane), kind),
            pltpu.VMEM((JOBS, 2, 2, SIDE, rows, lane), kind),
            pltpu.VMEM((JOBS, 2, rows, lane), kind),
            pltpu.VMEM((JOBS, 2, 2, rows, lane), kind),
            pltpu.VMEM((JOBS, rows, lane), kind),
            dma((JOBS, Gather.sems)),
            dma((JOBS, Gather.sems)),
            dma((JOBS, Reduce.sems)),
            dma((JOBS, Reduce.sems)),
            dma((JOBS, Gather.sems)),
            dma((JOBS, Gather.sems)),
            dma((CHUNKS, Swap.sems)),
            dma((CHUNKS, Swap.sems)),
            dma((CHUNKS, Swap.sems)),
            dma((CHUNKS, Swap.sems)),
            dma((CHUNKS, Lend.sems)),
            dma((CHUNKS, Lend.sems)),
            dma((CHUNKS, Gather.sems)),
            dma((CHUNKS, Gather.sems)),
            dma((CHUNKS, Gather.sems)),
            dma((CHUNKS, Gather.sems)),
            dma((CHUNKS, Swap.sems)),
            dma((CHUNKS, Swap.sems)),
            dma((JOBS,)),
            dma((JOBS,)),
            dma((3,)),
            dma((CHUNKS,)),
            dma((CHUNKS,)),
            dma((3 * CHUNKS + 1,)),
            dma((3 * CHUNKS + 1,)),
        ],
        compiler_params=pltpu.CompilerParams(
            collective_id=1, has_side_effects=True, vmem_limit_bytes=60 * 1024 * 1024
        ),
        name="band",
    )(acts, targets, bias, enc_bias, enc, dec_own, dec_cross)


def weights_kernel(
    acts_in, grads_in, rows_in, feats_in, far_in, first_in, far_first_in, pre_in, far_pre_in,
    enc_out, own_out, cross_out,
    acts, grads, rows, feats, first, pre, enc_g, own_g, cross_g, load_sem, store_sem,
):
    dp = lax.axis_index("dp")
    half = SIDE // 2
    n_feat, width = own_g.shape
    block = width // 2
    started = []

    def load(src, dst):
        copy = pltpu.make_async_copy(src, dst, load_sem.at[len(started)])
        copy.start()
        started.append(copy)
        return copy

    ys = [pl.ds(half * part, half) for part in (0, 1)]
    first_loads = [load(feats_in, feats.at[0]), load(far_in, feats.at[1])]
    grad_loads = [[load(grads_in.at[slot, y], grads.at[i, y]) for i, slot in ((0, dp), (1, 2))] for y in ys]
    pre_loads = [load(pre_in, pre.at[0]), load(far_pre_in, pre.at[1])]
    act_loads = [[load(acts_in.at[slot, y], acts.at[i, y]) for i, slot in ((0, dp), (1, 2))] for y in ys]
    cross_loads = [load(first_in, first.at[0]), load(far_first_in, first.at[1])]
    upper = lax.axis_index("layer") == 1
    mine = pl.ds(half * dp, half)

    def load_rows(i, here, slot):
        at = len(started)

        @pl.when(here)
        def _():
            pltpu.make_async_copy(grads_in.at[slot, mine], rows.at[i], load_sem.at[at]).start()

        @pl.when(jnp.logical_not(here))
        def _():
            pltpu.make_async_copy(rows_in.at[i], rows.at[i], load_sem.at[at]).start()

        started.append(pltpu.make_async_copy(rows_in.at[i], rows.at[i], load_sem.at[at]))
        return started[-1]

    cross_loads += [load_rows(0, upper, 1), load_rows(1, jnp.logical_and(upper, dp == 1), 2)]
    stores = []

    def store(src, dst):
        copy = pltpu.make_async_copy(src, dst, store_sem.at[len(stores)])
        copy.start()
        stores.append(copy)

    def both(a, b):
        return matmul(a[0], b[0], 1, 1) + matmul(a[1], b[1], 1, 1)

    step = n_feat // 2

    def by_feats(left, right, out, columns):
        @pl.loop(0, 2)
        def _(m):
            at = pl.ds(pl.multiple_of(m * step, step), step)
            out[at, columns] = both((left[0, at, :], left[1, at, :]), right())

    for copy in first_loads:
        copy.wait()
    for part in (0, 1):
        for copy in grad_loads[part]:
            copy.wait()
        columns = pl.ds(part * block, block)
        by_feats(feats, lambda: [grads[i, ys[part]].reshape(block, -1) for i in (0, 1)], own_g, columns)
        store(own_g.at[:, columns], own_out.at[:, columns])
    for copy in pre_loads:
        copy.wait()
    for part in (0, 1):
        for copy in act_loads[part]:
            copy.wait()
        for y in range(half * part, half * part + half):
            at = pl.ds(y * (width // SIDE), width // SIDE)
            enc_g[at, :] = both([acts[i, y].reshape(width // SIDE, -1) for i in (0, 1)], [pre[0], pre[1]])
            store(enc_g.at[at, :], enc_out.at[at, :])
    for copy in cross_loads:
        copy.wait()
    by_feats(first, lambda: [rows[i].reshape(block, -1) for i in (0, 1)], cross_g, pl.ds(0, block))
    store(cross_g, cross_out)
    for copy in stores:
        copy.wait()


def weights(acts, grads, lent, feats, far, first, far_first, pre, far_pre):
    rows, tokens = acts.shape[3:]
    n_feat = feats.shape[0]
    half = SIDE * SIDE * rows
    kind = acts.dtype
    f32 = jnp.float32
    away = pl.BlockSpec(memory_space=pl.ANY)
    shapes = [(half, n_feat), (n_feat, half), (n_feat, half // 2)]
    return pl.pallas_call(
        weights_kernel,
        out_shape=[jax.ShapeDtypeStruct(s, f32) for s in shapes],
        in_specs=[away] * 9,
        out_specs=[away] * 3,
        scratch_shapes=[
            pltpu.VMEM((2, SIDE, SIDE, rows, tokens), kind),
            pltpu.VMEM((2, SIDE, SIDE, rows, tokens), kind),
            pltpu.VMEM(lent.shape, kind),
            pltpu.VMEM((2, n_feat, tokens), kind),
            pltpu.VMEM((2, n_feat, tokens), kind),
            pltpu.VMEM((2, n_feat, tokens), kind),
        ]
        + [pltpu.VMEM(s, f32) for s in shapes]
        + [pltpu.SemaphoreType.DMA((16,)), pltpu.SemaphoreType.DMA((8,))],
        compiler_params=pltpu.CompilerParams(vmem_limit_bytes=60 * 1024 * 1024),
        name="weights",
    )(acts, grads, lent, feats, far, first, far_first, pre, far_pre)


def local(acts, targets, enc, enc_bias, dec_own, dec_cross, dec_bias):
    tokens, rows = acts.shape[1:]
    scale = float(tokens * lax.axis_size("dp")) ** (-0.5)
    bias = dec_bias.astype(jnp.float32).reshape(rows, 1)
    residual, gathered, grads, feats, first, far, far_first, pre, far_pre, lent = band(
        acts[0].T, targets[0].T, bias, enc_bias, enc[0], dec_own[0], dec_cross, scale
    )[:10]
    grad_enc, grad_own, grad_cross = weights(gathered, grads, lent, feats, far, first, far_first, pre, far_pre)
    return (residual.T[None], grad_enc[None], grad_own[None], grad_cross)


def solution(mesh):
    in_specs = (
        P("layer", "dp", "feat"),
        P("layer", "dp", "feat"),
        P("layer", None, "feat"),
        P("layer", "feat"),
        P("layer", "feat", None),
        P("feat", "layer"),
        P("layer", "feat"),
    )
    out_specs = (
        P("layer", "dp", "feat"),
        P("layer", "dp", "feat"),
        P("layer", "feat", "dp"),
        P("feat", ("layer", "dp")),
    )
    return jax.shard_map(local, mesh=mesh, in_specs=in_specs, out_specs=out_specs, check_vma=False)
```

```python
import functools

import jax
import jax.numpy as jnp
from jax import lax
from jax.experimental import pallas as pl
from jax.experimental.pallas import tpu as pltpu
from jax.sharding import PartitionSpec as P

MESH = pl.DeviceIdType.MESH
ALL = slice(None)
SIDE = 4
JOBS = 8


class Place:
    def __init__(self):
        feat = lax.axis_index("feat")
        self.core = lax.axis_index("layer")
        self.dp = lax.axis_index("dp")
        self.x = lax.rem(feat, SIDE)
        self.y = lax.rem(lax.div(feat, SIDE), SIDE)
        self.zl = lax.div(feat, SIDE * SIDE)

    def feat(self, zl=None, y=None, x=None):
        zl = self.zl if zl is None else zl
        y = self.y if y is None else y
        x = self.x if x is None else x
        return (zl * SIDE + y) * SIDE + x

    def at(self, axis):
        return self.x if axis == "x" else self.y

    def along(self, axis, step):
        return lax.rem(self.at(axis) + (step + SIDE), SIDE)

    def neighbour(self, axis, step):
        return {"feat": self.feat(**{axis: self.along(axis, step)})}

    def pair(self):
        return {"feat": self.feat(zl=1 - self.zl)}

    def across(self, zl):
        return {"feat": self.feat(zl=zl), "dp": 1 - self.dp}

    def other_core(self):
        return {"layer": 1 - self.core}

    def greet(self):
        peers = [self.neighbour(a, s) for a in "xy" for s in (1, -1)]
        peers += [self.pair(), self.across(0), self.across(1)]
        peers.append(self.other_core())
        peers += [dict(self.pair(), **self.other_core()), dict(self.across(1 - self.zl), **self.other_core())]
        barrier = pltpu.get_barrier_semaphore()
        for peer in peers:
            pl.semaphore_signal(barrier, inc=1, device_id=peer, device_id_type=MESH)
        pl.semaphore_wait(barrier, len(peers))


def remote(src, dst, send, recv, device):
    return pltpu.make_async_remote_copy(
        src_ref=src, dst_ref=dst, send_sem=send, recv_sem=recv, device_id=device, device_id_type=MESH
    )


class Gather:
    sems = 11
    steps = 6

    whole, right, left = (slice(0, 2), ALL), (slice(0, 1), ALL), (slice(1, 2), ALL)

    def __init__(self, place, buf, own, lanes, flip, send, recv, local, job):
        self.place, self.buf, self.own, self.lanes = place, buf, own, lanes
        self.first, self.second = ("y", "x") if flip else ("x", "y")
        self.send, self.recv, self.local, self.job = send, recv, local, job
        self.sent = []

    def first_block(self, part, at):
        p = self.place
        slots, rows = part
        index = (slots, p.y, at, rows, self.lanes) if self.first == "x" else (slots, at, p.x, rows, self.lanes)
        return self.buf.at[index]

    def second_block(self, part, at):
        slots, rows = part
        index = (slots, at, ALL, rows, self.lanes) if self.second == "y" else (slots, ALL, at, rows, self.lanes)
        return self.buf.at[index]

    def copy(self, sem, src, dst, device, recv=None):
        return remote(src, dst, self.send.at[self.job, sem], self.recv.at[self.job, sem if recv is None else recv], device)

    def out(self, sem, block, device):
        copy = self.copy(sem, block, block, device)
        copy.start()
        self.sent.append(copy)
        return copy

    def ring(self, sem, axis, block):
        p = self.place
        own = block(self.whole, p.at(axis))
        return (self.out(sem, own, p.neighbour(axis, 1)), self.out(sem + 1, own, p.neighbour(axis, -1)))

    def forward(self, sem, axis, block):
        p = self.place
        return (
            self.out(sem, block(self.right, p.along(axis, -1)), p.neighbour(axis, 1)),
            self.out(sem + 1, block(self.left, p.along(axis, 1)), p.neighbour(axis, -1)),
        )

    def begin(self):
        p = self.place
        here = self.buf.at[p.zl, p.y, p.x, :, self.lanes]
        self.kept = pltpu.make_async_copy(self.own, here, self.local.at[self.job])
        self.kept.start()
        self.waits = [self.copy(0, self.own, here, p.pair())]
        self.waits[0].start()
        self.sent += self.waits

    def settle(self):
        self.kept.wait()

    def step(self, number):
        if number == 0:
            self.begin()
            return
        for copy in self.waits:
            copy.wait_recv()
        if number == 1:
            self.settle()
            self.waits = self.ring(3, self.first, self.first_block)
        elif number == 2:
            self.waits = self.forward(5, self.first, self.first_block)
        elif number == 3:
            self.waits = self.ring(7, self.second, self.second_block)
        elif number == 4:
            self.waits = self.forward(9, self.second, self.second_block)

    def finish(self):
        for copy in self.sent:
            copy.wait_send()


class Extra(Gather):
    def __init__(self, *args):
        super().__init__(*args)
        rows = self.own.shape[0]
        cut = (rows // 32 + rows % 32 // 16) * 16
        slot = slice(2, 3)
        self.whole, self.right, self.left = (slot, ALL), (slot, pl.ds(0, cut)), (slot, pl.ds(cut, rows - cut))

    def begin(self):
        p = self.place
        there = self.buf.at[2, p.y, p.x, :, self.lanes]
        self.cross = [self.copy(1 + zl, self.own, there, p.across(zl), recv=1) for zl in (0, 1)]

        @pl.when(p.zl != p.dp)
        def _():
            for copy in self.cross:
                copy.start()

        self.waits = [self.cross[0]]

    def settle(self):
        pass

    def finish(self):
        super().finish()

        @pl.when(self.place.zl != self.place.dp)
        def _():
            for copy in self.cross:
                copy.wait_send()


class Reduce:
    sems = 13
    steps = 6

    def __init__(self, place, part, lanes, flip, room, send, recv, job, finish):
        self.place, self.part, self.lanes = place, part, lanes
        self.first, self.second = ("x", "y") if flip else ("y", "x")
        self.far1, self.far2, self.near1, self.near2, self.last = room
        self.send, self.recv, self.job, self.done = send, recv, job, finish
        self.sent = []

    def first_block(self, z, at):
        return (z, at, ALL, ALL, self.lanes) if self.first == "y" else (z, ALL, at, ALL, self.lanes)

    def second_block(self, z, at):
        p = self.place
        return (z, p.y, at, ALL, self.lanes) if self.first == "y" else (z, at, p.x, ALL, self.lanes)

    def out(self, sem, src, dst, device):
        copy = remote(src, dst, self.send.at[self.job, sem], self.recv.at[self.job, sem], device)
        copy.start()
        self.sent.append(copy)
        return copy

    def add(self, index, *refs):
        total = self.part[index].astype(jnp.float32)
        for ref in refs:
            total = total + ref[...].astype(jnp.float32)
        self.part[index] = total.astype(self.part.dtype)

    def begin(self, sem, axis, block, one, two):
        p = self.place
        right, left = p.neighbour(axis, 1), p.neighbour(axis, -1)
        far, up, down = p.along(axis, 2), p.along(axis, 1), p.along(axis, -1)
        j = self.job
        self.relay = (
            self.out(sem, self.part.at[block(0, far)], one.at[j, 0], right),
            self.out(sem + 1, self.part.at[block(1, far)], one.at[j, 1], left),
        )
        self.early = (
            self.out(sem + 2, self.part.at[block(1, up)], two.at[j, 0, 1], right),
            self.out(sem + 3, self.part.at[block(0, down)], two.at[j, 1, 0], left),
        )

    def pass_on(self, sem, axis, block, one, two):
        p = self.place
        right, left = p.neighbour(axis, 1), p.neighbour(axis, -1)
        up, down = p.along(axis, 1), p.along(axis, -1)
        j = self.job
        self.relay[0].wait_recv()
        self.add(block(0, up), one.at[j, 0])
        late = self.out(sem, self.part.at[block(0, up)], two.at[j, 0, 0], right)
        self.relay[1].wait_recv()
        self.add(block(1, down), one.at[j, 1])
        self.late = (late, self.out(sem + 1, self.part.at[block(1, down)], two.at[j, 1, 1], left))

    def collect(self, axis, block, two):
        for copy in self.early + self.late:
            copy.wait_recv()
        self.add(block(slice(0, 2), self.place.at(axis)), two.at[self.job, 0], two.at[self.job, 1])

    def step(self, number):
        p = self.place
        if number == 0:
            self.begin(0, self.first, self.first_block, self.far1, self.far2)
        elif number == 1:
            self.pass_on(4, self.first, self.first_block, self.far1, self.far2)
        elif number == 2:
            self.collect(self.first, self.first_block, self.far2)
            self.begin(6, self.second, self.second_block, self.near1, self.near2)
        elif number == 3:
            self.pass_on(10, self.second, self.second_block, self.near1, self.near2)
        elif number == 4:
            self.collect(self.second, self.second_block, self.near2)
            gone = self.part.at[1 - p.zl, p.y, p.x, :, self.lanes]
            self.pair = self.out(12, gone, self.last.at[self.job], p.pair())
        else:
            self.pair.wait_recv()
            mine = self.part[p.zl, p.y, p.x, :, self.lanes].astype(jnp.float32)
            self.done(mine + self.last[self.job].astype(jnp.float32), self.lanes)

    def finish(self):
        for copy in self.sent:
            copy.wait_send()


class Swap:
    sems = 4

    def __init__(self, place, src, relay, dst, send, recv, job):
        self.place, self.src, self.relay, self.dst = place, src, relay, dst
        self.send, self.recv, self.job = send, recv, job
        self.sent = []

    def device(self, sem):
        p = self.place
        turn = p.zl if sem % 2 == 0 else 1 - p.zl
        return {"feat": p.feat(zl=1 - p.zl), "dp": lax.rem(p.dp + turn, 2)}

    def out(self, sem, src, dst):
        copy = remote(src, dst, self.send.at[self.job, sem], self.recv.at[self.job, sem], self.device(sem))
        copy.start()
        self.sent.append(copy)

    def step(self, number):
        if number == 0:
            for way in (0, 1):
                self.out(way, self.src[way], self.relay[way])
        elif number == 1:
            for way in (0, 1):
                self.sent[way].wait_recv()
                self.out(2 + way, self.relay[way], self.dst[way])
        else:
            for way in (0, 1):
                self.sent[2 + way].wait_recv()

    def finish(self):
        for copy in self.sent:
            copy.wait_send()


class Lend:
    sems = 8

    def __init__(self, place, buf, relay, rows, lanes, send, recv, job):
        p = self.place = place
        self.lanes = lanes
        half = SIDE // 2
        self.upper = p.core == 1
        self.upper_gives = jnp.logical_and(self.upper, p.dp == 0)
        self.lower_gets = jnp.logical_and(p.core == 0, p.dp == 0)
        self.over_z = p.core == 1 - p.dp
        ys = pl.ds(half * p.dp, half)
        own, far = rows.at[0, :, :, :, lanes], rows.at[1, :, :, :, lanes]
        copy = lambda sem, src, dst, device: remote(src, dst, send.at[job, sem], recv.at[job, sem], device)
        self.give_own = copy(0, buf.at[0, ys, :, :, lanes], own, p.other_core())
        self.give_far = copy(1, buf.at[2, ys, :, :, lanes], far, p.other_core())
        self.first, self.second = [], []
        for way in range(2):
            turn = p.zl if way == 0 else 1 - p.zl
            dp = lax.rem(p.dp + turn, 2)
            device = {"feat": p.feat(zl=1 - p.zl), "dp": dp}
            src = buf.at[p.dp, pl.ds(half * (1 - p.dp) + way, 1), :, :, lanes]
            self.first.append(copy(2 + way, src, relay.at[job, way], device))
            dst = rows.at[1, pl.ds(way, 1), :, :, lanes]
            self.second.append(copy(4 + way, relay.at[job, way], dst, dict(device, layer=1 - dp)))

    def step(self, number):
        if number == 0:

            @pl.when(self.upper)
            def _():
                for copy in self.first + [self.give_own]:
                    copy.start()

        elif number == 1:

            @pl.when(self.upper)
            def _():
                for way in range(2):
                    self.first[way].wait_recv()
                    self.second[way].start()

        else:

            @pl.when(self.upper_gives)
            def _():
                self.give_far.start()

    def finish(self):
        @pl.when(self.upper)
        def _():
            for copy in self.first + self.second + [self.give_own]:
                copy.wait_send()

        @pl.when(jnp.logical_not(self.upper))
        def _():
            self.give_own.wait_recv()

        @pl.when(self.upper_gives)
        def _():
            self.give_far.wait_send()

        @pl.when(self.lower_gets)
        def _():
            self.give_far.wait_recv()

        @pl.when(self.over_z)
        def _():
            for copy in self.second:
                copy.wait_recv()


def matmul(a, b, over_a=1, over_b=0):
    return lax.dot_general(a, b, (((over_a,), (over_b,)), ((), ())), preferred_element_type=jnp.float32)


CHUNKS = JOBS // 2

ORDER = (
    ("A", 6, 0), ("A", 7, 0), ("A", 4, 0), ("A", 5, 0), ("A", 2, 0), ("A", 3, 0), ("A", 0, 0), ("A", 1, 0),
    ("a", 0, 0), ("A", 6, 1), ("A", 7, 1), ("A", 4, 1), ("A", 5, 1), ("a", 1, 0), ("T", 0), ("A", 2, 1),
    ("A", 3, 1), ("a", 2, 0), ("T", 1), ("A", 0, 1), ("A", 1, 1), ("T", 2), ("a", 3, 0), ("T", 3), ("A", 6, 2),
    ("A", 7, 2), ("T", 4), ("T", 5), ("A", 4, 2), ("A", 5, 2), ("T", 6), ("T", 7), ("a", 0, 1), ("A", 2, 2),
    ("A", 3, 2), ("T", 8), ("a", 1, 1), ("T", 9), ("A", 0, 2), ("A", 1, 2), ("T", 10), ("A", 6, 3), ("A", 7, 3),
    ("T", 11), ("A", 4, 3), ("A", 5, 3), ("T", 12), ("A", 3, 3), ("T", 13), ("T", 14), ("T", 15), ("A", 2, 3),
    ("T", 16), ("A", 0, 3), ("A", 1, 3), ("T", 17), ("T", 18), ("T", 19), ("T", 20), ("T", 21), ("T", 22),
    ("T", 23), ("T", 24), ("T", 25), ("T", 26), ("T", 27), ("A", 7, 4), ("A", 6, 4), ("A", 5, 4), ("A", 4, 4),
    ("A", 3, 4), ("A", 2, 4), ("A", 1, 4), ("A", 0, 4), ("A", 7, 5), ("A", 6, 5), ("L", 3), ("F", 3), ("A", 5, 5),
    ("A", 4, 5), ("L", 2), ("a", 2, 1), ("a", 3, 1), ("A", 3, 5), ("A", 2, 5), ("L", 1), ("F", 2), ("D", 3, 0),
    ("D", 3, 1), ("R", 6, 0), ("R", 7, 0), ("S", 3, 1), ("D", 2, 0), ("D", 2, 1), ("R", 4, 0), ("R", 5, 0),
    ("R", 6, 1), ("R", 7, 1), ("S", 3, 2), ("S", 2, 1), ("F", 1), ("A", 1, 5), ("A", 0, 5), ("L", 0), ("R", 4, 1),
    ("R", 5, 1), ("S", 2, 2), ("D", 1, 0), ("D", 1, 1), ("R", 2, 0), ("R", 3, 0), ("S", 1, 1), ("R", 6, 2),
    ("R", 7, 2), ("F", 0), ("R", 4, 2), ("R", 5, 2), ("S", 1, 2), ("R", 2, 1), ("R", 3, 1), ("D", 0, 0),
    ("R", 7, 3), ("R", 6, 3), ("R", 5, 3), ("R", 4, 3), ("D", 0, 1), ("R", 0, 0), ("R", 1, 0), ("S", 0, 1),
    ("R", 2, 2), ("R", 7, 4), ("R", 6, 4), ("R", 5, 4), ("R", 4, 4), ("R", 3, 2), ("R", 0, 1), ("R", 1, 1),
    ("R", 7, 5), ("G", 7, 0), ("R", 6, 5), ("G", 6, 0), ("R", 5, 5), ("G", 5, 0), ("R", 4, 5), ("G", 4, 0),
    ("S", 0, 2), ("g", 2, 0), ("R", 3, 3), ("g", 3, 0), ("R", 2, 3), ("a", 1, 2), ("G", 7, 1), ("a", 0, 2),
    ("G", 6, 1), ("G", 5, 1), ("G", 4, 1), ("R", 0, 2), ("R", 3, 4), ("R", 2, 4), ("R", 1, 2), ("a", 2, 2),
    ("G", 7, 2), ("a", 3, 2), ("G", 6, 2), ("a", 0, 3), ("R", 3, 5), ("G", 3, 0), ("R", 2, 5), ("G", 5, 2),
    ("G", 2, 0), ("G", 4, 2), ("g", 1, 0), ("a", 1, 3), ("R", 1, 3), ("R", 0, 3), ("G", 7, 3), ("G", 3, 1),
    ("G", 2, 1), ("G", 6, 3), ("G", 4, 3), ("G", 5, 3), ("R", 1, 4), ("R", 0, 4), ("G", 3, 2), ("R", 1, 5),
    ("G", 1, 0), ("R", 0, 5), ("G", 0, 0), ("g", 0, 0), ("G", 1, 1), ("G", 0, 1), ("G", 7, 4), ("G", 6, 4),
    ("G", 2, 2), ("G", 4, 4), ("G", 5, 4), ("G", 3, 3), ("G", 0, 2), ("G", 1, 2), ("G", 7, 5), ("G", 6, 5),
    ("M", 3), ("g", 3, 1), ("G", 2, 3), ("B", 3, 0), ("G", 4, 5), ("G", 5, 5), ("M", 2), ("G", 1, 3), ("W", 3),
    ("B", 2, 0), ("B", 3, 1), ("W", 2), ("G", 3, 4), ("a", 2, 3), ("B", 2, 1), ("G", 2, 4), ("G", 0, 3),
    ("P", 3, 1), ("g", 2, 1), ("G", 1, 4), ("G", 3, 5), ("a", 3, 3), ("G", 2, 5), ("M", 1), ("P", 2, 1),
    ("B", 1, 0), ("G", 1, 5), ("g", 1, 1), ("a", 0, 4), ("P", 3, 2), ("a", 1, 4), ("G", 0, 4), ("B", 1, 1),
    ("W", 1), ("g", 0, 1), ("g", 3, 2), ("g", 2, 2), ("P", 2, 2), ("a", 0, 5), ("a", 2, 4), ("a", 3, 4),
    ("a", 1, 5), ("G", 0, 5), ("M", 0), ("P", 1, 1), ("g", 1, 2), ("g", 0, 2), ("g", 2, 3), ("g", 3, 3),
    ("B", 0, 0), ("a", 2, 5), ("a", 3, 5), ("W", 0), ("B", 0, 1), ("g", 1, 3), ("g", 0, 3), ("P", 1, 2),
    ("g", 2, 4), ("g", 3, 4), ("P", 0, 1), ("g", 0, 4), ("g", 1, 4), ("g", 2, 5), ("g", 3, 5), ("P", 0, 2),
    ("g", 0, 5), ("g", 1, 5),
)


def band_kernel(
    scale, acts_in, target_ref, bias_ref, enc_bias_ref, enc_in, dec_in, cross_in,
    resid_ref, acts_buf, grad_buf, feats_out, lower_out, far_out, far_lower_ref, pre_ref, far_pre_ref, rows_buf,
    relay, pre_relay, rows_relay, acts_relay,
    enc_n, dec_n, enc_t, dec_t, cross_t, cross_ref, feats_ref, lower_ref, far_ref, bias_t, enc_bias_t, positive_ref, down_ref, up_ref,
    chunk, part, shard, far1, far2, near1, near2, last,
    send_a, recv_a, send_r, recv_r, send_g, recv_g, send_s, recv_s, send_p, recv_p, send_l, recv_l,
    send_xa, recv_xa, send_xg, recv_xg, send_z, recv_z,
    local_a, local_g, load_sem, chunk_sem, grad_sem, out_sem, core_send, core_recv,
):
    tokens = acts_in.shape[1]
    wide = tokens // CHUNKS
    lane = wide // 2
    rows = acts_in.shape[0]
    n_feat = feats_ref.shape[0]
    half = cross_ref.shape[2]
    width = 2 * half
    place = Place()
    first_core = place.core == 0

    loads = [
        pltpu.make_async_copy(enc_in, enc_n, load_sem.at[0]),
        pltpu.make_async_copy(dec_in, dec_n, load_sem.at[1]),
        pltpu.make_async_copy(cross_in, cross_ref.at[place.core], load_sem.at[2]),
    ]
    for load in loads:
        load.start()
    place.greet()

    def swap_cross():
        at = 3 * CHUNKS
        copy = remote(cross_in, cross_ref.at[place.core], core_send.at[at], core_recv.at[at], place.other_core())
        copy.start()
        return copy

    def finish_residual(total, lanes):
        resid = total + bias_t[:, 0:1] - target_ref[:, lanes].astype(jnp.float32)
        resid_ref[:, lanes] = resid
        shard[:, lanes] = (resid * scale).astype(shard.dtype)

    room = (far1, far2, near1, near2, last)
    gathers, reduces, grads, swaps, lent, far_lent, pre_swaps, lends, downs = [], [], [], [], [], [], [], [], []
    act_extras, grad_extras, act_swaps = [], [], []
    for job in range(JOBS):
        c, flip = job // 2, job % 2
        lanes = pl.ds(job * lane, lane)
        gathers.append(
            Gather(place, acts_buf, acts_in.at[:, lanes], lanes, flip, send_a, recv_a, local_a, job)
        )
        grads.append(Gather(place, grad_buf, shard.at[:, lanes], lanes, flip, send_g, recv_g, local_g, job))
        inner = pl.ds(flip * lane, lane)
        done = functools.partial(lambda whole, total, _: finish_residual(total, whole), lanes)
        reduces.append(Reduce(place, part.at[c], inner, flip, room, send_r, recv_r, job, done))
    for c in range(CHUNKS):
        lanes = pl.ds(c * wide, wide)
        ways = [pl.ds(way * (n_feat // 2), n_feat // 2) for way in (0, 1)]

        def dp_swap(here, between, there, send, recv):
            return Swap(
                place, [here.at[w, lanes] for w in ways], [between.at[c, way] for way in (0, 1)],
                [there.at[w, lanes] for w in ways], send, recv, c,
            )

        def to_core(kind, here, there):
            at = kind * CHUNKS + c
            return remote(
                here.at[:, lanes], there.at[:, lanes], core_send.at[at], core_recv.at[at], place.other_core()
            )

        swaps.append(dp_swap(feats_ref, relay, far_ref, send_s, recv_s))
        pre_swaps.append(dp_swap(pre_ref, pre_relay, far_pre_ref, send_p, recv_p))
        lent.append(to_core(0, feats_ref, lower_ref))
        far_lent.append(to_core(1, far_ref, far_lower_ref))
        downs.append(to_core(2, down_ref, up_ref))
        act_extras.append(
            Extra(place, acts_buf, acts_in.at[:, lanes], lanes, c % 2, send_xa, recv_xa, None, c)
        )
        grad_extras.append(Extra(place, grad_buf, shard.at[:, lanes], lanes, c % 2, send_xg, recv_xg, None, c))
        y_halves = [pl.ds(way * (SIDE // 2), SIDE // 2) for way in (0, 1)]
        act_swaps.append(
            Swap(
                place, [acts_buf.at[1 - place.dp, ys, :, :, lanes] for ys in y_halves],
                [acts_relay.at[c, way] for way in (0, 1)], [acts_buf.at[2, ys, :, :, lanes] for ys in y_halves],
                send_z, recv_z, c,
            )
        )
        lends.append(Lend(place, grad_buf, rows_relay, rows_buf, lanes, send_l, recv_l, c))

    def load_chunk(c):
        return pltpu.make_async_copy(
            acts_buf.at[pl.ds(0, 2), :, :, :, pl.ds(c * wide, wide)], chunk.at[c % 2], chunk_sem.at[c]
        )

    def encode(c):
        load_chunk(c).wait()
        lanes = pl.ds(c * wide, wide)
        pre_act = matmul(enc_t[...], chunk[c % 2].reshape(width, wide)) + enc_bias_t[:, 0:1]
        positive = jnp.maximum(pre_act, 0.0)
        positive_ref[:, lanes] = positive
        feats_ref[:, lanes] = (positive * positive).astype(feats_ref.dtype)

        @pl.when(first_core)
        def _():
            lent[c].start()
            lower_ref[:, lanes] = feats_ref[:, lanes]

        swaps[c].step(0)

    outs = [
        pltpu.make_async_copy(here, there, out_sem.at[i])
        for i, (here, there) in enumerate([(feats_ref, feats_out), (lower_ref, lower_out), (far_ref, far_out)])
    ]
    lent_far = []

    def lend_far(c):
        swaps[c].step(2)
        lent_far.append(c)
        if len(lent_far) == CHUNKS:
            for copy in outs:
                copy.start()
        lanes = pl.ds(c * wide, wide)

        @pl.when(first_core)
        def _():
            far_lent[c].start()
            far_lower_ref[:, lanes] = far_ref[:, lanes]

    def decode(c, side):
        lanes = pl.ds(c * wide, wide)
        block = SIDE * rows

        def store(i, total):
            part[c, lax.div(i, SIDE), lax.rem(i, SIDE)] = total.astype(part.dtype).reshape(SIDE, rows, wide)

        def at(i):
            return pl.ds(pl.multiple_of(i * block, 16), block)

        @pl.when(first_core)
        def _():
            @pl.loop(side * SIDE, side * SIDE + SIDE)
            def _(i):
                store(i, matmul(dec_t[at(i), :], feats_ref[:, lanes]))

        @pl.when(jnp.logical_not(first_core))
        def _():
            if side == 0:
                lent[c].wait_recv()

            @pl.loop(side * SIDE, side * SIDE + SIDE)
            def _(i):
                total = matmul(dec_t[at(i), :], feats_ref[:, lanes]) + matmul(cross_t[at(i), :], lower_ref[:, lanes])
                store(i, total)

    def load_grads(c):
        return pltpu.make_async_copy(
            grad_buf.at[pl.ds(0, 2), :, :, :, pl.ds(c * wide, wide)], chunk.at[c % 2], grad_sem.at[c]
        )

    def finish_grads(c):
        load_grads(c).start()
        lends[c].step(0)

    def extra_grads(c, number):
        grad_extras[c].step(number)
        if number == Gather.steps - 1:
            lends[c].step(2)

    def backward(c, part):
        lanes = pl.ds(c * wide, wide)
        here = chunk.at[c % 2]
        if part == 0:
            load_grads(c).wait()
            send_down(c, lanes, here)
        else:
            make_pre(c, lanes, here)

    def send_down(c, lanes, here):
        @pl.when(jnp.logical_not(first_core))
        def _():
            down = matmul(cross_ref[0], here[0].reshape(half, wide)) + matmul(cross_ref[1], here[1].reshape(half, wide))
            down_ref[:, lanes] = down.astype(down_ref.dtype)
            downs[c].start()

    def make_pre(c, lanes, here):
        grad_feats = matmul(dec_n[...], here[...].reshape(width, wide))

        @pl.when(first_core)
        def _():
            downs[c].wait_recv()
            total = grad_feats + up_ref[:, lanes].astype(jnp.float32)
            pre_ref[:, lanes] = (total * 2.0 * positive_ref[:, lanes]).astype(pre_ref.dtype)

        @pl.when(jnp.logical_not(first_core))
        def _():
            pre_ref[:, lanes] = (grad_feats * 2.0 * positive_ref[:, lanes]).astype(pre_ref.dtype)

        pre_swaps[c].step(0)

    cross_swap = []

    def turn_enc(i):
        if i == 0:
            bias_t[...] = jnp.broadcast_to(bias_ref[...], (128, rows)).T
            enc_bias_t[...] = jnp.broadcast_to(enc_bias_ref[...], (128, n_feat)).T
            loads[0].wait()
        block = pl.ds(i * n_feat, n_feat)
        enc_t[:, block] = enc_n[block, :].T

    def turn_dec(i):
        if i == 0:
            loads[1].wait()
        block = pl.ds(i * n_feat, n_feat)
        dec_t[block, :] = dec_n[:, block].T

    def turn_cross(i):
        if i == 0:
            loads[2].wait()
            cross_swap[0].wait_recv()
        z, at = divmod(i * 256, half)
        cross_t[pl.ds(i * 256, 256), :] = cross_ref[z, :, pl.ds(at, 256)].T

    background = [functools.partial(turn_enc, i) for i in range(width // n_feat)]
    background += [functools.partial(turn_dec, i) for i in range(width // n_feat)]
    background += [functools.partial(turn_cross, i) for i in range(width // 256)]

    cross_swap.append(swap_cross())
    act_jobs = {
        "A": lambda i, n: gathers[i].step(n),
        "a": lambda i, n: act_extras[i].step(n),
        "Z": lambda i, n: act_swaps[i].step(n),
        "T": lambda i: background[i](),
        "L": lambda i: load_chunk(i).start(),
        "F": encode,
        "D": decode,
        "R": lambda i, n: reduces[i].step(n),
        "G": lambda i, n: grads[i].step(n),
        "g": extra_grads,
        "M": finish_grads,
        "B": backward,
        "S": lambda i, n: swaps[i].step(1) if n == 1 else lend_far(i),
        "P": lambda i, n: pre_swaps[i].step(n),
        "W": lambda i: lends[i].step(1),
    }
    for name, *numbers in ORDER:
        act_jobs[name](*numbers)
    used = {(name, numbers[0]) for name, *numbers in ORDER}
    act_extras = [job for i, job in enumerate(act_extras) if ("a", i) in used]
    act_swaps = [job for i, job in enumerate(act_swaps) if ("Z", i) in used]
    everything = gathers + act_extras + act_swaps + reduces + grads + grad_extras + swaps + pre_swaps + lends
    for job in everything:
        job.finish()
    cross_swap[0].wait_send()
    for copy in outs:
        copy.wait()

    @pl.when(first_core)
    def _():
        for copy in lent + far_lent:
            copy.wait_send()

    @pl.when(jnp.logical_not(first_core))
    def _():
        for copy in far_lent:
            copy.wait_recv()
        for copy in downs:
            copy.wait_send()


def band(acts, targets, bias, enc_bias, enc, dec_own, dec_cross, scale):
    rows, tokens = targets.shape
    width, n_feat = enc.shape
    lane = tokens // JOBS
    wide = tokens // CHUNKS
    kind = acts.dtype
    whole = pl.BlockSpec(memory_space=pltpu.VMEM)
    away = pl.BlockSpec(memory_space=pl.ANY)
    gathered = jax.ShapeDtypeStruct((3, SIDE, SIDE, rows, tokens), kind)
    feats = jax.ShapeDtypeStruct((n_feat, tokens), kind)
    dma = pltpu.SemaphoreType.DMA
    return pl.pallas_call(
        functools.partial(band_kernel, scale),
        out_shape=(
            jax.ShapeDtypeStruct((rows, tokens), jnp.float32),
            gathered,
            gathered,
            feats, feats, feats, feats, feats, feats,
            jax.ShapeDtypeStruct((2, SIDE // 2, SIDE, rows, tokens), kind),
            jax.ShapeDtypeStruct((CHUNKS, 2, n_feat // 2, wide), kind),
            jax.ShapeDtypeStruct((CHUNKS, 2, n_feat // 2, wide), kind),
            jax.ShapeDtypeStruct((CHUNKS, 2, 1, SIDE, rows, wide), kind),
            jax.ShapeDtypeStruct((CHUNKS, 2, SIDE // 2, SIDE, rows, wide), kind),
        ),
        in_specs=[whole] * 4 + [away] * 3,
        out_specs=(whole, away, away) + (away,) * 3 + (whole,) * 3 + (away,) * 5,
        scratch_shapes=[
            pltpu.VMEM((width, n_feat), kind),
            pltpu.VMEM((n_feat, width), kind),
            pltpu.VMEM((n_feat, width), kind),
            pltpu.VMEM((width, n_feat), kind),
            pltpu.VMEM((width, n_feat), kind),
            pltpu.VMEM((2,) + dec_cross.shape, kind),
            pltpu.VMEM((n_feat, tokens), kind),
            pltpu.VMEM((n_feat, tokens), kind),
            pltpu.VMEM((n_feat, tokens), kind),
            pltpu.VMEM((rows, 128), jnp.float32),
            pltpu.VMEM((n_feat, 128), jnp.float32),
            pltpu.VMEM((n_feat, tokens), jnp.float32),
            pltpu.VMEM((n_feat, tokens), kind),
            pltpu.VMEM((n_feat, tokens), kind),
            pltpu.VMEM((2, 2, SIDE, SIDE, rows, wide), kind),
            pltpu.VMEM((CHUNKS, 2, SIDE, SIDE, rows, wide), kind),
            pltpu.VMEM((rows, tokens), kind),
            pltpu.VMEM((JOBS, 2, SIDE, rows, lane), kind),
            pltpu.VMEM((JOBS, 2, 2, SIDE, rows, lane), kind),
            pltpu.VMEM((JOBS, 2, rows, lane), kind),
            pltpu.VMEM((JOBS, 2, 2, rows, lane), kind),
            pltpu.VMEM((JOBS, rows, lane), kind),
            dma((JOBS, Gather.sems)),
            dma((JOBS, Gather.sems)),
            dma((JOBS, Reduce.sems)),
            dma((JOBS, Reduce.sems)),
            dma((JOBS, Gather.sems)),
            dma((JOBS, Gather.sems)),
            dma((CHUNKS, Swap.sems)),
            dma((CHUNKS, Swap.sems)),
            dma((CHUNKS, Swap.sems)),
            dma((CHUNKS, Swap.sems)),
            dma((CHUNKS, Lend.sems)),
            dma((CHUNKS, Lend.sems)),
            dma((CHUNKS, Gather.sems)),
            dma((CHUNKS, Gather.sems)),
            dma((CHUNKS, Gather.sems)),
            dma((CHUNKS, Gather.sems)),
            dma((CHUNKS, Swap.sems)),
            dma((CHUNKS, Swap.sems)),
            dma((JOBS,)),
            dma((JOBS,)),
            dma((3,)),
            dma((CHUNKS,)),
            dma((CHUNKS,)),
            dma((3,)),
            dma((3 * CHUNKS + 1,)),
            dma((3 * CHUNKS + 1,)),
        ],
        compiler_params=pltpu.CompilerParams(
            collective_id=1, has_side_effects=True, vmem_limit_bytes=60 * 1024 * 1024
        ),
        name="band",
    )(acts, targets, bias, enc_bias, enc, dec_own, dec_cross)


def weights_kernel(
    acts_in, grads_in, rows_in, feats_in, far_in, first_in, far_first_in, pre_in, far_pre_in,
    enc_out, own_out, cross_out,
    acts, grads, rows, feats, first, pre, enc_g, own_g, cross_g, load_sem, store_sem,
):
    dp = lax.axis_index("dp")
    half = SIDE // 2
    n_feat, width = own_g.shape
    block = width // 2
    started = []

    def load(src, dst):
        copy = pltpu.make_async_copy(src, dst, load_sem.at[len(started)])
        copy.start()
        started.append(copy)
        return copy

    ys = [pl.ds(half * part, half) for part in (0, 1)]
    first_loads = [load(feats_in, feats.at[0]), load(far_in, feats.at[1])]
    grad_loads = [[load(grads_in.at[slot, y], grads.at[i, y]) for i, slot in ((0, dp), (1, 2))] for y in ys]
    pre_loads = [load(pre_in, pre.at[0]), load(far_pre_in, pre.at[1])]
    act_loads = [[load(acts_in.at[slot, y], acts.at[i, y]) for i, slot in ((0, dp), (1, 2))] for y in ys]
    cross_loads = [load(first_in, first.at[0]), load(far_first_in, first.at[1])]
    upper = lax.axis_index("layer") == 1
    mine = pl.ds(half * dp, half)

    def load_rows(i, here, slot):
        at = len(started)

        @pl.when(here)
        def _():
            pltpu.make_async_copy(grads_in.at[slot, mine], rows.at[i], load_sem.at[at]).start()

        @pl.when(jnp.logical_not(here))
        def _():
            pltpu.make_async_copy(rows_in.at[i], rows.at[i], load_sem.at[at]).start()

        started.append(pltpu.make_async_copy(rows_in.at[i], rows.at[i], load_sem.at[at]))
        return started[-1]

    cross_loads += [load_rows(0, upper, 1), load_rows(1, jnp.logical_and(upper, dp == 1), 2)]
    stores = []

    def store(src, dst):
        copy = pltpu.make_async_copy(src, dst, store_sem.at[len(stores)])
        copy.start()
        stores.append(copy)

    def both(a, b):
        return matmul(a[0], b[0], 1, 1) + matmul(a[1], b[1], 1, 1)

    def by_feats(left, right, out, columns):
        out[:, columns] = both((left[0], left[1]), right())

    for copy in first_loads:
        copy.wait()
    for part in (0, 1):
        for copy in grad_loads[part]:
            copy.wait()
        columns = pl.ds(part * block, block)
        by_feats(feats, lambda: [grads[i, ys[part]].reshape(block, -1) for i in (0, 1)], own_g, columns)
        store(own_g.at[:, columns], own_out.at[:, columns])
    for copy in pre_loads:
        copy.wait()
    for part in (0, 1):
        for copy in act_loads[part]:
            copy.wait()
        for y in range(half * part, half * part + half):
            at = pl.ds(y * (width // SIDE), width // SIDE)
            enc_g[at, :] = both([acts[i, y].reshape(width // SIDE, -1) for i in (0, 1)], [pre[0], pre[1]])
            store(enc_g.at[at, :], enc_out.at[at, :])
    for copy in cross_loads:
        copy.wait()
    by_feats(first, lambda: [rows[i].reshape(block, -1) for i in (0, 1)], cross_g, pl.ds(0, block))
    store(cross_g, cross_out)
    for copy in stores:
        copy.wait()


def weights(acts, grads, lent, feats, far, first, far_first, pre, far_pre):
    rows, tokens = acts.shape[3:]
    n_feat = feats.shape[0]
    half = SIDE * SIDE * rows
    kind = acts.dtype
    f32 = jnp.float32
    away = pl.BlockSpec(memory_space=pl.ANY)
    shapes = [(half, n_feat), (n_feat, half), (n_feat, half // 2)]
    return pl.pallas_call(
        weights_kernel,
        out_shape=[jax.ShapeDtypeStruct(s, f32) for s in shapes],
        in_specs=[away] * 9,
        out_specs=[away] * 3,
        scratch_shapes=[
            pltpu.VMEM((2, SIDE, SIDE, rows, tokens), kind),
            pltpu.VMEM((2, SIDE, SIDE, rows, tokens), kind),
            pltpu.VMEM(lent.shape, kind),
            pltpu.VMEM((2, n_feat, tokens), kind),
            pltpu.VMEM((2, n_feat, tokens), kind),
            pltpu.VMEM((2, n_feat, tokens), kind),
        ]
        + [pltpu.VMEM(s, f32) for s in shapes]
        + [pltpu.SemaphoreType.DMA((16,)), pltpu.SemaphoreType.DMA((8,))],
        compiler_params=pltpu.CompilerParams(vmem_limit_bytes=60 * 1024 * 1024),
        name="weights",
    )(acts, grads, lent, feats, far, first, far_first, pre, far_pre)


def local(acts, targets, enc, enc_bias, dec_own, dec_cross, dec_bias):
    tokens, rows = acts.shape[1:]
    scale = float(tokens * lax.axis_size("dp")) ** (-0.5)
    bias = dec_bias.astype(jnp.float32)
    residual, gathered, grads, feats, first, far, far_first, pre, far_pre, lent = band(
        acts[0].T, targets[0].T, bias, enc_bias, enc[0], dec_own[0], dec_cross, scale
    )[:10]
    grad_enc, grad_own, grad_cross = weights(gathered, grads, lent, feats, far, first, far_first, pre, far_pre)
    return (residual.T[None], grad_enc[None], grad_own[None], grad_cross)


def solution(mesh):
    in_specs = (
        P("layer", "dp", "feat"),
        P("layer", "dp", "feat"),
        P("layer", None, "feat"),
        P("layer", "feat"),
        P("layer", "feat", None),
        P("feat", "layer"),
        P("layer", "feat"),
    )
    out_specs = (
        P("layer", "dp", "feat"),
        P("layer", "dp", "feat"),
        P("layer", "feat", "dp"),
        P("feat", ("layer", "dp")),
    )
    return jax.shard_map(local, mesh=mesh, in_specs=in_specs, out_specs=out_specs, check_vma=False)
```

```python
import functools

import jax
import jax.numpy as jnp
from jax import lax
from jax.experimental import pallas as pl
from jax.experimental.pallas import tpu as pltpu
from jax.sharding import PartitionSpec as P

MESH = pl.DeviceIdType.MESH
ALL = slice(None)
SIDE = 4
JOBS = 8


class Place:
    def __init__(self):
        feat = lax.axis_index("feat")
        self.core = lax.axis_index("layer")
        self.dp = lax.axis_index("dp")
        self.x = lax.rem(feat, SIDE)
        self.y = lax.rem(lax.div(feat, SIDE), SIDE)
        self.zl = lax.div(feat, SIDE * SIDE)

    def feat(self, zl=None, y=None, x=None):
        zl = self.zl if zl is None else zl
        y = self.y if y is None else y
        x = self.x if x is None else x
        return (zl * SIDE + y) * SIDE + x

    def at(self, axis):
        return self.x if axis == "x" else self.y

    def along(self, axis, step):
        return lax.rem(self.at(axis) + (step + SIDE), SIDE)

    def neighbour(self, axis, step):
        return {"feat": self.feat(**{axis: self.along(axis, step)})}

    def pair(self):
        return {"feat": self.feat(zl=1 - self.zl)}

    def across(self, zl):
        return {"feat": self.feat(zl=zl), "dp": 1 - self.dp}

    def other_core(self):
        return {"layer": 1 - self.core}

    def greet(self):
        peers = [self.neighbour(a, s) for a in "xy" for s in (1, -1)]
        peers += [self.pair(), self.across(0), self.across(1)]
        peers.append(self.other_core())
        peers += [dict(self.pair(), **self.other_core()), dict(self.across(1 - self.zl), **self.other_core())]
        barrier = pltpu.get_barrier_semaphore()
        for peer in peers:
            pl.semaphore_signal(barrier, inc=1, device_id=peer, device_id_type=MESH)
        pl.semaphore_wait(barrier, len(peers))


def remote(src, dst, send, recv, device):
    return pltpu.make_async_remote_copy(
        src_ref=src, dst_ref=dst, send_sem=send, recv_sem=recv, device_id=device, device_id_type=MESH
    )


class Gather:
    sems = 11
    steps = 6

    whole, right, left = (slice(0, 2), ALL), (slice(0, 1), ALL), (slice(1, 2), ALL)

    def __init__(self, place, buf, own, lanes, flip, send, recv, local, job):
        self.place, self.buf, self.own, self.lanes = place, buf, own, lanes
        self.first, self.second = ("y", "x") if flip else ("x", "y")
        self.send, self.recv, self.local, self.job = send, recv, local, job
        self.sent = []

    def first_block(self, part, at):
        p = self.place
        slots, rows = part
        index = (slots, p.y, at, rows, self.lanes) if self.first == "x" else (slots, at, p.x, rows, self.lanes)
        return self.buf.at[index]

    def second_block(self, part, at):
        slots, rows = part
        index = (slots, at, ALL, rows, self.lanes) if self.second == "y" else (slots, ALL, at, rows, self.lanes)
        return self.buf.at[index]

    def copy(self, sem, src, dst, device, recv=None):
        return remote(src, dst, self.send.at[self.job, sem], self.recv.at[self.job, sem if recv is None else recv], device)

    def out(self, sem, block, device):
        copy = self.copy(sem, block, block, device)
        copy.start()
        self.sent.append(copy)
        return copy

    def ring(self, sem, axis, block):
        p = self.place
        own = block(self.whole, p.at(axis))
        return (self.out(sem, own, p.neighbour(axis, 1)), self.out(sem + 1, own, p.neighbour(axis, -1)))

    def forward(self, sem, axis, block):
        p = self.place
        return (
            self.out(sem, block(self.right, p.along(axis, -1)), p.neighbour(axis, 1)),
            self.out(sem + 1, block(self.left, p.along(axis, 1)), p.neighbour(axis, -1)),
        )

    def begin(self):
        p = self.place
        here = self.buf.at[p.zl, p.y, p.x, :, self.lanes]
        if self.local is not None:
            self.kept = [pltpu.make_async_copy(self.own, here, self.local.at[self.job])]
            self.kept[0].start()
        self.waits = [self.copy(0, self.own, here, p.pair())]
        self.waits[0].start()
        self.sent += self.waits

    def settle(self):
        while self.kept:
            self.kept.pop().wait()

    def step(self, number):
        if number == 0:
            self.begin()
            return
        for copy in self.waits:
            copy.wait_recv()
        if number == 1:
            self.settle()
            self.waits = self.ring(3, self.first, self.first_block)
        elif number == 2:
            self.waits = self.forward(5, self.first, self.first_block)
        elif number == 3:
            self.waits = self.ring(7, self.second, self.second_block)
        elif number == 4:
            self.waits = self.forward(9, self.second, self.second_block)

    def finish(self):
        for copy in self.sent:
            copy.wait_send()


class Extra(Gather):
    def __init__(self, *args):
        super().__init__(*args)
        rows = self.own.shape[0]
        cut = (rows // 32 + rows % 32 // 16) * 16
        slot = slice(2, 3)
        self.whole, self.right, self.left = (slot, ALL), (slot, pl.ds(0, cut)), (slot, pl.ds(cut, rows - cut))

    def begin(self):
        p = self.place
        there = self.buf.at[2, p.y, p.x, :, self.lanes]
        self.cross = [self.copy(1 + zl, self.own, there, p.across(zl), recv=1) for zl in (0, 1)]

        @pl.when(p.zl != p.dp)
        def _():
            for copy in self.cross:
                copy.start()

        self.waits = [self.cross[0]]

    def settle(self):
        pass

    def finish(self):
        super().finish()

        @pl.when(self.place.zl != self.place.dp)
        def _():
            for copy in self.cross:
                copy.wait_send()


class Reduce:
    sems = 13
    steps = 6

    def __init__(self, place, part, lanes, flip, room, send, recv, job, finish):
        self.place, self.part, self.lanes = place, part, lanes
        self.first, self.second = ("x", "y") if flip else ("y", "x")
        self.far1, self.far2, self.near1, self.near2, self.last = room
        self.send, self.recv, self.job, self.done = send, recv, job, finish
        self.sent = []

    def first_block(self, z, at):
        return (z, at, ALL, ALL, self.lanes) if self.first == "y" else (z, ALL, at, ALL, self.lanes)

    def second_block(self, z, at):
        p = self.place
        return (z, p.y, at, ALL, self.lanes) if self.first == "y" else (z, at, p.x, ALL, self.lanes)

    def out(self, sem, src, dst, device):
        copy = remote(src, dst, self.send.at[self.job, sem], self.recv.at[self.job, sem], device)
        copy.start()
        self.sent.append(copy)
        return copy

    def add(self, index, *refs):
        total = self.part[index].astype(jnp.float32)
        for ref in refs:
            total = total + ref[...].astype(jnp.float32)
        self.part[index] = total.astype(self.part.dtype)

    def begin(self, sem, axis, block, one, two):
        p = self.place
        right, left = p.neighbour(axis, 1), p.neighbour(axis, -1)
        far, up, down = p.along(axis, 2), p.along(axis, 1), p.along(axis, -1)
        j = self.job
        self.relay = (
            self.out(sem, self.part.at[block(0, far)], one.at[j, 0], right),
            self.out(sem + 1, self.part.at[block(1, far)], one.at[j, 1], left),
        )
        self.early = (
            self.out(sem + 2, self.part.at[block(1, up)], two.at[j, 0, 1], right),
            self.out(sem + 3, self.part.at[block(0, down)], two.at[j, 1, 0], left),
        )

    def pass_on(self, sem, axis, block, one, two):
        p = self.place
        right, left = p.neighbour(axis, 1), p.neighbour(axis, -1)
        up, down = p.along(axis, 1), p.along(axis, -1)
        j = self.job
        self.relay[0].wait_recv()
        self.add(block(0, up), one.at[j, 0])
        late = self.out(sem, self.part.at[block(0, up)], two.at[j, 0, 0], right)
        self.relay[1].wait_recv()
        self.add(block(1, down), one.at[j, 1])
        self.late = (late, self.out(sem + 1, self.part.at[block(1, down)], two.at[j, 1, 1], left))

    def collect(self, axis, block, two):
        for copy in self.early + self.late:
            copy.wait_recv()
        self.add(block(slice(0, 2), self.place.at(axis)), two.at[self.job, 0], two.at[self.job, 1])

    def step(self, number):
        p = self.place
        if number == 0:
            self.begin(0, self.first, self.first_block, self.far1, self.far2)
        elif number == 1:
            self.pass_on(4, self.first, self.first_block, self.far1, self.far2)
        elif number == 2:
            self.collect(self.first, self.first_block, self.far2)
            self.begin(6, self.second, self.second_block, self.near1, self.near2)
        elif number == 3:
            self.pass_on(10, self.second, self.second_block, self.near1, self.near2)
        elif number == 4:
            self.collect(self.second, self.second_block, self.near2)
            gone = self.part.at[1 - p.zl, p.y, p.x, :, self.lanes]
            self.pair = self.out(12, gone, self.last.at[self.job], p.pair())
        else:
            self.pair.wait_recv()
            mine = self.part[p.zl, p.y, p.x, :, self.lanes].astype(jnp.float32)
            self.done(mine + self.last[self.job].astype(jnp.float32), self.lanes)

    def finish(self):
        for copy in self.sent:
            copy.wait_send()


class Swap:
    sems = 4

    def __init__(self, place, src, relay, dst, send, recv, job):
        self.place, self.src, self.relay, self.dst = place, src, relay, dst
        self.send, self.recv, self.job = send, recv, job
        self.sent = []

    def device(self, sem):
        p = self.place
        turn = p.zl if sem % 2 == 0 else 1 - p.zl
        return {"feat": p.feat(zl=1 - p.zl), "dp": lax.rem(p.dp + turn, 2)}

    def out(self, sem, src, dst):
        copy = remote(src, dst, self.send.at[self.job, sem], self.recv.at[self.job, sem], self.device(sem))
        copy.start()
        self.sent.append(copy)

    def step(self, number):
        if number == 0:
            for way in (0, 1):
                self.out(way, self.src[way], self.relay[way])
        elif number == 1:
            for way in (0, 1):
                self.sent[way].wait_recv()
                self.out(2 + way, self.relay[way], self.dst[way])
        else:
            for way in (0, 1):
                self.sent[2 + way].wait_recv()

    def finish(self):
        for copy in self.sent:
            copy.wait_send()


class Lend:
    sems = 8

    def __init__(self, place, buf, relay, rows, lanes, send, recv, job):
        p = self.place = place
        self.lanes = lanes
        half = SIDE // 2
        self.upper = p.core == 1
        self.upper_gives = jnp.logical_and(self.upper, p.dp == 0)
        self.lower_gets = jnp.logical_and(p.core == 0, p.dp == 0)
        self.over_z = p.core == 1 - p.dp
        ys = pl.ds(half * p.dp, half)
        own, far = rows.at[0, :, :, :, lanes], rows.at[1, :, :, :, lanes]
        copy = lambda sem, src, dst, device: remote(src, dst, send.at[job, sem], recv.at[job, sem], device)
        self.give_own = copy(0, buf.at[0, ys, :, :, lanes], own, p.other_core())
        self.give_far = copy(1, buf.at[2, ys, :, :, lanes], far, p.other_core())
        self.first, self.second = [], []
        for way in range(2):
            turn = p.zl if way == 0 else 1 - p.zl
            dp = lax.rem(p.dp + turn, 2)
            device = {"feat": p.feat(zl=1 - p.zl), "dp": dp}
            src = buf.at[p.dp, pl.ds(half * (1 - p.dp) + way, 1), :, :, lanes]
            self.first.append(copy(2 + way, src, relay.at[job, way], device))
            dst = rows.at[1, pl.ds(way, 1), :, :, lanes]
            self.second.append(copy(4 + way, relay.at[job, way], dst, dict(device, layer=1 - dp)))

    def step(self, number):
        if number == 0:

            @pl.when(self.upper)
            def _():
                for copy in self.first + [self.give_own]:
                    copy.start()

        elif number == 1:

            @pl.when(self.upper)
            def _():
                for way in range(2):
                    self.first[way].wait_recv()
                    self.second[way].start()

        else:

            @pl.when(self.upper_gives)
            def _():
                self.give_far.start()

    def finish(self):
        @pl.when(self.upper)
        def _():
            for copy in self.first + self.second + [self.give_own]:
                copy.wait_send()

        @pl.when(jnp.logical_not(self.upper))
        def _():
            self.give_own.wait_recv()

        @pl.when(self.upper_gives)
        def _():
            self.give_far.wait_send()

        @pl.when(self.lower_gets)
        def _():
            self.give_far.wait_recv()

        @pl.when(self.over_z)
        def _():
            for copy in self.second:
                copy.wait_recv()


def matmul(a, b, over_a=1, over_b=0):
    return lax.dot_general(a, b, (((over_a,), (over_b,)), ((), ())), preferred_element_type=jnp.float32)


CHUNKS = JOBS // 2

ORDER = (
    ("A", 6, 0), ("A", 7, 0), ("A", 4, 0), ("A", 5, 0), ("A", 2, 0), ("A", 3, 0), ("A", 0, 0), ("A", 1, 0),
    ("a", 0, 0), ("A", 6, 1), ("A", 7, 1), ("A", 4, 1), ("A", 5, 1), ("a", 1, 0), ("T", 0), ("A", 2, 1),
    ("A", 3, 1), ("a", 2, 0), ("T", 1), ("A", 0, 1), ("A", 1, 1), ("T", 2), ("a", 3, 0), ("T", 3), ("A", 6, 2),
    ("A", 7, 2), ("T", 4), ("T", 5), ("A", 4, 2), ("A", 5, 2), ("T", 6), ("T", 7), ("a", 0, 1), ("A", 2, 2),
    ("A", 3, 2), ("T", 8), ("a", 1, 1), ("T", 9), ("A", 0, 2), ("A", 1, 2), ("T", 10), ("A", 6, 3), ("A", 7, 3),
    ("T", 11), ("A", 4, 3), ("A", 5, 3), ("T", 12), ("A", 3, 3), ("T", 13), ("T", 14), ("T", 15), ("A", 2, 3),
    ("T", 16), ("A", 0, 3), ("A", 1, 3), ("T", 17), ("T", 18), ("T", 19), ("T", 20), ("T", 21), ("T", 22),
    ("T", 23), ("T", 24), ("T", 25), ("T", 26), ("T", 27), ("A", 7, 4), ("A", 6, 4), ("A", 5, 4), ("A", 4, 4),
    ("A", 3, 4), ("A", 2, 4), ("A", 1, 4), ("A", 0, 4), ("A", 7, 5), ("A", 6, 5), ("L", 3), ("F", 3), ("A", 5, 5),
    ("A", 4, 5), ("L", 2), ("a", 2, 1), ("a", 3, 1), ("A", 3, 5), ("A", 2, 5), ("L", 1), ("F", 2), ("D", 3, 0),
    ("D", 3, 1), ("R", 6, 0), ("R", 7, 0), ("S", 3, 1), ("D", 2, 0), ("D", 2, 1), ("R", 4, 0), ("R", 5, 0),
    ("R", 6, 1), ("R", 7, 1), ("S", 3, 2), ("S", 2, 1), ("F", 1), ("A", 1, 5), ("A", 0, 5), ("L", 0), ("R", 4, 1),
    ("R", 5, 1), ("S", 2, 2), ("D", 1, 0), ("D", 1, 1), ("R", 2, 0), ("R", 3, 0), ("S", 1, 1), ("R", 6, 2),
    ("R", 7, 2), ("F", 0), ("R", 4, 2), ("R", 5, 2), ("S", 1, 2), ("R", 2, 1), ("R", 3, 1), ("D", 0, 0),
    ("R", 7, 3), ("R", 6, 3), ("R", 5, 3), ("R", 4, 3), ("D", 0, 1), ("R", 0, 0), ("R", 1, 0), ("S", 0, 1),
    ("R", 2, 2), ("R", 7, 4), ("R", 6, 4), ("R", 5, 4), ("R", 4, 4), ("R", 3, 2), ("R", 0, 1), ("R", 1, 1),
    ("R", 7, 5), ("G", 7, 0), ("R", 6, 5), ("G", 6, 0), ("R", 5, 5), ("G", 5, 0), ("R", 4, 5), ("G", 4, 0),
    ("S", 0, 2), ("g", 2, 0), ("R", 3, 3), ("g", 3, 0), ("R", 2, 3), ("a", 1, 2), ("G", 7, 1), ("a", 0, 2),
    ("G", 6, 1), ("G", 5, 1), ("G", 4, 1), ("R", 0, 2), ("R", 3, 4), ("R", 2, 4), ("R", 1, 2), ("a", 2, 2),
    ("G", 7, 2), ("a", 3, 2), ("G", 6, 2), ("a", 0, 3), ("R", 3, 5), ("G", 3, 0), ("R", 2, 5), ("G", 5, 2),
    ("G", 2, 0), ("G", 4, 2), ("g", 1, 0), ("a", 1, 3), ("R", 1, 3), ("R", 0, 3), ("G", 7, 3), ("G", 3, 1),
    ("G", 2, 1), ("G", 6, 3), ("G", 4, 3), ("G", 5, 3), ("R", 1, 4), ("R", 0, 4), ("G", 3, 2), ("R", 1, 5),
    ("G", 1, 0), ("R", 0, 5), ("G", 0, 0), ("g", 0, 0), ("G", 1, 1), ("G", 0, 1), ("G", 7, 4), ("G", 6, 4),
    ("G", 2, 2), ("G", 4, 4), ("G", 5, 4), ("G", 3, 3), ("G", 0, 2), ("G", 1, 2), ("G", 7, 5), ("G", 6, 5),
    ("M", 3), ("g", 3, 1), ("G", 2, 3), ("B", 3, 0), ("G", 4, 5), ("G", 5, 5), ("M", 2), ("G", 1, 3), ("W", 3),
    ("B", 2, 0), ("B", 3, 1), ("W", 2), ("G", 3, 4), ("a", 2, 3), ("B", 2, 1), ("G", 2, 4), ("G", 0, 3),
    ("P", 3, 1), ("g", 2, 1), ("G", 1, 4), ("G", 3, 5), ("a", 3, 3), ("G", 2, 5), ("M", 1), ("P", 2, 1),
    ("B", 1, 0), ("G", 1, 5), ("g", 1, 1), ("a", 0, 4), ("P", 3, 2), ("a", 1, 4), ("G", 0, 4), ("B", 1, 1),
    ("W", 1), ("g", 0, 1), ("g", 3, 2), ("g", 2, 2), ("P", 2, 2), ("a", 0, 5), ("a", 2, 4), ("a", 3, 4),
    ("a", 1, 5), ("G", 0, 5), ("M", 0), ("P", 1, 1), ("g", 1, 2), ("g", 0, 2), ("g", 2, 3), ("g", 3, 3),
    ("B", 0, 0), ("a", 2, 5), ("a", 3, 5), ("W", 0), ("B", 0, 1), ("g", 1, 3), ("g", 0, 3), ("P", 1, 2),
    ("g", 2, 4), ("g", 3, 4), ("P", 0, 1), ("g", 0, 4), ("g", 1, 4), ("g", 2, 5), ("g", 3, 5), ("P", 0, 2),
    ("g", 0, 5), ("g", 1, 5),
)


def band_kernel(
    scale, acts_in, target_ref, bias_ref, enc_bias_ref, enc_in, dec_in, cross_in,
    resid_ref, acts_buf, grad_buf, feats_out, lower_out, far_out, far_lower_ref, pre_ref, far_pre_ref, rows_buf,
    relay, pre_relay, rows_relay, acts_relay,
    enc_n, dec_n, enc_t, dec_t, cross_t, cross_ref, feats_ref, lower_ref, far_ref, bias_t, enc_bias_t, positive_ref, down_ref, up_ref,
    chunk, part, shard, far1, far2, near1, near2, last,
    send_a, recv_a, send_r, recv_r, send_g, recv_g, send_s, recv_s, send_p, recv_p, send_l, recv_l,
    send_xa, recv_xa, send_xg, recv_xg, send_z, recv_z,
    local_a, local_g, load_sem, chunk_sem, grad_sem, out_sem, core_send, core_recv,
):
    tokens = acts_in.shape[1]
    wide = tokens // CHUNKS
    lane = wide // 2
    rows = acts_in.shape[0]
    n_feat = feats_ref.shape[0]
    half = cross_ref.shape[2]
    width = 2 * half
    place = Place()
    first_core = place.core == 0

    loads = [
        pltpu.make_async_copy(enc_in, enc_n, load_sem.at[0]),
        pltpu.make_async_copy(dec_in, dec_n, load_sem.at[1]),
        pltpu.make_async_copy(cross_in, cross_ref.at[place.core], load_sem.at[2]),
    ]
    for load in loads:
        load.start()
    place.greet()

    def swap_cross():
        at = 3 * CHUNKS
        copy = remote(cross_in, cross_ref.at[place.core], core_send.at[at], core_recv.at[at], place.other_core())
        copy.start()
        return copy

    def finish_residual(total, lanes):
        resid = total + bias_t[:, 0:1] - target_ref[:, lanes].astype(jnp.float32)
        resid_ref[:, lanes] = resid
        shard[:, lanes] = (resid * scale).astype(shard.dtype)

    room = (far1, far2, near1, near2, last)
    gathers, reduces, grads, swaps, lent, far_lent, pre_swaps, lends, downs = [], [], [], [], [], [], [], [], []
    act_extras, grad_extras, act_swaps = [], [], []
    for job in range(JOBS):
        c, flip = job // 2, job % 2
        lanes = pl.ds(job * lane, lane)
        gathers.append(
            Gather(place, acts_buf, acts_in.at[:, lanes], lanes, flip, send_a, recv_a, None, job)
        )
        grads.append(Gather(place, grad_buf, shard.at[:, lanes], lanes, flip, send_g, recv_g, local_g, job))
        inner = pl.ds(flip * lane, lane)
        done = functools.partial(lambda whole, total, _: finish_residual(total, whole), lanes)
        reduces.append(Reduce(place, part.at[c], inner, flip, room, send_r, recv_r, job, done))
    for c in range(CHUNKS):
        lanes = pl.ds(c * wide, wide)
        ways = [pl.ds(way * (n_feat // 2), n_feat // 2) for way in (0, 1)]

        def dp_swap(here, between, there, send, recv):
            return Swap(
                place, [here.at[w, lanes] for w in ways], [between.at[c, way] for way in (0, 1)],
                [there.at[w, lanes] for w in ways], send, recv, c,
            )

        def to_core(kind, here, there):
            at = kind * CHUNKS + c
            return remote(
                here.at[:, lanes], there.at[:, lanes], core_send.at[at], core_recv.at[at], place.other_core()
            )

        swaps.append(dp_swap(feats_ref, relay, far_ref, send_s, recv_s))
        pre_swaps.append(dp_swap(pre_ref, pre_relay, far_pre_ref, send_p, recv_p))
        lent.append(to_core(0, feats_ref, lower_ref))
        far_lent.append(to_core(1, far_ref, far_lower_ref))
        downs.append(to_core(2, down_ref, up_ref))
        act_extras.append(
            Extra(place, acts_buf, acts_in.at[:, lanes], lanes, c % 2, send_xa, recv_xa, None, c)
        )
        grad_extras.append(Extra(place, grad_buf, shard.at[:, lanes], lanes, c % 2, send_xg, recv_xg, None, c))
        y_halves = [pl.ds(way * (SIDE // 2), SIDE // 2) for way in (0, 1)]
        act_swaps.append(
            Swap(
                place, [acts_buf.at[1 - place.dp, ys, :, :, lanes] for ys in y_halves],
                [acts_relay.at[c, way] for way in (0, 1)], [acts_buf.at[2, ys, :, :, lanes] for ys in y_halves],
                send_z, recv_z, c,
            )
        )
        lends.append(Lend(place, grad_buf, rows_relay, rows_buf, lanes, send_l, recv_l, c))

    def load_chunk(c):
        return pltpu.make_async_copy(
            acts_buf.at[pl.ds(0, 2), :, :, :, pl.ds(c * wide, wide)], chunk.at[c % 2], chunk_sem.at[c]
        )

    def encode(c):
        load_chunk(c).wait()
        lanes = pl.ds(c * wide, wide)
        pre_act = matmul(enc_t[...], chunk[c % 2].reshape(width, wide)) + enc_bias_t[:, 0:1]
        positive = jnp.maximum(pre_act, 0.0)
        positive_ref[:, lanes] = positive
        feats_ref[:, lanes] = (positive * positive).astype(feats_ref.dtype)

        @pl.when(first_core)
        def _():
            lent[c].start()
            lower_ref[:, lanes] = feats_ref[:, lanes]

        swaps[c].step(0)

    outs = [
        pltpu.make_async_copy(here, there, out_sem.at[i])
        for i, (here, there) in enumerate([(feats_ref, feats_out), (lower_ref, lower_out), (far_ref, far_out)])
    ]
    lent_far = []

    def lend_far(c):
        swaps[c].step(2)
        lent_far.append(c)
        if len(lent_far) == CHUNKS:
            for copy in outs:
                copy.start()
        lanes = pl.ds(c * wide, wide)

        @pl.when(first_core)
        def _():
            far_lent[c].start()
            far_lower_ref[:, lanes] = far_ref[:, lanes]

    def decode(c, side):
        lanes = pl.ds(c * wide, wide)
        block = SIDE * rows

        def store(i, total):
            part[c, lax.div(i, SIDE), lax.rem(i, SIDE)] = total.astype(part.dtype).reshape(SIDE, rows, wide)

        def at(i):
            return pl.ds(pl.multiple_of(i * block, 16), block)

        @pl.when(first_core)
        def _():
            @pl.loop(side * SIDE, side * SIDE + SIDE)
            def _(i):
                store(i, matmul(dec_t[at(i), :], feats_ref[:, lanes]))

        @pl.when(jnp.logical_not(first_core))
        def _():
            if side == 0:
                lent[c].wait_recv()

            @pl.loop(side * SIDE, side * SIDE + SIDE)
            def _(i):
                total = matmul(dec_t[at(i), :], feats_ref[:, lanes]) + matmul(cross_t[at(i), :], lower_ref[:, lanes])
                store(i, total)

    def load_grads(c):
        return pltpu.make_async_copy(
            grad_buf.at[pl.ds(0, 2), :, :, :, pl.ds(c * wide, wide)], chunk.at[c % 2], grad_sem.at[c]
        )

    def finish_grads(c):
        load_grads(c).start()
        lends[c].step(0)

    def extra_grads(c, number):
        grad_extras[c].step(number)
        if number == Gather.steps - 1:
            lends[c].step(2)

    def backward(c, part):
        lanes = pl.ds(c * wide, wide)
        here = chunk.at[c % 2]
        if part == 0:
            load_grads(c).wait()
            send_down(c, lanes, here)
        else:
            make_pre(c, lanes, here)

    def send_down(c, lanes, here):
        @pl.when(jnp.logical_not(first_core))
        def _():
            down = matmul(cross_ref[0], here[0].reshape(half, wide)) + matmul(cross_ref[1], here[1].reshape(half, wide))
            down_ref[:, lanes] = down.astype(down_ref.dtype)
            downs[c].start()

    def make_pre(c, lanes, here):
        grad_feats = matmul(dec_n[...], here[...].reshape(width, wide))

        @pl.when(first_core)
        def _():
            downs[c].wait_recv()
            total = grad_feats + up_ref[:, lanes].astype(jnp.float32)
            pre_ref[:, lanes] = (total * 2.0 * positive_ref[:, lanes]).astype(pre_ref.dtype)

        @pl.when(jnp.logical_not(first_core))
        def _():
            pre_ref[:, lanes] = (grad_feats * 2.0 * positive_ref[:, lanes]).astype(pre_ref.dtype)

        pre_swaps[c].step(0)

    cross_swap = []

    def turn_enc(i):
        if i == 0:
            bias_t[...] = jnp.broadcast_to(bias_ref[...], (128, rows)).T
            enc_bias_t[...] = jnp.broadcast_to(enc_bias_ref[...], (128, n_feat)).T
            loads[0].wait()
        block = pl.ds(i * n_feat, n_feat)
        enc_t[:, block] = enc_n[block, :].T

    def turn_dec(i):
        if i == 0:
            loads[1].wait()
        block = pl.ds(i * n_feat, n_feat)
        dec_t[block, :] = dec_n[:, block].T

    def turn_cross(i):
        if i == 0:
            loads[2].wait()
            cross_swap[0].wait_recv()
        z, at = divmod(i * 256, half)
        cross_t[pl.ds(i * 256, 256), :] = cross_ref[z, :, pl.ds(at, 256)].T

    background = [functools.partial(turn_enc, i) for i in range(width // n_feat)]
    background += [functools.partial(turn_dec, i) for i in range(width // n_feat)]
    background += [functools.partial(turn_cross, i) for i in range(width // 256)]

    cross_swap.append(swap_cross())
    kept = [pltpu.make_async_copy(acts_in, acts_buf.at[place.zl, place.y, place.x], local_a.at[0])]
    kept[0].start()
    for job in gathers:
        job.kept = kept
    act_jobs = {
        "A": lambda i, n: gathers[i].step(n),
        "a": lambda i, n: act_extras[i].step(n),
        "Z": lambda i, n: act_swaps[i].step(n),
        "T": lambda i: background[i](),
        "L": lambda i: load_chunk(i).start(),
        "F": encode,
        "D": decode,
        "R": lambda i, n: reduces[i].step(n),
        "G": lambda i, n: grads[i].step(n),
        "g": extra_grads,
        "M": finish_grads,
        "B": backward,
        "S": lambda i, n: swaps[i].step(1) if n == 1 else lend_far(i),
        "P": lambda i, n: pre_swaps[i].step(n),
        "W": lambda i: lends[i].step(1),
    }
    for name, *numbers in ORDER:
        act_jobs[name](*numbers)
    used = {(name, numbers[0]) for name, *numbers in ORDER}
    act_extras = [job for i, job in enumerate(act_extras) if ("a", i) in used]
    act_swaps = [job for i, job in enumerate(act_swaps) if ("Z", i) in used]
    everything = gathers + act_extras + act_swaps + reduces + grads + grad_extras + swaps + pre_swaps + lends
    for job in everything:
        job.finish()
    cross_swap[0].wait_send()
    for copy in outs:
        copy.wait()

    @pl.when(first_core)
    def _():
        for copy in lent + far_lent:
            copy.wait_send()

    @pl.when(jnp.logical_not(first_core))
    def _():
        for copy in far_lent:
            copy.wait_recv()
        for copy in downs:
            copy.wait_send()


def band(acts, targets, bias, enc_bias, enc, dec_own, dec_cross, scale):
    rows, tokens = targets.shape
    width, n_feat = enc.shape
    lane = tokens // JOBS
    wide = tokens // CHUNKS
    kind = acts.dtype
    whole = pl.BlockSpec(memory_space=pltpu.VMEM)
    away = pl.BlockSpec(memory_space=pl.ANY)
    gathered = jax.ShapeDtypeStruct((3, SIDE, SIDE, rows, tokens), kind)
    feats = jax.ShapeDtypeStruct((n_feat, tokens), kind)
    dma = pltpu.SemaphoreType.DMA
    return pl.pallas_call(
        functools.partial(band_kernel, scale),
        out_shape=(
            jax.ShapeDtypeStruct((rows, tokens), jnp.float32),
            gathered,
            gathered,
            feats, feats, feats, feats, feats, feats,
            jax.ShapeDtypeStruct((2, SIDE // 2, SIDE, rows, tokens), kind),
            jax.ShapeDtypeStruct((CHUNKS, 2, n_feat // 2, wide), kind),
            jax.ShapeDtypeStruct((CHUNKS, 2, n_feat // 2, wide), kind),
            jax.ShapeDtypeStruct((CHUNKS, 2, 1, SIDE, rows, wide), kind),
            jax.ShapeDtypeStruct((CHUNKS, 2, SIDE // 2, SIDE, rows, wide), kind),
        ),
        in_specs=[whole] * 4 + [away] * 3,
        out_specs=(whole, away, away) + (away,) * 3 + (whole,) * 3 + (away,) * 5,
        scratch_shapes=[
            pltpu.VMEM((width, n_feat), kind),
            pltpu.VMEM((n_feat, width), kind),
            pltpu.VMEM((n_feat, width), kind),
            pltpu.VMEM((width, n_feat), kind),
            pltpu.VMEM((width, n_feat), kind),
            pltpu.VMEM((2,) + dec_cross.shape, kind),
            pltpu.VMEM((n_feat, tokens), kind),
            pltpu.VMEM((n_feat, tokens), kind),
            pltpu.VMEM((n_feat, tokens), kind),
            pltpu.VMEM((rows, 128), jnp.float32),
            pltpu.VMEM((n_feat, 128), jnp.float32),
            pltpu.VMEM((n_feat, tokens), jnp.float32),
            pltpu.VMEM((n_feat, tokens), kind),
            pltpu.VMEM((n_feat, tokens), kind),
            pltpu.VMEM((2, 2, SIDE, SIDE, rows, wide), kind),
            pltpu.VMEM((CHUNKS, 2, SIDE, SIDE, rows, wide), kind),
            pltpu.VMEM((rows, tokens), kind),
            pltpu.VMEM((JOBS, 2, SIDE, rows, lane), kind),
            pltpu.VMEM((JOBS, 2, 2, SIDE, rows, lane), kind),
            pltpu.VMEM((JOBS, 2, rows, lane), kind),
            pltpu.VMEM((JOBS, 2, 2, rows, lane), kind),
            pltpu.VMEM((JOBS, rows, lane), kind),
            dma((JOBS, Gather.sems)),
            dma((JOBS, Gather.sems)),
            dma((JOBS, Reduce.sems)),
            dma((JOBS, Reduce.sems)),
            dma((JOBS, Gather.sems)),
            dma((JOBS, Gather.sems)),
            dma((CHUNKS, Swap.sems)),
            dma((CHUNKS, Swap.sems)),
            dma((CHUNKS, Swap.sems)),
            dma((CHUNKS, Swap.sems)),
            dma((CHUNKS, Lend.sems)),
            dma((CHUNKS, Lend.sems)),
            dma((CHUNKS, Gather.sems)),
            dma((CHUNKS, Gather.sems)),
            dma((CHUNKS, Gather.sems)),
            dma((CHUNKS, Gather.sems)),
            dma((CHUNKS, Swap.sems)),
            dma((CHUNKS, Swap.sems)),
            dma((JOBS,)),
            dma((JOBS,)),
            dma((3,)),
            dma((CHUNKS,)),
            dma((CHUNKS,)),
            dma((3,)),
            dma((3 * CHUNKS + 1,)),
            dma((3 * CHUNKS + 1,)),
        ],
        compiler_params=pltpu.CompilerParams(
            collective_id=1, has_side_effects=True, vmem_limit_bytes=60 * 1024 * 1024
        ),
        name="band",
    )(acts, targets, bias, enc_bias, enc, dec_own, dec_cross)


def weights_kernel(
    acts_in, grads_in, rows_in, feats_in, far_in, first_in, far_first_in, pre_in, far_pre_in,
    enc_out, own_out, cross_out,
    acts, grads, rows, feats, first, pre, enc_g, own_g, cross_g, load_sem, store_sem,
):
    dp = lax.axis_index("dp")
    half = SIDE // 2
    n_feat, width = own_g.shape
    block = width // 2
    started = []

    def load(src, dst):
        copy = pltpu.make_async_copy(src, dst, load_sem.at[len(started)])
        copy.start()
        started.append(copy)
        return copy

    ys = [pl.ds(half * part, half) for part in (0, 1)]
    first_loads = [load(feats_in, feats.at[0]), load(far_in, feats.at[1])]
    grad_loads = [[load(grads_in.at[slot, y], grads.at[i, y]) for i, slot in ((0, dp), (1, 2))] for y in ys]
    pre_loads = [load(pre_in, pre.at[0]), load(far_pre_in, pre.at[1])]
    act_loads = [[load(acts_in.at[slot, y], acts.at[i, y]) for i, slot in ((0, dp), (1, 2))] for y in ys]
    cross_loads = [load(first_in, first.at[0]), load(far_first_in, first.at[1])]
    upper = lax.axis_index("layer") == 1
    mine = pl.ds(half * dp, half)

    def load_rows(i, here, slot):
        at = len(started)

        @pl.when(here)
        def _():
            pltpu.make_async_copy(grads_in.at[slot, mine], rows.at[i], load_sem.at[at]).start()

        @pl.when(jnp.logical_not(here))
        def _():
            pltpu.make_async_copy(rows_in.at[i], rows.at[i], load_sem.at[at]).start()

        started.append(pltpu.make_async_copy(rows_in.at[i], rows.at[i], load_sem.at[at]))
        return started[-1]

    cross_loads += [load_rows(0, upper, 1), load_rows(1, jnp.logical_and(upper, dp == 1), 2)]
    stores = []

    def store(src, dst):
        copy = pltpu.make_async_copy(src, dst, store_sem.at[len(stores)])
        copy.start()
        stores.append(copy)

    def both(a, b):
        return matmul(a[0], b[0], 1, 1) + matmul(a[1], b[1], 1, 1)

    def by_feats(left, right, out, columns):
        out[:, columns] = both((left[0], left[1]), right())

    for copy in first_loads:
        copy.wait()
    for part in (0, 1):
        for copy in grad_loads[part]:
            copy.wait()
        columns = pl.ds(part * block, block)
        by_feats(feats, lambda: [grads[i, ys[part]].reshape(block, -1) for i in (0, 1)], own_g, columns)
        store(own_g.at[:, columns], own_out.at[:, columns])
    for copy in pre_loads:
        copy.wait()
    for part in (0, 1):
        for copy in act_loads[part]:
            copy.wait()
        for y in range(half * part, half * part + half):
            at = pl.ds(y * (width // SIDE), width // SIDE)
            enc_g[at, :] = both([acts[i, y].reshape(width // SIDE, -1) for i in (0, 1)], [pre[0], pre[1]])
            store(enc_g.at[at, :], enc_out.at[at, :])
    for copy in cross_loads:
        copy.wait()
    by_feats(first, lambda: [rows[i].reshape(block, -1) for i in (0, 1)], cross_g, pl.ds(0, block))
    store(cross_g, cross_out)
    for copy in stores:
        copy.wait()


def weights(acts, grads, lent, feats, far, first, far_first, pre, far_pre):
    rows, tokens = acts.shape[3:]
    n_feat = feats.shape[0]
    half = SIDE * SIDE * rows
    kind = acts.dtype
    f32 = jnp.float32
    away = pl.BlockSpec(memory_space=pl.ANY)
    shapes = [(half, n_feat), (n_feat, half), (n_feat, half // 2)]
    return pl.pallas_call(
        weights_kernel,
        out_shape=[jax.ShapeDtypeStruct(s, f32) for s in shapes],
        in_specs=[away] * 9,
        out_specs=[away] * 3,
        scratch_shapes=[
            pltpu.VMEM((2, SIDE, SIDE, rows, tokens), kind),
            pltpu.VMEM((2, SIDE, SIDE, rows, tokens), kind),
            pltpu.VMEM(lent.shape, kind),
            pltpu.VMEM((2, n_feat, tokens), kind),
            pltpu.VMEM((2, n_feat, tokens), kind),
            pltpu.VMEM((2, n_feat, tokens), kind),
        ]
        + [pltpu.VMEM(s, f32) for s in shapes]
        + [pltpu.SemaphoreType.DMA((16,)), pltpu.SemaphoreType.DMA((8,))],
        compiler_params=pltpu.CompilerParams(vmem_limit_bytes=60 * 1024 * 1024),
        name="weights",
    )(acts, grads, lent, feats, far, first, far_first, pre, far_pre)


def local(acts, targets, enc, enc_bias, dec_own, dec_cross, dec_bias):
    tokens, rows = acts.shape[1:]
    scale = float(tokens * lax.axis_size("dp")) ** (-0.5)
    bias = dec_bias.astype(jnp.float32)
    residual, gathered, grads, feats, first, far, far_first, pre, far_pre, lent = band(
        acts[0].T, targets[0].T, bias, enc_bias, enc[0], dec_own[0], dec_cross, scale
    )[:10]
    grad_enc, grad_own, grad_cross = weights(gathered, grads, lent, feats, far, first, far_first, pre, far_pre)
    return (residual.T[None], grad_enc[None], grad_own[None], grad_cross)


def solution(mesh):
    in_specs = (
        P("layer", "dp", "feat"),
        P("layer", "dp", "feat"),
        P("layer", None, "feat"),
        P("layer", "feat"),
        P("layer", "feat", None),
        P("feat", "layer"),
        P("layer", "feat"),
    )
    out_specs = (
        P("layer", "dp", "feat"),
        P("layer", "dp", "feat"),
        P("layer", "feat", "dp"),
        P("feat", ("layer", "dp")),
    )
    return jax.shard_map(local, mesh=mesh, in_specs=in_specs, out_specs=out_specs, check_vma=False)
```
